256 devices in a mesh: img: 8 (over z_hi, core), sp: 32 (over x, z_lo, y).
Axes of the slice: x: 4, y: 4, z: 8 (z_hi: 4, z_lo: 2; z = z_hi * 2 + z_lo), core: 2. Of those that a mesh axis runs over, the one named last changes fastest.
Arguments:
- y_one: bfloat16 [32768, 1408], P(('img', 'sp')), parts along dimension 0, may hold values from -6 to 6
- second_stream_state: bfloat16 [32768, 1408], P(('img', 'sp')), parts along dimension 0, may hold values from -6 to 6
- cot: bfloat16 [1024, 128, 256], P(('img', 'sp')), parts along dimension 0, may hold values from -6 to 6
- layer_norm_gain: float32 [1408], replicated, may hold values from 0.1 to 1.9
- w_qkv: bfloat16 [1408, 2112], P('sp'), may hold values from -1 to 1
- w_out: bfloat16 [704, 1408], P('sp'), may hold values from -0.21875 to 0.21875
- w_deconv: bfloat16 [1408, 1536], P('sp'), may hold values from -0.15625 to 0.15625
- w_lateral: bfloat16 [384, 256], replicated, may hold values from -0.3125 to 0.3125
- lat_gain: float32 [256], replicated, may hold values from 0.1 to 1.9
- w_conv: bfloat16 [3, 3, 256, 256], replicated, may hold values from -0.125 to 0.125
- conv_gain: float32 [256], replicated, may hold values from 0.1 to 1.9
Outputs:
- x_one: bfloat16 [32768, 1408], P(('img', 'sp')), parts along dimension 0
- d_x1: bfloat16 [32768, 1408], P(('img', 'sp')), parts along dimension 0
- second_input_gradient: bfloat16 [32768, 1408], P(('img', 'sp')), parts along dimension 0
- g_out: float32 [5632, 1408], P(('img', 'sp')), parts along dimension 0
- g_deconv: float32 [11264, 1536], P(('img', 'sp')), parts along dimension 0
- g_lateral: float32 [3072, 256], P(('img', 'sp')), parts along dimension 0
- g_conv: float32 [24, 3, 256, 256], P('img', None, 'sp'), parts along dimension 0
The draws below stay inside these ranges and needn't reach their ends.
There are 8 independent parts, one for each index of `img`. The reference program is written for one: setup_inputs(seed, part) draws one part's arguments, and reference() takes and returns one part's arrays. A program takes and returns all parts, laid end to end along the dimension named above; an argument that names none is the same for every part. Nothing has to cross between parts.
All inputs are finite; a program needn't handle non-finite values.
Results may differ from the reference program's by a relative error of at most 0.03.
Values may be sent and summed in bfloat16 or wider, within the bound.
A program may use at most 128 MiB of HBM per device.

```python
import jax
import jax.numpy as jnp
from jax import lax

D = 1408
HEADS = 8
HEAD = 88
DEC = 384
LAT = 256
GRID_W = 64
ROWS_DEV = 2
INNER = 704
GRID_H = 64
TOKENS = 4096
TOK_DEV = 128
PIX_H = 128
PIX_W = 128
N_SP = 32


def draw_w_qkv(key, part):
    key = jax.random.fold_in(key, 7)
    query_key, key_key, value_key = jax.random.split(key, 3)
    base = 1.7 * D ** (-0.5)
    w_query = jax.random.normal(query_key, (D, HEADS, HEAD), jnp.float32) * base
    w_value = jax.random.normal(value_key, (D, HEADS * HEAD), jnp.float32) * D ** (-0.5)
    w_key = jax.random.normal(key_key, (D, HEADS, HEAD), jnp.float32) * base
    whole = jnp.concatenate([w_query.reshape(D, HEADS * HEAD), w_key.reshape(D, HEADS * HEAD), w_value], axis=1)
    return jnp.clip(whole, -1.0, 1.0).astype(jnp.bfloat16)


def steps_of(key, dims, cuts, smallest, largest):
    factor_of, own = 1.0, jax.random.fold_in(key, 6)
    for axis_at, parts in cuts:
        steps = jnp.exp(jax.random.uniform(jax.random.fold_in(own, axis_at), (parts,), jnp.float32, smallest / len(cuts), largest / len(cuts)))
        factor_of = factor_of * jnp.repeat(steps, dims[axis_at] // parts).reshape([-1 if axis == axis_at else 1 for axis in range(len(dims))])
    return factor_of


def normal_values(key, extent, width, most, cuts=(), kind=jnp.bfloat16):
    values = width * jax.random.normal(key, extent, jnp.float32)
    if cuts:
        values = values * steps_of(key, extent, cuts, -0.22, 0.18)
    return jnp.clip(values, -most, most).astype(kind)


def setup_inputs(seed: int = 0, part: int = 0) -> dict:
    streams_of = jax.random.split(jax.random.key(seed), 12)
    part_keys = jax.random.split(jax.random.fold_in(streams_of[11], part), 12)
    return {
        "y_one": normal_values(part_keys[0], (TOKENS, D), 1.0, 6.0, ((0, 32),)),
        "second_stream_state": normal_values(part_keys[1], (TOKENS, D), 1.0, 6.0, ((0, 32),)),
        "cot": normal_values(part_keys[2], (PIX_H, PIX_W, LAT), 1.0, 6.0, ((0, 32),)),
        "layer_norm_gain": jnp.clip(1.0 + 0.18 * jax.random.normal(streams_of[3], (D,), jnp.float32), 0.1, 1.9),
        "w_qkv": draw_w_qkv(jax.random.fold_in(streams_of[11], 71), part),
        "w_out": normal_values(streams_of[5], (INNER, D), INNER ** -0.5, 0.21875, ((0, 32),)),
        "w_deconv": normal_values(streams_of[6], (D, 4 * DEC), D ** -0.5, 0.15625, ((0, 32),)),
        "w_lateral": normal_values(streams_of[7], (DEC, LAT), DEC ** -0.5, 0.3125),
        "lat_gain": jnp.clip(1.0 + 0.18 * jax.random.normal(streams_of[8], (LAT,), jnp.float32), 0.1, 1.9),
        "w_conv": normal_values(streams_of[9], (3, 3, LAT, LAT), (9 * LAT) ** -0.5, 0.125),
        "conv_gain": jnp.clip(1.0 + 0.18 * jax.random.normal(streams_of[10], (LAT,), jnp.float32), 0.1, 1.9),
    }


epsilon = 1e-06
grad_scale = 0.015625

def apply_layer_norm(values):
    centered = values - lax.optimization_barrier(jnp.mean(values, axis=-1, keepdims=True))
    inverse = lax.rsqrt(lax.optimization_barrier(jnp.mean(centered * centered, axis=-1, keepdims=True)) + epsilon)
    return (centered * inverse, inverse)

def layer_norm_reverse(upstream, normalized_rows, inverse):
    first = lax.optimization_barrier(jnp.mean(upstream, axis=-1, keepdims=True))
    second = lax.optimization_barrier(jnp.mean(upstream * normalized_rows, axis=-1, keepdims=True))
    return inverse * (upstream - first - normalized_rows * second)

def conv_valid(padded, kernel):
    result = lax.conv_general_dilated(padded[None], kernel, (1, 1), 'VALID', dimension_numbers=('NHWC', 'HWIO', 'NHWC'), preferred_element_type=jnp.float32)
    return result[0]

def softmax_rows(scores):
    shifted = jnp.exp(scores - lax.optimization_barrier(jnp.max(scores, axis=1, keepdims=True)))
    return shifted / lax.optimization_barrier(jnp.sum(shifted, axis=1, keepdims=True))

def band_total(left, right, band_rows):

    def accumulate(total, index):
        left_band = lax.dynamic_slice_in_dim(left, index * band_rows, band_rows, 0)
        right_band = lax.dynamic_slice_in_dim(right, index * band_rows, band_rows, 0)
        product = lax.dot_general(left_band, right_band, (((0,), (0,)), ((), ())), preferred_element_type=jnp.float32)
        rounded = lax.optimization_barrier((product * grad_scale).astype(jnp.bfloat16))
        return (total + rounded.astype(jnp.float32), None)
    start = jnp.zeros((left.shape[1], right.shape[1]), jnp.float32)
    total, _ = lax.scan(accumulate, start, jnp.arange(N_SP, dtype=jnp.int32))
    return total

def conv_band_total(padded_act, grads):
    band_rows = 2 * ROWS_DEV

    def accumulate(total, index):
        window = lax.dynamic_slice_in_dim(padded_act, index * band_rows, band_rows + 2, 0)
        grad_band = lax.dynamic_slice_in_dim(grads, index * band_rows, band_rows, 0)
        patches = jnp.stack([window[row_shift:row_shift + band_rows, col_shift:col_shift + PIX_W].reshape(-1, LAT) for row_shift in range(3) for col_shift in range(3)])
        product = jnp.einsum('kpc,pd->kcd', patches.astype(jnp.float32), grad_band.reshape(-1, LAT).astype(jnp.float32))
        rounded = lax.optimization_barrier((product.reshape(3, 3, LAT, LAT) * grad_scale).astype(jnp.bfloat16))
        return (total + rounded.astype(jnp.float32), None)
    start = jnp.zeros((3, 3, LAT, LAT), jnp.float32)
    total, _ = lax.scan(accumulate, start, jnp.arange(N_SP, dtype=jnp.int32))
    return total

def split_heads(values):
    return values.reshape(TOKENS, HEADS, HEAD).transpose(1, 0, 2)

def merge_heads(values):
    return values.transpose(1, 0, 2).reshape(TOKENS, INNER)

def reference(y_one, second_stream_state, cot, layer_norm_gain, w_qkv, w_out, w_deconv, w_lateral, lat_gain, w_conv, conv_gain):
    score_scale = HEAD ** (-0.5)
    standardized_input, inverse_deviation = apply_layer_norm(second_stream_state.astype(jnp.float32))
    normalized_rows = (standardized_input * layer_norm_gain).astype(jnp.bfloat16)
    qkv = jnp.dot(normalized_rows, w_qkv, preferred_element_type=jnp.float32)
    queries = split_heads((qkv[:, :INNER] * score_scale).astype(jnp.bfloat16))
    keys = split_heads(qkv[:, INNER:2 * INNER].astype(jnp.bfloat16))
    values = split_heads(qkv[:, 2 * INNER:].astype(jnp.bfloat16))

    def head_forward(operands):
        query_head, key_head, value_head = operands
        probs = softmax_rows(jnp.dot(query_head, key_head.T, preferred_element_type=jnp.float32))
        return jnp.dot(probs.astype(jnp.bfloat16), value_head, preferred_element_type=jnp.float32).astype(jnp.bfloat16)
    attn = merge_heads(lax.map(head_forward, (queries, keys, values)))
    mixed = jnp.dot(attn, w_out, preferred_element_type=jnp.float32)
    x_one = (y_one.astype(jnp.float32) - mixed).astype(jnp.bfloat16)
    feature = ((y_one.astype(jnp.float32) + second_stream_state.astype(jnp.float32)) * 0.5).astype(jnp.bfloat16)
    upsampled = jnp.dot(feature, w_deconv, preferred_element_type=jnp.float32).astype(jnp.bfloat16)
    pixels = upsampled.reshape(GRID_H, GRID_W, 2, 2, DEC).transpose(0, 2, 1, 3, 4).reshape(PIX_H * PIX_W, DEC)
    lhat, linv = apply_layer_norm(jnp.dot(pixels, w_lateral, preferred_element_type=jnp.float32))
    activation = (lhat * lat_gain).astype(jnp.bfloat16).reshape(PIX_H, PIX_W, LAT)
    padded_act = jnp.pad(activation, ((1, 1), (1, 1), (0, 0)))
    chat, cinv = apply_layer_norm(conv_valid(padded_act, w_conv))
    dconv = layer_norm_reverse(cot.astype(jnp.float32) * conv_gain, chat, cinv).astype(jnp.bfloat16)
    flipped = w_conv[::-1, ::-1].transpose(0, 1, 3, 2)
    dact = conv_valid(jnp.pad(dconv, ((1, 1), (1, 1), (0, 0))), flipped)
    dlat = layer_norm_reverse(dact.reshape(PIX_H * PIX_W, LAT) * lat_gain, lhat, linv).astype(jnp.bfloat16)
    dpixels = jnp.dot(dlat, w_lateral.T, preferred_element_type=jnp.float32).astype(jnp.bfloat16)
    dup = dpixels.reshape(GRID_H, 2, GRID_W, 2, DEC).transpose(0, 2, 1, 3, 4).reshape(TOKENS, 4 * DEC)
    halfway_split = 0.5 * jnp.dot(dup, w_deconv.T, preferred_element_type=jnp.float32)
    d_x1 = halfway_split.astype(jnp.bfloat16)
    dattn = split_heads(jnp.dot(d_x1, w_out.T, preferred_element_type=jnp.float32).astype(jnp.bfloat16))

    def head_backward(operands):
        query_head, key_head, value_head, grad_head = operands
        probs = softmax_rows(jnp.dot(query_head, key_head.T, preferred_element_type=jnp.float32))
        weights = lax.optimization_barrier(probs.astype(jnp.bfloat16))
        wide = weights.astype(jnp.float32)
        dprob = jnp.dot(grad_head, value_head.T, preferred_element_type=jnp.float32)
        dscore = (wide * (dprob - lax.optimization_barrier(jnp.sum(wide * dprob, axis=1, keepdims=True)))).astype(jnp.bfloat16)
        query_grad = (jnp.dot(dscore, key_head, preferred_element_type=jnp.float32) * score_scale).astype(jnp.bfloat16)
        key_grad = jnp.dot(dscore.T, query_head, preferred_element_type=jnp.float32).astype(jnp.bfloat16)
        value_grad = jnp.dot(weights.T, grad_head, preferred_element_type=jnp.float32).astype(jnp.bfloat16)
        return (query_grad, key_grad, value_grad)
    query_grads, key_grads, value_grads = lax.map(head_backward, (queries, keys, values, dattn))
    dqkv = jnp.concatenate([merge_heads(query_grads), merge_heads(key_grads), merge_heads(value_grads)], axis=1)
    normalized_gradient = jnp.dot(dqkv, w_qkv.T, preferred_element_type=jnp.float32)
    second_input_gradient = (halfway_split + layer_norm_reverse(normalized_gradient * layer_norm_gain, standardized_input, inverse_deviation)).astype(jnp.bfloat16)
    g_out = band_total(attn, d_x1, TOK_DEV)
    g_deconv = band_total(feature, dup, TOK_DEV)
    g_lateral = band_total(pixels, dlat, 4 * TOK_DEV)
    g_conv = conv_band_total(padded_act, dconv)
    return (x_one, d_x1, second_input_gradient, g_out, g_deconv, g_lateral, g_conv)
```

```python
import functools

import jax
import jax.numpy as jnp
from jax import lax
from jax.experimental import pallas as pl
from jax.experimental.pallas import tpu as pltpu
from jax.sharding import PartitionSpec as P

HEADS = 8
HEAD = 88
DEC = 384
LAT = 256
GRID_W = 64


epsilon = 1e-06
grad_scale = 0.015625


def padded_2(block, sides, width):
    for axis, dim in sides:
        count = lax.axis_size(axis)
        forward = [(i, i + 1) for i in range(count - 1)]
        backward = [(target, source) for source, target in forward]
        low = lax.ppermute(
            lax.slice_in_dim(block, block.shape[dim] - width, None, axis=dim), axis, forward
        )
        high = lax.ppermute(lax.slice_in_dim(block, 0, width, axis=dim), axis, backward)
        block = jnp.concatenate([low, block, high], axis=dim)
    return block


def shifted_2(array, axis, by):
    count = lax.axis_size(axis)
    pairs = [(i, i + by) for i in range(count) if 0 <= i + by < count]
    return lax.ppermute(array, axis, pairs)


def apply_layer_norm(values):
    centered = values - jnp.mean(values, axis=-1, keepdims=True)
    inverse = lax.rsqrt(jnp.mean(centered * centered, axis=-1, keepdims=True) + epsilon)
    return (centered * inverse, inverse)


def layer_norm_reverse(upstream, normalized_rows, inverse):
    first = jnp.mean(upstream, axis=-1, keepdims=True)
    second = jnp.mean(upstream * normalized_rows, axis=-1, keepdims=True)
    return inverse * (upstream - first - normalized_rows * second)


def conv_valid(padded, kernel):
    result = lax.conv_general_dilated(
        padded[None],
        kernel,
        (1, 1),
        "VALID",
        dimension_numbers=("NHWC", "HWIO", "NHWC"),
        preferred_element_type=jnp.float32,
    )
    return result[0]


def rounded_part(left, right):
    product = lax.dot_general(
        left, right, (((0,), (0,)), ((), ())), preferred_element_type=jnp.float32
    )
    return (product * grad_scale).astype(jnp.bfloat16)


def to_heads(features, pieces):
    width = features.shape[0] // HEADS
    columns = features.shape[1] // pieces
    grouped = features.reshape(HEADS, width, pieces, columns).transpose(0, 2, 1, 3)
    return grouped.reshape(HEADS * pieces, width, columns)


def from_heads(received, pieces):
    width = received.shape[1]
    columns = received.shape[2]
    grouped = received.reshape(HEADS, pieces, width, columns).transpose(0, 2, 1, 3)
    return grouped.reshape(HEADS * width, pieces * columns)


def copies(features, pieces):
    width = features.shape[0] // HEADS
    columns = features.shape[1]
    spread = jnp.broadcast_to(
        features.reshape(HEADS, 1, width, columns), (HEADS, pieces, width, columns)
    )
    return spread.reshape(HEADS * pieces, width, columns)


MESH = pl.DeviceIdType.MESH
ROWS_PAD = 48
HEAD_PAD = 96
OUT_ROWS_PAD = 32
OUT_COLS_PAD = 1536


def place():
    s, i = lax.axis_index("sp"), lax.axis_index("img")
    return s // 8, (s // 4) % 2, s % 4, i // 2, i % 2


def at_sp(x, zl, y):
    return {"sp": (x * 2 + zl) * 4 + y}


def greet(targets):
    barrier = pltpu.get_barrier_semaphore()
    for target in targets:
        pl.semaphore_signal(barrier, inc=1, device_id=target, device_id_type=MESH)
    pl.semaphore_wait(barrier, len(targets))


def gather_kernel(shapes, *refs):
    count = len(shapes)
    ins, outs, shards, packs = (refs[k * count : (k + 1) * count] for k in range(4))
    send, recv, local = refs[4 * count :]
    x, zl, y, zh, core = place()
    xm, xp, xo = (x + 3) % 4, (x + 1) % 4, (x + 2) % 4
    left, right = at_sp(xm, zl, y), at_sp(xp, zl, y)
    across = (x * 2 + 1 - zl) * 4 + y
    up = {"img": ((zh + zl) % 4) * 2 + core, "sp": across}
    down = {"img": ((zh + zl + 3) % 4) * 2 + core, "sp": across}
    twin = {"img": zh * 2 + 1 - core}
    column = [at_sp(x, zl, (y + k) % 4) for k in (1, 2, 3)]
    greet(column + [left, right, up, down, twin])
    copies = {}

    def push(a, slot, src, dst, target):
        copy = pltpu.make_async_remote_copy(
            src_ref=src,
            dst_ref=dst,
            send_sem=send.at[a, slot],
            recv_sem=recv.at[a, slot],
            device_id=target,
            device_id_type=MESH,
        )
        copy.start()
        copies[a, slot] = copy

    def part(a):
        half = shapes[a][3] // 2
        return half, pl.multiple_of(core * half, 128)

    def region(a, bx, bz, lo, size):
        half, first = part(a)
        return outs[a].at[bx * 2 + bz, pl.ds(lo, size), pl.ds(first, half)]

    def forward(a, slot, bx, bz, lo, size, target):
        piece = region(a, bx, bz, lo, size)
        push(a, slot, piece, piece, target)

    for a in range(count):
        half, first = part(a)
        mine = ins[a].at[:, pl.ds(first, half)]
        for k in range(3):
            push(a, k, mine, shards[a].at[y], column[k])
        shards[a][y] = ins[a][:, pl.ds(first, half)]
    keeps = []
    for a in range(count):
        rows, per, block, _ = shapes[a]
        half, first = part(a)
        low = (block // 32) * 16
        high = block - low
        for k in range(3):
            copies[a, k].wait_recv()
        r = lax.broadcasted_iota(jnp.int32, (block, 4 * rows), 0)
        c = lax.broadcasted_iota(jnp.int32, (block, 4 * rows), 1)
        skipped = jnp.zeros_like(r)
        for k in (1, 2, 3):
            skipped += jnp.where(r >= k * per, rows - per, 0)
        pick = jnp.where(c == r + skipped, 1.0, 0.0).astype(jnp.bfloat16)
        packs[a][...] = jnp.dot(
            pick, shards[a][...].reshape(4 * rows, half), preferred_element_type=jnp.float32
        ).astype(jnp.bfloat16)
        own, whole = packs[a], region(a, x, zl, 0, block)
        keep = pltpu.make_async_copy(own, whole, local.at[a])
        keep.start()
        keeps.append(keep)
        push(a, 3, own, whole, right)
        push(a, 4, own, whole, left)
        push(a, 7, own.at[pl.ds(0, low)], region(a, x, zl, 0, low), up)
        push(a, 8, own.at[pl.ds(low, high)], region(a, x, zl, low, high), down)
        push(a, 15, own, whole, twin)

    def near(a):
        block = shapes[a][2]
        low = (block // 32) * 16
        high = block - low
        copies[a, 3].wait_recv()
        forward(a, 5, xm, zl, 0, low, right)
        forward(a, 9, xm, zl, 0, low, up)
        forward(a, 10, xm, zl, low, high, down)
        forward(a, 16, xm, zl, 0, block, twin)
        copies[a, 4].wait_recv()
        forward(a, 6, xp, zl, low, high, left)
        forward(a, 11, xp, zl, 0, low, up)
        forward(a, 12, xp, zl, low, high, down)
        forward(a, 17, xp, zl, 0, block, twin)

    def far(a):
        block = shapes[a][2]
        low = (block // 32) * 16
        high = block - low
        copies[a, 5].wait_recv()
        forward(a, 13, xo, zl, 0, low, up)
        forward(a, 18, xo, zl, 0, low, twin)
        copies[a, 6].wait_recv()
        forward(a, 14, xo, zl, low, high, down)
        forward(a, 19, xo, zl, low, high, twin)

    def deep(a):
        block = shapes[a][2]
        low = (block // 32) * 16
        high = block - low
        for n, bx in enumerate((x, xm, xp, xo)):
            copies[a, 7 + 2 * n].wait_recv()
            forward(a, 20 + 2 * n, bx, 1 - zl, 0, low, twin)
            copies[a, 8 + 2 * n].wait_recv()
            forward(a, 21 + 2 * n, bx, 1 - zl, low, high, twin)

    for step in range(count + 2):
        if step < count:
            near(step)
        if 0 <= step - 1 < count:
            far(step - 1)
        if 0 <= step - 2 < count:
            deep(step - 2)
    for a in range(count):
        for slot in range(15, 28):
            copies[a, slot].wait_recv()
    for keep in keeps:
        keep.wait()
    for copy in copies.values():
        copy.wait_send()


def gather_weights(shards, pers):
    count = len(shards)
    shapes = []
    for shard, per in zip(shards, pers):
        block = -(-4 * per // 16) * 16
        shapes.append((shard.shape[0], per, block, shard.shape[1]))
    halves = [(rows, block, width // 2) for rows, _, block, width in shapes]
    return pl.pallas_call(
        functools.partial(gather_kernel, shapes),
        out_shape=[
            jax.ShapeDtypeStruct((8, block, width), jnp.bfloat16) for _, _, block, width in shapes
        ],
        in_specs=[pl.BlockSpec(memory_space=pltpu.VMEM)] * count,
        out_specs=[pl.BlockSpec(memory_space=pl.ANY)] * count,
        scratch_shapes=[pltpu.VMEM((4, rows, half), jnp.bfloat16) for rows, _, half in halves]
        + [pltpu.VMEM((block, half), jnp.bfloat16) for _, block, half in halves]
        + [
            pltpu.SemaphoreType.DMA((count, 28)),
            pltpu.SemaphoreType.DMA((count, 28)),
            pltpu.SemaphoreType.DMA((count,)),
        ],
        compiler_params=pltpu.CompilerParams(
            collective_id=0, has_side_effects=True, vmem_limit_bytes=32 * 2**20
        ),
    )(*shards)


def pad_heads(features):
    groups = features.reshape(-1, HEAD, features.shape[-1])
    return jnp.pad(groups, ((0, 0), (0, HEAD_PAD - HEAD), (0, 0))).reshape(
        -1, features.shape[-1]
    )


def trim_heads(features):
    groups = features.reshape(-1, HEAD_PAD, features.shape[-1])
    return groups[:, :HEAD].reshape(-1, features.shape[-1])


def per_device(
    y_one,
    second_stream_state,
    cot,
    layer_norm_gain,
    w_qkv,
    w_out,
    w_deconv,
    w_lateral,
    lat_gain,
    w_conv,
    conv_gain,
):
    devices = lax.axis_size("sp")
    pieces = devices // HEADS
    tokens_here = y_one.shape[0]
    rows_here = tokens_here // GRID_W
    inner = HEADS * HEAD
    score_scale = HEAD ** (-0.5)
    standardized_input, inverse_deviation = apply_layer_norm(
        second_stream_state.astype(jnp.float32)
    )
    normalized_rows = (standardized_input * layer_norm_gain).astype(jnp.bfloat16)
    depth, out_depth = w_qkv.shape[0], w_out.shape[0]
    qkv_shard = jnp.pad(
        w_qkv.reshape(depth, 3 * HEADS, HEAD),
        ((0, ROWS_PAD - depth), (0, 0), (0, HEAD_PAD - HEAD)),
    ).reshape(ROWS_PAD, 3 * HEADS * HEAD_PAD)
    out_shard = jnp.pad(
        w_out, ((0, OUT_ROWS_PAD - out_depth), (0, OUT_COLS_PAD - w_out.shape[1]))
    )
    deconv_shard = jnp.pad(w_deconv, ((0, ROWS_PAD - depth), (0, 0)))
    deconv_full, qkv_full, out_full = gather_weights(
        [deconv_shard, qkv_shard, out_shard], [depth, depth, out_depth]
    )
    deconv_full = deconv_full.reshape(devices * depth, -1)
    qkv_full = qkv_full.reshape(devices * depth, -1)
    out_full = out_full[:, :HEAD, : w_out.shape[1]].reshape(inner, -1)
    projected = trim_heads(
        lax.dot_general(
            qkv_full, normalized_rows, (((0,), (1,)), ((), ())), preferred_element_type=jnp.float32
        )
    )
    queries = (projected[:inner] * score_scale).astype(jnp.bfloat16)
    keys = projected[inner : 2 * inner].astype(jnp.bfloat16)
    values = projected[2 * inner :].astype(jnp.bfloat16)
    query_head = lax.all_to_all(
        to_heads(queries, pieces), "sp", split_axis=0, concat_axis=2, tiled=True
    )[0]
    key_routed, value_routed = (
        lax.all_to_all(copies(keys, pieces), "sp", split_axis=0, concat_axis=2, tiled=True),
        lax.all_to_all(copies(values, pieces), "sp", split_axis=0, concat_axis=2, tiled=True),
    )
    key_head = key_routed[0]
    value_head = value_routed[0]
    total_queries = query_head.shape[1]
    block = min(512, total_queries)
    count_blocks = total_queries // block
    query_blocks = query_head.reshape(HEAD, count_blocks, block).transpose(1, 0, 2)

    def attend(query_block):
        scores = lax.dot_general(
            query_block, key_head, (((0,), (0,)), ((), ())), preferred_element_type=jnp.float32
        )
        shifted = jnp.exp(scores - jnp.max(scores, axis=1, keepdims=True))
        weights = (shifted / jnp.sum(shifted, axis=1, keepdims=True)).astype(jnp.bfloat16)
        output = lax.dot_general(
            value_head, weights, (((1,), (1,)), ((), ())), preferred_element_type=jnp.float32
        ).astype(jnp.bfloat16)
        return (output, weights)

    attended, kept_weights = lax.map(attend, query_blocks)
    attended = attended.transpose(1, 0, 2).reshape(1, HEAD, total_queries)
    attn_band = from_heads(
        lax.all_to_all(attended, "sp", split_axis=2, concat_axis=0, tiled=True), pieces
    )
    mixed = lax.dot_general(
        attn_band, out_full, (((0,), (0,)), ((), ())), preferred_element_type=jnp.float32
    )
    x_one = (y_one.astype(jnp.float32) - mixed).astype(jnp.bfloat16)
    feature = ((y_one.astype(jnp.float32) + second_stream_state.astype(jnp.float32)) * 0.5).astype(
        jnp.bfloat16
    )
    upsampled = jnp.dot(feature, deconv_full, preferred_element_type=jnp.float32).astype(
        jnp.bfloat16
    )
    pixel_rows = 2 * rows_here
    pixel_cols = 2 * GRID_W
    pixels = (
        upsampled.reshape(rows_here, GRID_W, 2, 2, DEC)
        .transpose(0, 2, 1, 3, 4)
        .reshape(pixel_rows * pixel_cols, DEC)
    )
    lhat, linv = apply_layer_norm(jnp.dot(pixels, w_lateral, preferred_element_type=jnp.float32))
    activation = (lhat * lat_gain).astype(jnp.bfloat16).reshape(pixel_rows, pixel_cols, LAT)
    extended = padded_2(activation, (("sp", 0),), 1)
    padded = jnp.pad(extended, ((0, 0), (1, 1), (0, 0)))
    chat, cinv = apply_layer_norm(conv_valid(padded, w_conv))
    dconv = layer_norm_reverse(cot.astype(jnp.float32) * conv_gain, chat, cinv).astype(jnp.bfloat16)
    flipped = w_conv[::-1, ::-1].transpose(0, 1, 3, 2)
    spread_rows = conv_valid(jnp.pad(dconv, ((2, 2), (1, 1), (0, 0))), flipped)
    from_below = shifted_2(spread_rows[-1].astype(jnp.bfloat16), "sp", 1).astype(jnp.float32)
    from_above = shifted_2(spread_rows[0].astype(jnp.bfloat16), "sp", -1).astype(jnp.float32)
    dact = spread_rows[1:-1]
    dact = dact.at[0].add(from_below).at[-1].add(from_above)
    patches = jnp.stack(
        [
            padded[row_shift : row_shift + pixel_rows, col_shift : col_shift + pixel_cols].reshape(
                -1, LAT
            )
            for row_shift in range(3)
            for col_shift in range(3)
        ]
    )
    conv_product = jnp.einsum(
        "kpc,pd->ckd", patches, dconv.reshape(-1, LAT), preferred_element_type=jnp.float32
    )
    conv_part = (conv_product.reshape(LAT, 9 * LAT) * grad_scale).astype(jnp.bfloat16)
    dlat = layer_norm_reverse(dact.reshape(-1, LAT) * lat_gain, lhat, linv).astype(jnp.bfloat16)
    lat_part = rounded_part(pixels, dlat)
    dpixels = lax.dot_general(
        dlat, w_lateral, (((1,), (1,)), ((), ())), preferred_element_type=jnp.float32
    ).astype(jnp.bfloat16)
    dup = (
        dpixels.reshape(rows_here, 2, GRID_W, 2, DEC)
        .transpose(0, 2, 1, 3, 4)
        .reshape(tokens_here, 4 * DEC)
    )
    dec_part = rounded_part(feature, dup)
    g_deconv = lax.psum_scatter(dec_part, "sp", scatter_dimension=0, tiled=True).astype(jnp.float32)
    halfway_split = 0.5 * lax.dot_general(
        dup, deconv_full, (((1,), (1,)), ((), ())), preferred_element_type=jnp.float32
    )
    d_x1 = halfway_split.astype(jnp.bfloat16)
    dattn = lax.dot_general(
        out_full, d_x1, (((1,), (1,)), ((), ())), preferred_element_type=jnp.float32
    ).astype(jnp.bfloat16)
    out_product = lax.dot_general(
        attn_band, d_x1, (((1,), (0,)), ((), ())), preferred_element_type=jnp.float32
    )
    out_part = (out_product * grad_scale).astype(jnp.bfloat16)
    g_out = lax.psum_scatter(out_part, "sp", scatter_dimension=0, tiled=True).astype(jnp.float32)
    grad_head = lax.all_to_all(
        to_heads(dattn, pieces), "sp", split_axis=0, concat_axis=2, tiled=True
    )[0]
    grad_blocks = grad_head.reshape(HEAD, count_blocks, block).transpose(1, 0, 2)

    def backward_block(carry, operands):
        key_grad, value_grad = carry
        query_block, grad_block, weights = operands
        wide = weights.astype(jnp.float32)
        dprob = lax.dot_general(
            grad_block, value_head, (((0,), (0,)), ((), ())), preferred_element_type=jnp.float32
        )
        dscore = (wide * (dprob - jnp.sum(wide * dprob, axis=1, keepdims=True))).astype(
            jnp.bfloat16
        )
        query_grad = lax.dot_general(
            key_head, dscore, (((1,), (1,)), ((), ())), preferred_element_type=jnp.float32
        )
        query_grad = (query_grad * score_scale).astype(jnp.bfloat16)
        key_grad = key_grad + lax.dot_general(
            query_block, dscore, (((1,), (0,)), ((), ())), preferred_element_type=jnp.float32
        )
        value_grad = value_grad + lax.dot_general(
            grad_block, weights, (((1,), (0,)), ((), ())), preferred_element_type=jnp.float32
        )
        return ((key_grad, value_grad), query_grad)

    zero_grads = jnp.zeros(key_head.shape, jnp.float32)
    (key_grad, value_grad), query_grads = lax.scan(
        backward_block, (zero_grads, zero_grads), (query_blocks, grad_blocks, kept_weights)
    )
    query_grads = query_grads.transpose(1, 0, 2).reshape(1, HEAD, total_queries)
    dq_band = from_heads(
        lax.all_to_all(query_grads, "sp", split_axis=2, concat_axis=0, tiled=True), pieces
    )
    key_parts, value_parts = (
        lax.all_to_all(
            key_grad.astype(jnp.bfloat16), "sp", split_axis=1, concat_axis=0, tiled=True
        ).astype(key_grad.dtype),
        lax.all_to_all(
            value_grad.astype(jnp.bfloat16), "sp", split_axis=1, concat_axis=0, tiled=True
        ).astype(value_grad.dtype),
    )
    dk_band = (
        key_parts.reshape(HEADS, pieces, HEAD, tokens_here)
        .sum(axis=1)
        .reshape(inner, tokens_here)
        .astype(jnp.bfloat16)
    )
    dv_band = (
        value_parts.reshape(HEADS, pieces, HEAD, tokens_here)
        .sum(axis=1)
        .reshape(inner, tokens_here)
        .astype(jnp.bfloat16)
    )
    dqkv = jnp.concatenate([dq_band, dk_band, dv_band], axis=0)
    normalized_gradient = lax.dot_general(
        pad_heads(dqkv), qkv_full, (((0,), (1,)), ((), ())), preferred_element_type=jnp.float32
    )
    second_input_gradient = (
        halfway_split
        + layer_norm_reverse(
            normalized_gradient * layer_norm_gain, standardized_input, inverse_deviation
        )
    ).astype(jnp.bfloat16)
    g_lateral, conv_rows = (
        lax.psum_scatter(lat_part, "sp", scatter_dimension=0, tiled=True).astype(jnp.float32),
        lax.psum_scatter(conv_part, "sp", scatter_dimension=0, tiled=True).astype(jnp.float32),
    )
    g_conv = conv_rows.reshape(conv_rows.shape[0], 3, 3, LAT).transpose(1, 2, 0, 3)
    return (x_one, d_x1, second_input_gradient, g_out, g_deconv, g_lateral, g_conv)


def solution(mesh):
    return jax.shard_map(
        per_device,
        mesh=mesh,
        in_specs=(
            P(("img", "sp"), None),
            P(("img", "sp"), None),
            P(("img", "sp"), None, None),
            P(),
            P("sp", None),
            P("sp", None),
            P("sp", None),
            P(),
            P(),
            P(),
            P(),
        ),
        out_specs=(
            P(("img", "sp"), None),
            P(("img", "sp"), None),
            P(("img", "sp"), None),
            P(("img", "sp"), None),
            P(("img", "sp"), None),
            P(("img", "sp"), None),
            P("img", None, "sp", None),
        ),
        check_vma=False,
    )
```

```python
import functools

import jax
import jax.numpy as jnp
from jax import lax
from jax.experimental import pallas as pl
from jax.experimental.pallas import tpu as pltpu
from jax.sharding import PartitionSpec as P

HEADS = 8
HEAD = 88
DEC = 384
LAT = 256
GRID_W = 64


epsilon = 1e-06
grad_scale = 0.015625


def padded_2(block, sides, width):
    for axis, dim in sides:
        count = lax.axis_size(axis)
        forward = [(i, i + 1) for i in range(count - 1)]
        backward = [(target, source) for source, target in forward]
        low = lax.ppermute(
            lax.slice_in_dim(block, block.shape[dim] - width, None, axis=dim), axis, forward
        )
        high = lax.ppermute(lax.slice_in_dim(block, 0, width, axis=dim), axis, backward)
        block = jnp.concatenate([low, block, high], axis=dim)
    return block


def shifted_2(array, axis, by):
    count = lax.axis_size(axis)
    pairs = [(i, i + by) for i in range(count) if 0 <= i + by < count]
    return lax.ppermute(array, axis, pairs)


def apply_layer_norm(values):
    centered = values - jnp.mean(values, axis=-1, keepdims=True)
    inverse = lax.rsqrt(jnp.mean(centered * centered, axis=-1, keepdims=True) + epsilon)
    return (centered * inverse, inverse)


def layer_norm_reverse(upstream, normalized_rows, inverse):
    first = jnp.mean(upstream, axis=-1, keepdims=True)
    second = jnp.mean(upstream * normalized_rows, axis=-1, keepdims=True)
    return inverse * (upstream - first - normalized_rows * second)


def conv_valid(padded, kernel):
    result = lax.conv_general_dilated(
        padded[None],
        kernel,
        (1, 1),
        "VALID",
        dimension_numbers=("NHWC", "HWIO", "NHWC"),
        preferred_element_type=jnp.float32,
    )
    return result[0]


def rounded_part(left, right):
    product = lax.dot_general(
        left, right, (((0,), (0,)), ((), ())), preferred_element_type=jnp.float32
    )
    return (product * grad_scale).astype(jnp.bfloat16)


def to_heads(features, pieces):
    width = features.shape[0] // HEADS
    columns = features.shape[1] // pieces
    grouped = features.reshape(HEADS, width, pieces, columns).transpose(0, 2, 1, 3)
    return grouped.reshape(HEADS * pieces, width, columns)


def from_heads(received, pieces):
    width = received.shape[1]
    columns = received.shape[2]
    grouped = received.reshape(HEADS, pieces, width, columns).transpose(0, 2, 1, 3)
    return grouped.reshape(HEADS * width, pieces * columns)


def copies(features, pieces):
    width = features.shape[0] // HEADS
    columns = features.shape[1]
    spread = jnp.broadcast_to(
        features.reshape(HEADS, 1, width, columns), (HEADS, pieces, width, columns)
    )
    return spread.reshape(HEADS * pieces, width, columns)


MESH = pl.DeviceIdType.MESH
ROWS_PAD = 48
HEAD_PAD = 96
OUT_ROWS_PAD = 32
OUT_COLS_PAD = 1536


def place():
    s, i = lax.axis_index("sp"), lax.axis_index("img")
    return s // 8, (s // 4) % 2, s % 4, i // 2, i % 2


def at_sp(x, zl, y):
    return {"sp": (x * 2 + zl) * 4 + y}


def greet(targets):
    barrier = pltpu.get_barrier_semaphore()
    for target in targets:
        pl.semaphore_signal(barrier, inc=1, device_id=target, device_id_type=MESH)
    pl.semaphore_wait(barrier, len(targets))


def gather_kernel(shapes, *refs):
    count = len(shapes)
    ins, outs, shards, packs = (refs[k * count : (k + 1) * count] for k in range(4))
    send, recv, local = refs[4 * count :]
    x, zl, y, zh, core = place()
    xm, xp, xo = (x + 3) % 4, (x + 1) % 4, (x + 2) % 4
    left, right = at_sp(xm, zl, y), at_sp(xp, zl, y)
    across = (x * 2 + 1 - zl) * 4 + y
    up = {"img": ((zh + zl) % 4) * 2 + core, "sp": across}
    down = {"img": ((zh + zl + 3) % 4) * 2 + core, "sp": across}
    twin = {"img": zh * 2 + 1 - core}
    column = [at_sp(x, zl, (y + k) % 4) for k in (1, 2, 3)]
    greet(column + [left, right, up, down, twin])
    copies = {}

    def push(a, slot, src, dst, target):
        copy = pltpu.make_async_remote_copy(
            src_ref=src,
            dst_ref=dst,
            send_sem=send.at[a, slot],
            recv_sem=recv.at[a, slot],
            device_id=target,
            device_id_type=MESH,
        )
        copy.start()
        copies[a, slot] = copy

    def part(a):
        half = shapes[a][3] // 2
        return half, pl.multiple_of(core * half, 128)

    def region(a, bx, bz, lo, size):
        half, first = part(a)
        return outs[a].at[bx * 2 + bz, pl.ds(lo, size), pl.ds(first, half)]

    def forward(a, slot, bx, bz, lo, size, target):
        piece = region(a, bx, bz, lo, size)
        push(a, slot, piece, piece, target)

    for a in range(count):
        half, first = part(a)
        mine = ins[a].at[:, pl.ds(first, half)]
        for k in range(3):
            push(a, k, mine, shards[a].at[y], column[k])
        shards[a][y] = ins[a][:, pl.ds(first, half)]
    keeps = []
    for a in range(count):
        rows, per, block, _ = shapes[a]
        half, first = part(a)
        low = (block // 32) * 16
        high = block - low
        for k in range(3):
            copies[a, k].wait_recv()
        r = lax.broadcasted_iota(jnp.int32, (block, 4 * rows), 0)
        c = lax.broadcasted_iota(jnp.int32, (block, 4 * rows), 1)
        skipped = jnp.zeros_like(r)
        for k in (1, 2, 3):
            skipped += jnp.where(r >= k * per, rows - per, 0)
        pick = jnp.where(c == r + skipped, 1.0, 0.0).astype(jnp.bfloat16)
        packs[a][...] = jnp.dot(
            pick, shards[a][...].reshape(4 * rows, half), preferred_element_type=jnp.float32
        ).astype(jnp.bfloat16)
        own, whole = packs[a], region(a, x, zl, 0, block)
        keep = pltpu.make_async_copy(own, whole, local.at[a])
        keep.start()
        keeps.append(keep)
        push(a, 3, own, whole, right)
        push(a, 4, own, whole, left)
        push(a, 7, own.at[pl.ds(0, low)], region(a, x, zl, 0, low), up)
        push(a, 8, own.at[pl.ds(low, high)], region(a, x, zl, low, high), down)
        push(a, 15, own, whole, twin)

    def near(a):
        block = shapes[a][2]
        low = (block // 32) * 16
        high = block - low
        copies[a, 3].wait_recv()
        forward(a, 5, xm, zl, 0, low, right)
        forward(a, 9, xm, zl, 0, low, up)
        forward(a, 10, xm, zl, low, high, down)
        forward(a, 16, xm, zl, 0, block, twin)
        copies[a, 4].wait_recv()
        forward(a, 6, xp, zl, low, high, left)
        forward(a, 11, xp, zl, 0, low, up)
        forward(a, 12, xp, zl, low, high, down)
        forward(a, 17, xp, zl, 0, block, twin)

    def far(a):
        block = shapes[a][2]
        low = (block // 32) * 16
        high = block - low
        copies[a, 5].wait_recv()
        forward(a, 13, xo, zl, 0, low, up)
        forward(a, 18, xo, zl, 0, low, twin)
        copies[a, 6].wait_recv()
        forward(a, 14, xo, zl, low, high, down)
        forward(a, 19, xo, zl, low, high, twin)

    def deep(a):
        block = shapes[a][2]
        low = (block // 32) * 16
        high = block - low
        for n, bx in enumerate((x, xm, xp, xo)):
            copies[a, 7 + 2 * n].wait_recv()
            forward(a, 20 + 2 * n, bx, 1 - zl, 0, low, twin)
            copies[a, 8 + 2 * n].wait_recv()
            forward(a, 21 + 2 * n, bx, 1 - zl, low, high, twin)

    for step in range(count + 2):
        if step < count:
            near(step)
        if 0 <= step - 1 < count:
            far(step - 1)
        if 0 <= step - 2 < count:
            deep(step - 2)
    for a in range(count):
        for slot in range(15, 28):
            copies[a, slot].wait_recv()
    for keep in keeps:
        keep.wait()
    for copy in copies.values():
        copy.wait_send()


def gather_weights(shards, pers):
    count = len(shards)
    shapes = []
    for shard, per in zip(shards, pers):
        block = -(-4 * per // 16) * 16
        shapes.append((shard.shape[0], per, block, shard.shape[1]))
    halves = [(rows, block, width // 2) for rows, _, block, width in shapes]
    return pl.pallas_call(
        functools.partial(gather_kernel, shapes),
        out_shape=[
            jax.ShapeDtypeStruct((8, block, width), jnp.bfloat16) for _, _, block, width in shapes
        ],
        in_specs=[pl.BlockSpec(memory_space=pltpu.VMEM)] * count,
        out_specs=[pl.BlockSpec(memory_space=pl.ANY)] * count,
        scratch_shapes=[pltpu.VMEM((4, rows, half), jnp.bfloat16) for rows, _, half in halves]
        + [pltpu.VMEM((block, half), jnp.bfloat16) for _, block, half in halves]
        + [
            pltpu.SemaphoreType.DMA((count, 28)),
            pltpu.SemaphoreType.DMA((count, 28)),
            pltpu.SemaphoreType.DMA((count,)),
        ],
        compiler_params=pltpu.CompilerParams(
            collective_id=0, has_side_effects=True, vmem_limit_bytes=32 * 2**20
        ),
    )(*shards)


def pad_heads(features):
    groups = features.reshape(-1, HEAD, features.shape[-1])
    return jnp.pad(groups, ((0, 0), (0, HEAD_PAD - HEAD), (0, 0))).reshape(
        -1, features.shape[-1]
    )


def trim_heads(features):
    groups = features.reshape(-1, HEAD_PAD, features.shape[-1])
    return groups[:, :HEAD].reshape(-1, features.shape[-1])


def scatter_kernel(plan, *refs):
    count = len(plan)
    arrays = 1 + max(source for source, _, _, _ in plan)
    ins, outs = refs[:arrays], refs[arrays : arrays + count]
    rest = refs[arrays + count :]
    land1, sum1, land2, sum2, land3 = (rest[k * count : (k + 1) * count] for k in range(5))
    send, recv = rest[5 * count :]
    x, zl, y, zh, core = place()
    across = at_sp(x, 1 - zl, y)
    row = [(x + k) % 4 for k in (1, 2, 3)]
    column = [(y + k) % 4 for k in (1, 2, 3)]
    greet([at_sp(k, zl, y) for k in row] + [at_sp(x, zl, k) for k in column] + [across])
    copies = {}

    def push(n, slot, src, dst, target):
        copy = pltpu.make_async_remote_copy(
            src_ref=src,
            dst_ref=dst,
            send_sem=send.at[n, slot],
            recv_sem=recv.at[n, slot],
            device_id=target,
            device_id_type=MESH,
        )
        copy.start()
        copies[n, slot] = copy

    def to_row(k):
        return at_sp(row[k], zl, y)

    def to_column(k):
        return at_sp(x, zl, column[k])

    for n, (source, first, width, x_first) in enumerate(plan):
        view = ins[source].at[:, :, :, :, pl.ds(first, width)]
        for k in range(3):
            if x_first:
                push(n, k, view.at[row[k]], land1[n].at[k], to_row(k))
            else:
                push(n, k, view.at[:, :, column[k]], land1[n].at[k], to_column(k))
    for n, (source, first, width, x_first) in enumerate(plan):
        for k in range(3):
            copies[n, k].wait_recv()
        outer, inner = sum1[n].shape[0], sum1[n].shape[1]

        def add(t, carry):
            p, q = t // inner, t % inner
            if x_first:
                own = ins[source][x, p, q, :, pl.ds(first, width)]
            else:
                own = ins[source][p, q, y, :, pl.ds(first, width)]
            total = own.astype(jnp.float32)
            for k in range(3):
                total += land1[n][k, p, q].astype(jnp.float32)
            sum1[n][p, q] = total.astype(jnp.bfloat16)
            return carry

        lax.fori_loop(0, outer * inner, add, 0)
        for k in range(3):
            if x_first:
                push(n, 3 + k, sum1[n].at[:, column[k]], land2[n].at[k], to_column(k))
            else:
                push(n, 3 + k, sum1[n].at[row[k]], land2[n].at[k], to_row(k))
    for n, (source, first, width, x_first) in enumerate(plan):
        for k in range(3):
            copies[n, 3 + k].wait_recv()
        for p in range(2):
            own = sum1[n][p, y] if x_first else sum1[n][x, p]
            total = own.astype(jnp.float32)
            for k in range(3):
                total += land2[n][k, p].astype(jnp.float32)
            sum2[n][p] = total.astype(jnp.bfloat16)
        push(n, 6, sum2[n].at[1 - zl], land3[n], across)
    for n in range(count):
        copies[n, 6].wait_recv()
        outs[n][...] = sum2[n][zl].astype(jnp.float32) + land3[n][...].astype(jnp.float32)
    for copy in copies.values():
        copy.wait_send()


def scatter_sums(parts, plan):
    count = len(plan)
    rows = [parts[source].shape[3] for source, _, _, _ in plan]
    widths = [width for _, _, width, _ in plan]

    def buffers(*lead):
        return [pltpu.VMEM((*lead, r, w), jnp.bfloat16) for r, w in zip(rows, widths)]

    def by_order(first, second, lead=()):
        return [
            pltpu.VMEM((*lead, *(first if order else second), r, w), jnp.bfloat16)
            for r, w, (_, _, _, order) in zip(rows, widths, plan)
        ]

    return pl.pallas_call(
        functools.partial(scatter_kernel, plan),
        out_shape=[jax.ShapeDtypeStruct((r, w), jnp.float32) for r, w in zip(rows, widths)],
        in_specs=[pl.BlockSpec(memory_space=pltpu.VMEM)] * len(parts),
        out_specs=[pl.BlockSpec(memory_space=pltpu.VMEM)] * count,
        scratch_shapes=by_order((2, 4), (4, 2), (3,))
        + by_order((2, 4), (4, 2))
        + buffers(3, 2)
        + buffers(2)
        + buffers()
        + [pltpu.SemaphoreType.DMA((count, 7)), pltpu.SemaphoreType.DMA((count, 7))],
        compiler_params=pltpu.CompilerParams(
            collective_id=1, has_side_effects=True, vmem_limit_bytes=48 * 2**20
        ),
    )(*parts)


def per_device(
    y_one,
    second_stream_state,
    cot,
    layer_norm_gain,
    w_qkv,
    w_out,
    w_deconv,
    w_lateral,
    lat_gain,
    w_conv,
    conv_gain,
):
    devices = lax.axis_size("sp")
    pieces = devices // HEADS
    tokens_here = y_one.shape[0]
    rows_here = tokens_here // GRID_W
    inner = HEADS * HEAD
    score_scale = HEAD ** (-0.5)
    standardized_input, inverse_deviation = apply_layer_norm(
        second_stream_state.astype(jnp.float32)
    )
    normalized_rows = (standardized_input * layer_norm_gain).astype(jnp.bfloat16)
    depth, out_depth = w_qkv.shape[0], w_out.shape[0]
    qkv_shard = jnp.pad(
        w_qkv.reshape(depth, 3 * HEADS, HEAD),
        ((0, ROWS_PAD - depth), (0, 0), (0, HEAD_PAD - HEAD)),
    ).reshape(ROWS_PAD, 3 * HEADS * HEAD_PAD)
    out_shard = jnp.pad(
        w_out, ((0, OUT_ROWS_PAD - out_depth), (0, OUT_COLS_PAD - w_out.shape[1]))
    )
    deconv_shard = jnp.pad(w_deconv, ((0, ROWS_PAD - depth), (0, 0)))
    deconv_full, qkv_full, out_full = gather_weights(
        [deconv_shard, qkv_shard, out_shard], [depth, depth, out_depth]
    )
    deconv_full = deconv_full.reshape(devices * depth, -1)
    qkv_full = qkv_full.reshape(devices * depth, -1)
    out_full = out_full[:, :HEAD, : w_out.shape[1]].reshape(inner, -1)
    projected = trim_heads(
        lax.dot_general(
            qkv_full, normalized_rows, (((0,), (1,)), ((), ())), preferred_element_type=jnp.float32
        )
    )
    queries = (projected[:inner] * score_scale).astype(jnp.bfloat16)
    keys = projected[inner : 2 * inner].astype(jnp.bfloat16)
    values = projected[2 * inner :].astype(jnp.bfloat16)
    query_head = lax.all_to_all(
        to_heads(queries, pieces), "sp", split_axis=0, concat_axis=2, tiled=True
    )[0]
    key_routed, value_routed = (
        lax.all_to_all(copies(keys, pieces), "sp", split_axis=0, concat_axis=2, tiled=True),
        lax.all_to_all(copies(values, pieces), "sp", split_axis=0, concat_axis=2, tiled=True),
    )
    key_head = key_routed[0]
    value_head = value_routed[0]
    total_queries = query_head.shape[1]
    block = min(512, total_queries)
    count_blocks = total_queries // block
    query_blocks = query_head.reshape(HEAD, count_blocks, block).transpose(1, 0, 2)

    def attend(query_block):
        scores = lax.dot_general(
            query_block, key_head, (((0,), (0,)), ((), ())), preferred_element_type=jnp.float32
        )
        shifted = jnp.exp(scores - jnp.max(scores, axis=1, keepdims=True))
        weights = (shifted / jnp.sum(shifted, axis=1, keepdims=True)).astype(jnp.bfloat16)
        output = lax.dot_general(
            value_head, weights, (((1,), (1,)), ((), ())), preferred_element_type=jnp.float32
        ).astype(jnp.bfloat16)
        return (output, weights)

    attended, kept_weights = lax.map(attend, query_blocks)
    attended = attended.transpose(1, 0, 2).reshape(1, HEAD, total_queries)
    attn_band = from_heads(
        lax.all_to_all(attended, "sp", split_axis=2, concat_axis=0, tiled=True), pieces
    )
    mixed = lax.dot_general(
        attn_band, out_full, (((0,), (0,)), ((), ())), preferred_element_type=jnp.float32
    )
    x_one = (y_one.astype(jnp.float32) - mixed).astype(jnp.bfloat16)
    feature = ((y_one.astype(jnp.float32) + second_stream_state.astype(jnp.float32)) * 0.5).astype(
        jnp.bfloat16
    )
    upsampled = jnp.dot(feature, deconv_full, preferred_element_type=jnp.float32).astype(
        jnp.bfloat16
    )
    pixel_rows = 2 * rows_here
    pixel_cols = 2 * GRID_W
    pixels = (
        upsampled.reshape(rows_here, GRID_W, 2, 2, DEC)
        .transpose(0, 2, 1, 3, 4)
        .reshape(pixel_rows * pixel_cols, DEC)
    )
    lhat, linv = apply_layer_norm(jnp.dot(pixels, w_lateral, preferred_element_type=jnp.float32))
    activation = (lhat * lat_gain).astype(jnp.bfloat16).reshape(pixel_rows, pixel_cols, LAT)
    extended = padded_2(activation, (("sp", 0),), 1)
    padded = jnp.pad(extended, ((0, 0), (1, 1), (0, 0)))
    chat, cinv = apply_layer_norm(conv_valid(padded, w_conv))
    dconv = layer_norm_reverse(cot.astype(jnp.float32) * conv_gain, chat, cinv).astype(jnp.bfloat16)
    flipped = w_conv[::-1, ::-1].transpose(0, 1, 3, 2)
    spread_rows = conv_valid(jnp.pad(dconv, ((2, 2), (1, 1), (0, 0))), flipped)
    from_below = shifted_2(spread_rows[-1].astype(jnp.bfloat16), "sp", 1).astype(jnp.float32)
    from_above = shifted_2(spread_rows[0].astype(jnp.bfloat16), "sp", -1).astype(jnp.float32)
    dact = spread_rows[1:-1]
    dact = dact.at[0].add(from_below).at[-1].add(from_above)
    patches = jnp.stack(
        [
            padded[row_shift : row_shift + pixel_rows, col_shift : col_shift + pixel_cols].reshape(
                -1, LAT
            )
            for row_shift in range(3)
            for col_shift in range(3)
        ]
    )
    conv_product = jnp.einsum(
        "kpc,pd->ckd", patches, dconv.reshape(-1, LAT), preferred_element_type=jnp.float32
    )
    conv_part = (conv_product.reshape(4, 2, 4, LAT // devices, 9 * LAT) * grad_scale).astype(
        jnp.bfloat16
    )
    dlat = layer_norm_reverse(dact.reshape(-1, LAT) * lat_gain, lhat, linv).astype(jnp.bfloat16)
    lat_rows = DEC // devices
    lat_part = rounded_part(pixels, dlat).reshape(devices, lat_rows, LAT)
    lat_part = jnp.pad(lat_part, ((0, 0), (0, 16 - lat_rows), (0, 0))).reshape(4, 2, 4, 16, LAT)
    dpixels = lax.dot_general(
        dlat, w_lateral, (((1,), (1,)), ((), ())), preferred_element_type=jnp.float32
    ).astype(jnp.bfloat16)
    dup = (
        dpixels.reshape(rows_here, 2, GRID_W, 2, DEC)
        .transpose(0, 2, 1, 3, 4)
        .reshape(tokens_here, 4 * DEC)
    )
    spread_feature = jnp.pad(
        feature.reshape(tokens_here, devices, depth), ((0, 0), (0, 0), (0, ROWS_PAD - depth))
    ).reshape(tokens_here, devices * ROWS_PAD)
    dec_part = rounded_part(spread_feature, dup).reshape(4, 2, 4, ROWS_PAD, 4 * DEC)
    halfway_split = 0.5 * lax.dot_general(
        dup, deconv_full, (((1,), (1,)), ((), ())), preferred_element_type=jnp.float32
    )
    d_x1 = halfway_split.astype(jnp.bfloat16)
    dattn = lax.dot_general(
        out_full, d_x1, (((1,), (1,)), ((), ())), preferred_element_type=jnp.float32
    ).astype(jnp.bfloat16)
    spread_attn = jnp.pad(
        attn_band.reshape(devices, out_depth, tokens_here), ((0, 0), (0, 24 - out_depth), (0, 0))
    ).reshape(devices * 24, tokens_here)
    out_product = lax.dot_general(
        spread_attn, d_x1, (((1,), (0,)), ((), ())), preferred_element_type=jnp.float32
    )
    out_part = (out_product * grad_scale).astype(jnp.bfloat16).reshape(4, 2, 4, 24, -1)
    grad_head = lax.all_to_all(
        to_heads(dattn, pieces), "sp", split_axis=0, concat_axis=2, tiled=True
    )[0]
    grad_blocks = grad_head.reshape(HEAD, count_blocks, block).transpose(1, 0, 2)

    def backward_block(carry, operands):
        key_grad, value_grad = carry
        query_block, grad_block, weights = operands
        wide = weights.astype(jnp.float32)
        dprob = lax.dot_general(
            grad_block, value_head, (((0,), (0,)), ((), ())), preferred_element_type=jnp.float32
        )
        dscore = (wide * (dprob - jnp.sum(wide * dprob, axis=1, keepdims=True))).astype(
            jnp.bfloat16
        )
        query_grad = lax.dot_general(
            key_head, dscore, (((1,), (1,)), ((), ())), preferred_element_type=jnp.float32
        )
        query_grad = (query_grad * score_scale).astype(jnp.bfloat16)
        key_grad = key_grad + lax.dot_general(
            query_block, dscore, (((1,), (0,)), ((), ())), preferred_element_type=jnp.float32
        )
        value_grad = value_grad + lax.dot_general(
            grad_block, weights, (((1,), (0,)), ((), ())), preferred_element_type=jnp.float32
        )
        return ((key_grad, value_grad), query_grad)

    zero_grads = jnp.zeros(key_head.shape, jnp.float32)
    (key_grad, value_grad), query_grads = lax.scan(
        backward_block, (zero_grads, zero_grads), (query_blocks, grad_blocks, kept_weights)
    )
    query_grads = query_grads.transpose(1, 0, 2).reshape(1, HEAD, total_queries)
    dq_band = from_heads(
        lax.all_to_all(query_grads, "sp", split_axis=2, concat_axis=0, tiled=True), pieces
    )
    key_parts, value_parts = (
        lax.all_to_all(
            key_grad.astype(jnp.bfloat16), "sp", split_axis=1, concat_axis=0, tiled=True
        ).astype(key_grad.dtype),
        lax.all_to_all(
            value_grad.astype(jnp.bfloat16), "sp", split_axis=1, concat_axis=0, tiled=True
        ).astype(value_grad.dtype),
    )
    dk_band = (
        key_parts.reshape(HEADS, pieces, HEAD, tokens_here)
        .sum(axis=1)
        .reshape(inner, tokens_here)
        .astype(jnp.bfloat16)
    )
    dv_band = (
        value_parts.reshape(HEADS, pieces, HEAD, tokens_here)
        .sum(axis=1)
        .reshape(inner, tokens_here)
        .astype(jnp.bfloat16)
    )
    dqkv = jnp.concatenate([dq_band, dk_band, dv_band], axis=0)
    normalized_gradient = lax.dot_general(
        pad_heads(dqkv), qkv_full, (((0,), (1,)), ((), ())), preferred_element_type=jnp.float32
    )
    second_input_gradient = (
        halfway_split
        + layer_norm_reverse(
            normalized_gradient * layer_norm_gain, standardized_input, inverse_deviation
        )
    ).astype(jnp.bfloat16)
    half = 2 * DEC
    dec_low, out_rows, dec_high, conv_rows, lat_sums = scatter_sums(
        [dec_part, out_part, conv_part, lat_part],
        [
            (0, 0, half, True),
            (1, 0, out_part.shape[4], False),
            (0, half, half, True),
            (2, 0, 9 * LAT, False),
            (3, 0, LAT, False),
        ],
    )
    g_deconv = jnp.concatenate([dec_low[:depth], dec_high[:depth]], axis=1)
    g_out = out_rows[:out_depth]
    g_lateral = lat_sums[:lat_rows]
    g_conv = conv_rows.reshape(conv_rows.shape[0], 3, 3, LAT).transpose(1, 2, 0, 3)
    return (x_one, d_x1, second_input_gradient, g_out, g_deconv, g_lateral, g_conv)


def solution(mesh):
    return jax.shard_map(
        per_device,
        mesh=mesh,
        in_specs=(
            P(("img", "sp"), None),
            P(("img", "sp"), None),
            P(("img", "sp"), None, None),
            P(),
            P("sp", None),
            P("sp", None),
            P("sp", None),
            P(),
            P(),
            P(),
            P(),
        ),
        out_specs=(
            P(("img", "sp"), None),
            P(("img", "sp"), None),
            P(("img", "sp"), None),
            P(("img", "sp"), None),
            P(("img", "sp"), None),
            P(("img", "sp"), None),
            P("img", None, "sp", None),
        ),
        check_vma=False,
    )
```

```python
import functools

import jax
import jax.numpy as jnp
from jax import lax
from jax.experimental import pallas as pl
from jax.experimental.pallas import tpu as pltpu
from jax.sharding import PartitionSpec as P

HEADS = 8
HEAD = 88
DEC = 384
LAT = 256
GRID_W = 64


epsilon = 1e-06
grad_scale = 0.015625


def padded_2(block, sides, width):
    for axis, dim in sides:
        count = lax.axis_size(axis)
        forward = [(i, i + 1) for i in range(count - 1)]
        backward = [(target, source) for source, target in forward]
        low = lax.ppermute(
            lax.slice_in_dim(block, block.shape[dim] - width, None, axis=dim), axis, forward
        )
        high = lax.ppermute(lax.slice_in_dim(block, 0, width, axis=dim), axis, backward)
        block = jnp.concatenate([low, block, high], axis=dim)
    return block


def shifted_2(array, axis, by):
    count = lax.axis_size(axis)
    pairs = [(i, i + by) for i in range(count) if 0 <= i + by < count]
    return lax.ppermute(array, axis, pairs)


def apply_layer_norm(values):
    centered = values - jnp.mean(values, axis=-1, keepdims=True)
    inverse = lax.rsqrt(jnp.mean(centered * centered, axis=-1, keepdims=True) + epsilon)
    return (centered * inverse, inverse)


def layer_norm_reverse(upstream, normalized_rows, inverse):
    first = jnp.mean(upstream, axis=-1, keepdims=True)
    second = jnp.mean(upstream * normalized_rows, axis=-1, keepdims=True)
    return inverse * (upstream - first - normalized_rows * second)


def conv_valid(padded, kernel):
    result = lax.conv_general_dilated(
        padded[None],
        kernel,
        (1, 1),
        "VALID",
        dimension_numbers=("NHWC", "HWIO", "NHWC"),
        preferred_element_type=jnp.float32,
    )
    return result[0]


def rounded_part(left, right):
    product = lax.dot_general(
        left, right, (((0,), (0,)), ((), ())), preferred_element_type=jnp.float32
    )
    return (product * grad_scale).astype(jnp.bfloat16)


MESH = pl.DeviceIdType.MESH
ROWS_PAD = 48
HEAD_PAD = 96
OUT_ROWS_PAD = 32
OUT_COLS_PAD = 1536


def place():
    s, i = lax.axis_index("sp"), lax.axis_index("img")
    return s // 8, (s // 4) % 2, s % 4, i // 2, i % 2


def at_sp(x, zl, y):
    return {"sp": (x * 2 + zl) * 4 + y}


def greet(targets):
    barrier = pltpu.get_barrier_semaphore()
    for target in targets:
        pl.semaphore_signal(barrier, inc=1, device_id=target, device_id_type=MESH)
    pl.semaphore_wait(barrier, len(targets))


def gather_kernel(shapes, *refs):
    count = len(shapes)
    ins, outs, shards, packs = (refs[k * count : (k + 1) * count] for k in range(4))
    send, recv, local = refs[4 * count :]
    x, zl, y, zh, core = place()
    xm, xp, xo = (x + 3) % 4, (x + 1) % 4, (x + 2) % 4
    left, right = at_sp(xm, zl, y), at_sp(xp, zl, y)
    across = (x * 2 + 1 - zl) * 4 + y
    up = {"img": ((zh + zl) % 4) * 2 + core, "sp": across}
    down = {"img": ((zh + zl + 3) % 4) * 2 + core, "sp": across}
    twin = {"img": zh * 2 + 1 - core}
    column = [at_sp(x, zl, (y + k) % 4) for k in (1, 2, 3)]
    greet(column + [left, right, up, down, twin])
    copies = {}

    def push(a, slot, src, dst, target):
        copy = pltpu.make_async_remote_copy(
            src_ref=src,
            dst_ref=dst,
            send_sem=send.at[a, slot],
            recv_sem=recv.at[a, slot],
            device_id=target,
            device_id_type=MESH,
        )
        copy.start()
        copies[a, slot] = copy

    def part(a):
        half = shapes[a][3] // 2
        return half, pl.multiple_of(core * half, 128)

    def region(a, bx, bz, lo, size):
        half, first = part(a)
        return outs[a].at[bx * 2 + bz, pl.ds(lo, size), pl.ds(first, half)]

    def forward(a, slot, bx, bz, lo, size, target):
        piece = region(a, bx, bz, lo, size)
        push(a, slot, piece, piece, target)

    for a in range(count):
        half, first = part(a)
        mine = ins[a].at[:, pl.ds(first, half)]
        for k in range(3):
            push(a, k, mine, shards[a].at[y], column[k])
        shards[a][y] = ins[a][:, pl.ds(first, half)]
    keeps = []
    for a in range(count):
        rows, per, block, _ = shapes[a]
        half, first = part(a)
        low = (block // 32) * 16
        high = block - low
        for k in range(3):
            copies[a, k].wait_recv()
        r = lax.broadcasted_iota(jnp.int32, (block, 4 * rows), 0)
        c = lax.broadcasted_iota(jnp.int32, (block, 4 * rows), 1)
        skipped = jnp.zeros_like(r)
        for k in (1, 2, 3):
            skipped += jnp.where(r >= k * per, rows - per, 0)
        pick = jnp.where(c == r + skipped, 1.0, 0.0).astype(jnp.bfloat16)
        packs[a][...] = jnp.dot(
            pick, shards[a][...].reshape(4 * rows, half), preferred_element_type=jnp.float32
        ).astype(jnp.bfloat16)
        own, whole = packs[a], region(a, x, zl, 0, block)
        keep = pltpu.make_async_copy(own, whole, local.at[a])
        keep.start()
        keeps.append(keep)
        push(a, 3, own, whole, right)
        push(a, 4, own, whole, left)
        push(a, 7, own.at[pl.ds(0, low)], region(a, x, zl, 0, low), up)
        push(a, 8, own.at[pl.ds(low, high)], region(a, x, zl, low, high), down)
        push(a, 15, own, whole, twin)

    def near(a):
        block = shapes[a][2]
        low = (block // 32) * 16
        high = block - low
        copies[a, 3].wait_recv()
        forward(a, 5, xm, zl, 0, low, right)
        forward(a, 9, xm, zl, 0, low, up)
        forward(a, 10, xm, zl, low, high, down)
        forward(a, 16, xm, zl, 0, block, twin)
        copies[a, 4].wait_recv()
        forward(a, 6, xp, zl, low, high, left)
        forward(a, 11, xp, zl, 0, low, up)
        forward(a, 12, xp, zl, low, high, down)
        forward(a, 17, xp, zl, 0, block, twin)

    def far(a):
        block = shapes[a][2]
        low = (block // 32) * 16
        high = block - low
        copies[a, 5].wait_recv()
        forward(a, 13, xo, zl, 0, low, up)
        forward(a, 18, xo, zl, 0, low, twin)
        copies[a, 6].wait_recv()
        forward(a, 14, xo, zl, low, high, down)
        forward(a, 19, xo, zl, low, high, twin)

    def deep(a):
        block = shapes[a][2]
        low = (block // 32) * 16
        high = block - low
        for n, bx in enumerate((x, xm, xp, xo)):
            copies[a, 7 + 2 * n].wait_recv()
            forward(a, 20 + 2 * n, bx, 1 - zl, 0, low, twin)
            copies[a, 8 + 2 * n].wait_recv()
            forward(a, 21 + 2 * n, bx, 1 - zl, low, high, twin)

    for step in range(count + 2):
        if step < count:
            near(step)
        if 0 <= step - 1 < count:
            far(step - 1)
        if 0 <= step - 2 < count:
            deep(step - 2)
    for a in range(count):
        for slot in range(15, 28):
            copies[a, slot].wait_recv()
    for keep in keeps:
        keep.wait()
    for copy in copies.values():
        copy.wait_send()


def gather_weights(shards, pers):
    count = len(shards)
    shapes = []
    for shard, per in zip(shards, pers):
        block = -(-4 * per // 16) * 16
        shapes.append((shard.shape[0], per, block, shard.shape[1]))
    halves = [(rows, block, width // 2) for rows, _, block, width in shapes]
    return pl.pallas_call(
        functools.partial(gather_kernel, shapes),
        out_shape=[
            jax.ShapeDtypeStruct((8, block, width), jnp.bfloat16) for _, _, block, width in shapes
        ],
        in_specs=[pl.BlockSpec(memory_space=pltpu.VMEM)] * count,
        out_specs=[pl.BlockSpec(memory_space=pl.ANY)] * count,
        scratch_shapes=[pltpu.VMEM((4, rows, half), jnp.bfloat16) for rows, _, half in halves]
        + [pltpu.VMEM((block, half), jnp.bfloat16) for _, block, half in halves]
        + [
            pltpu.SemaphoreType.DMA((count, 28)),
            pltpu.SemaphoreType.DMA((count, 28)),
            pltpu.SemaphoreType.DMA((count,)),
        ],
        compiler_params=pltpu.CompilerParams(
            collective_id=0, has_side_effects=True, vmem_limit_bytes=32 * 2**20
        ),
    )(*shards)


def scatter_kernel(plan, *refs):
    count = len(plan)
    arrays = 1 + max(source for source, _, _, _ in plan)
    ins, outs = refs[:arrays], refs[arrays : arrays + count]
    rest = refs[arrays + count :]
    land1, sum1, land2, sum2, land3 = (rest[k * count : (k + 1) * count] for k in range(5))
    send, recv = rest[5 * count :]
    x, zl, y, zh, core = place()
    across = at_sp(x, 1 - zl, y)
    row = [(x + k) % 4 for k in (1, 2, 3)]
    column = [(y + k) % 4 for k in (1, 2, 3)]
    greet([at_sp(k, zl, y) for k in row] + [at_sp(x, zl, k) for k in column] + [across])
    copies = {}

    def push(n, slot, src, dst, target):
        copy = pltpu.make_async_remote_copy(
            src_ref=src,
            dst_ref=dst,
            send_sem=send.at[n, slot],
            recv_sem=recv.at[n, slot],
            device_id=target,
            device_id_type=MESH,
        )
        copy.start()
        copies[n, slot] = copy

    def to_row(k):
        return at_sp(row[k], zl, y)

    def to_column(k):
        return at_sp(x, zl, column[k])

    for n, (source, first, width, x_first) in enumerate(plan):
        view = ins[source].at[:, :, :, :, pl.ds(first, width)]
        for k in range(3):
            if x_first:
                push(n, k, view.at[row[k]], land1[n].at[k], to_row(k))
            else:
                push(n, k, view.at[:, :, column[k]], land1[n].at[k], to_column(k))
    for n, (source, first, width, x_first) in enumerate(plan):
        for k in range(3):
            copies[n, k].wait_recv()
        outer, inner = sum1[n].shape[0], sum1[n].shape[1]

        def add(t, carry):
            p, q = t // inner, t % inner
            if x_first:
                own = ins[source][x, p, q, :, pl.ds(first, width)]
            else:
                own = ins[source][p, q, y, :, pl.ds(first, width)]
            total = own.astype(jnp.float32)
            for k in range(3):
                total += land1[n][k, p, q].astype(jnp.float32)
            sum1[n][p, q] = total.astype(jnp.bfloat16)
            return carry

        lax.fori_loop(0, outer * inner, add, 0)
        for k in range(3):
            if x_first:
                push(n, 3 + k, sum1[n].at[:, column[k]], land2[n].at[k], to_column(k))
            else:
                push(n, 3 + k, sum1[n].at[row[k]], land2[n].at[k], to_row(k))
    for n, (source, first, width, x_first) in enumerate(plan):
        for k in range(3):
            copies[n, 3 + k].wait_recv()
        for p in range(2):
            own = sum1[n][p, y] if x_first else sum1[n][x, p]
            total = own.astype(jnp.float32)
            for k in range(3):
                total += land2[n][k, p].astype(jnp.float32)
            sum2[n][p] = total.astype(jnp.bfloat16)
        push(n, 6, sum2[n].at[1 - zl], land3[n], across)
    for n in range(count):
        copies[n, 6].wait_recv()
        outs[n][...] = sum2[n][zl].astype(jnp.float32) + land3[n][...].astype(jnp.float32)
    for copy in copies.values():
        copy.wait_send()


def scatter_sums(parts, plan):
    count = len(plan)
    rows = [parts[source].shape[3] for source, _, _, _ in plan]
    widths = [width for _, _, width, _ in plan]

    def buffers(*lead):
        return [pltpu.VMEM((*lead, r, w), jnp.bfloat16) for r, w in zip(rows, widths)]

    def by_order(first, second, lead=()):
        return [
            pltpu.VMEM((*lead, *(first if order else second), r, w), jnp.bfloat16)
            for r, w, (_, _, _, order) in zip(rows, widths, plan)
        ]

    return pl.pallas_call(
        functools.partial(scatter_kernel, plan),
        out_shape=[jax.ShapeDtypeStruct((r, w), jnp.float32) for r, w in zip(rows, widths)],
        in_specs=[pl.BlockSpec(memory_space=pltpu.VMEM)] * len(parts),
        out_specs=[pl.BlockSpec(memory_space=pltpu.VMEM)] * count,
        scratch_shapes=by_order((2, 4), (4, 2), (3,))
        + by_order((2, 4), (4, 2))
        + buffers(3, 2)
        + buffers(2)
        + buffers()
        + [pltpu.SemaphoreType.DMA((count, 7)), pltpu.SemaphoreType.DMA((count, 7))],
        compiler_params=pltpu.CompilerParams(
            collective_id=1, has_side_effects=True, vmem_limit_bytes=48 * 2**20
        ),
    )(*parts)


TILE = 128
QUERY_BLOCK = 512
KEY_BLOCK = 1024


def turned(block):
    wide = block.astype(jnp.float32)
    zeros = jnp.zeros((TILE - HEAD_PAD, TILE), jnp.float32)
    return jnp.concatenate([wide, zeros], axis=0).T


def head_rows(block):
    return block.T[:HEAD_PAD].astype(jnp.bfloat16)


def attention_kernel(
    proj,
    grad,
    attn_out,
    dqkv_out,
    q_in,
    g_in,
    kv_in,
    key_t,
    value_t,
    key,
    value,
    query,
    cot,
    query_t,
    cot_t,
    score,
    weight,
    inverse,
    offset,
    attended,
    o_send,
    dq_send,
    d_send,
    d_land,
    d_sum,
    o_land,
    d_res,
    send,
    recv,
):
    x, zl, y, zh, core = place()
    m = x * 2 + zl
    plane = [(m + k) % 8 for k in range(8)]
    source = [(m + 8 - k) % 8 for k in range(8)]
    column = [(y + k) % 4 for k in range(4)]

    def at_plane(k):
        return {"sp": plane[k] * 4 + y}

    def at_column(k):
        return {"sp": m * 4 + column[k]}

    greet([at_plane(k) for k in range(1, 8)] + [at_column(k) for k in range(1, 4)])
    copies = {}

    def push(slot, src, dst, target):
        copy = pltpu.make_async_remote_copy(
            src_ref=src,
            dst_ref=dst,
            send_sem=send.at[slot],
            recv_sem=recv.at[slot],
            device_id=target,
            device_id_type=MESH,
        )
        copy.start()
        copies[slot] = copy

    kv_at, q_at, g_at, ring_at, o_at, dq_at, back_at, home_at = 0, 8, 16, 24, 48, 56, 64, 72
    for k in range(1, 8):
        push(kv_at + k, proj.at[pl.ds(1, 2), plane[k]], kv_in.at[y, m], at_plane(k))
    kv_in[y, m, 0] = proj[1, m]
    kv_in[y, m, 1] = proj[2, m]
    q_in[m] = proj[0, m]
    g_in[m] = grad[m]

    def pass_on(k):
        piece = kv_in.at[y, source[k]]
        for j in range(1, 4):
            push(ring_at + 3 * k + j - 1, piece, piece, at_column(j))

    pass_on(0)
    for k in range(1, 8):
        push(q_at + k, proj.at[0, plane[k]], q_in.at[m], at_plane(k))
    for k in range(1, 8):
        copies[kv_at + k].wait_recv()
        pass_on(k)
    for k in range(1, 8):
        push(g_at + k, grad.at[plane[k]], g_in.at[m], at_plane(k))
    zero_rows = jnp.zeros((TILE - HEAD_PAD, key_t.shape[1]), jnp.bfloat16)
    key_t[HEAD_PAD:] = zero_rows
    value_t[HEAD_PAD:] = zero_rows

    def prepare(t, carry):
        at = pl.ds(pl.multiple_of(t * TILE, TILE), TILE)
        block = kv_in[t // 8, t % 8, 0]
        key_t[:HEAD_PAD, at] = block
        key[at, :] = turned(block).astype(jnp.bfloat16)
        block = kv_in[t // 8, t % 8, 1]
        value_t[:HEAD_PAD, at] = block
        value[at, :] = turned(block).astype(jnp.bfloat16)
        return carry

    def prepare_queries(t, carry):
        query[pl.ds(pl.multiple_of(t * TILE, TILE), TILE), :] = turned(q_in[t]).astype(jnp.bfloat16)
        return carry

    def prepare_cots(t, carry):
        cot[pl.ds(pl.multiple_of(t * TILE, TILE), TILE), :] = turned(g_in[t]).astype(jnp.bfloat16)
        return carry

    lax.fori_loop(y * 8, y * 8 + 8, prepare, 0)
    for k in range(1, 8):
        copies[q_at + k].wait_recv()
    lax.fori_loop(0, 8, prepare_queries, 0)
    for j in range(1, 4):
        for k in range(8):
            copies[ring_at + 3 * k + j - 1].wait_recv()
        first = ((y + 4 - j) % 4) * 8
        lax.fori_loop(first, first + 8, prepare, 0)
    for k in range(1, 8):
        copies[g_at + k].wait_recv()
    lax.fori_loop(0, 8, prepare_cots, 0)

    tokens = key.shape[0]
    queries = query.shape[0]
    blocks = [pl.ds(c * KEY_BLOCK, KEY_BLOCK) for c in range(tokens // KEY_BLOCK)]

    def forward(i, carry):
        at = pl.ds(pl.multiple_of(i * QUERY_BLOCK, QUERY_BLOCK), QUERY_BLOCK)
        top = jnp.full((QUERY_BLOCK, 1), -jnp.inf, jnp.float32)
        for block in blocks:
            part = jnp.dot(query[at, :], key_t[:, block], preferred_element_type=jnp.float32)
            score[:, block] = part
            top = jnp.maximum(top, jnp.max(part, axis=1, keepdims=True))
        total = jnp.zeros((QUERY_BLOCK, 1), jnp.float32)
        mixed = jnp.zeros((QUERY_BLOCK, TILE), jnp.float32)
        for block in blocks:
            part = jnp.exp(score[:, block] - top)
            total += jnp.sum(part, axis=1, keepdims=True)
            rounded = part.astype(jnp.bfloat16)
            weight[at, block] = rounded
            mixed += jnp.dot(rounded, value[block, :], preferred_element_type=jnp.float32)
        inv = 1.0 / total
        mixed = mixed * inv
        attended[at, :] = mixed
        inverse[at, :] = inv
        offset[at, :] = jnp.sum(mixed * cot[at, :].astype(jnp.float32), axis=1, keepdims=True)
        return carry

    lax.fori_loop(0, queries // QUERY_BLOCK, forward, 0)
    for t in range(8):
        at = pl.ds(t * TILE, TILE)
        o_send[t] = head_rows(attended[at, :])
    for k in range(1, 8):
        push(o_at + k, o_send.at[plane[k]], o_land.at[m], at_plane(k))
    o_land[m] = o_send[m]
    for t in range(8):
        at = pl.ds(t * TILE, TILE)
        inv = inverse[at, :]
        query_t[:, at] = (query[at, :].astype(jnp.float32) * inv).T.astype(jnp.bfloat16)
        cot_t[:, at] = (cot[at, :].astype(jnp.float32) * inv).T.astype(jnp.bfloat16)

    def key_side(left, kind):
        for j in (1, 2, 3, 0):
            yy = column[j]
            at = pl.ds(pl.multiple_of(yy * 8 * TILE, 8 * TILE), 8 * TILE)
            result = jnp.dot(left[...], weight[:, at], preferred_element_type=jnp.float32)
            for t in range(8):
                d_send[kind, j, t] = result[:HEAD_PAD, t * TILE : (t + 1) * TILE].astype(
                    jnp.bfloat16
                )
            if j:
                push(back_at + 4 * kind + j, d_send.at[kind, j], d_land.at[kind, j - 1], at_column(j))

    def key_home(kind):
        for j in range(1, 4):
            copies[back_at + 4 * kind + j].wait_recv()
        for t in range(8):
            total = d_send[kind, 0, t].astype(jnp.float32)
            for j in range(3):
                total += d_land[kind, j, t].astype(jnp.float32)
            d_sum[kind, t] = total.astype(jnp.bfloat16)
        for k in range(1, 8):
            push(
                home_at + 8 * kind + k,
                d_sum.at[kind, plane[k]],
                d_res.at[kind + 1, m],
                at_plane(k),
            )
        d_res[kind + 1, m] = d_sum[kind, m]

    key_side(cot_t, 1)

    def backward(i, carry):
        at = pl.ds(pl.multiple_of(i * QUERY_BLOCK, QUERY_BLOCK), QUERY_BLOCK)
        query_grad = jnp.zeros((QUERY_BLOCK, TILE), jnp.float32)
        shift = offset[at, :]
        for block in blocks:
            dprob = jnp.dot(cot[at, :], value_t[:, block], preferred_element_type=jnp.float32)
            dscore = (weight[at, block].astype(jnp.float32) * (dprob - shift)).astype(jnp.bfloat16)
            weight[at, block] = dscore
            query_grad += jnp.dot(dscore, key[block, :], preferred_element_type=jnp.float32)
        attended[at, :] = query_grad * (inverse[at, :] * HEAD ** (-0.5))
        return carry

    lax.fori_loop(0, queries // QUERY_BLOCK, backward, 0)
    key_side(query_t, 0)
    for t in range(8):
        dq_send[t] = head_rows(attended[pl.ds(t * TILE, TILE), :])
    for k in range(1, 8):
        push(dq_at + k, dq_send.at[plane[k]], d_res.at[0, m], at_plane(k))
    d_res[0, m] = dq_send[m]
    key_home(1)
    key_home(0)
    for k in range(1, 8):
        copies[o_at + k].wait_recv()
    attn_out[...] = o_land[...]
    for first in (dq_at, home_at, home_at + 8):
        for k in range(1, 8):
            copies[first + k].wait_recv()
    dqkv_out[...] = d_res[...]
    for copy in copies.values():
        copy.wait_send()


def attend_both_ways(proj, grad):
    heads = grad.shape[0]
    tokens, queries = 32 * TILE, 8 * TILE
    bf16, f32 = jnp.bfloat16, jnp.float32
    block = (HEAD_PAD, TILE)
    shapes = [
        ((8, *block), bf16),
        ((8, *block), bf16),
        ((4, 8, 2, *block), bf16),
        ((TILE, tokens), bf16),
        ((TILE, tokens), bf16),
        ((tokens, TILE), bf16),
        ((tokens, TILE), bf16),
        ((queries, TILE), bf16),
        ((queries, TILE), bf16),
        ((TILE, queries), bf16),
        ((TILE, queries), bf16),
        ((QUERY_BLOCK, tokens), f32),
        ((queries, tokens), bf16),
        ((queries, 1), f32),
        ((queries, 1), f32),
        ((queries, TILE), f32),
        ((8, *block), bf16),
        ((8, *block), bf16),
        ((2, 4, 8, *block), bf16),
        ((2, 3, 8, *block), bf16),
        ((2, 8, *block), bf16),
        ((8, *block), bf16),
        ((3, 8, *block), bf16),
    ]
    return pl.pallas_call(
        attention_kernel,
        out_shape=[
            jax.ShapeDtypeStruct((heads, *block), bf16),
            jax.ShapeDtypeStruct((3, heads, *block), bf16),
        ],
        in_specs=[pl.BlockSpec(memory_space=pltpu.VMEM)] * 2,
        out_specs=[pl.BlockSpec(memory_space=pltpu.VMEM)] * 2,
        scratch_shapes=[pltpu.VMEM(shape, kind) for shape, kind in shapes]
        + [pltpu.SemaphoreType.DMA((88,)), pltpu.SemaphoreType.DMA((88,))],
        compiler_params=pltpu.CompilerParams(
            collective_id=2, has_side_effects=True, vmem_limit_bytes=56 * 2**20
        ),
    )(proj, grad)


def per_device(
    y_one,
    second_stream_state,
    cot,
    layer_norm_gain,
    w_qkv,
    w_out,
    w_deconv,
    w_lateral,
    lat_gain,
    w_conv,
    conv_gain,
):
    devices = lax.axis_size("sp")
    tokens_here = y_one.shape[0]
    rows_here = tokens_here // GRID_W
    score_scale = HEAD ** (-0.5)
    standardized_input, inverse_deviation = apply_layer_norm(
        second_stream_state.astype(jnp.float32)
    )
    normalized_rows = (standardized_input * layer_norm_gain).astype(jnp.bfloat16)
    depth, out_depth = w_qkv.shape[0], w_out.shape[0]
    qkv_shard = jnp.pad(
        w_qkv.reshape(depth, 3 * HEADS, HEAD),
        ((0, ROWS_PAD - depth), (0, 0), (0, HEAD_PAD - HEAD)),
    ).reshape(ROWS_PAD, 3 * HEADS * HEAD_PAD)
    out_shard = jnp.pad(
        w_out, ((0, OUT_ROWS_PAD - out_depth), (0, OUT_COLS_PAD - w_out.shape[1]))
    )
    deconv_shard = jnp.pad(w_deconv, ((0, ROWS_PAD - depth), (0, 0)))
    deconv_full, qkv_full, out_full = gather_weights(
        [deconv_shard, qkv_shard, out_shard], [depth, depth, out_depth]
    )
    deconv_full = deconv_full.reshape(devices * depth, -1)
    qkv_full = qkv_full.reshape(devices * depth, -1)
    out_full = out_full.reshape(HEADS * HEAD_PAD, -1)[:, : w_out.shape[1]]
    feature = ((y_one.astype(jnp.float32) + second_stream_state.astype(jnp.float32)) * 0.5).astype(
        jnp.bfloat16
    )
    upsampled = jnp.dot(feature, deconv_full, preferred_element_type=jnp.float32).astype(
        jnp.bfloat16
    )
    pixel_rows = 2 * rows_here
    pixel_cols = 2 * GRID_W
    pixels = (
        upsampled.reshape(rows_here, GRID_W, 2, 2, DEC)
        .transpose(0, 2, 1, 3, 4)
        .reshape(pixel_rows * pixel_cols, DEC)
    )
    lhat, linv = apply_layer_norm(jnp.dot(pixels, w_lateral, preferred_element_type=jnp.float32))
    activation = (lhat * lat_gain).astype(jnp.bfloat16).reshape(pixel_rows, pixel_cols, LAT)
    extended = padded_2(activation, (("sp", 0),), 1)
    padded = jnp.pad(extended, ((0, 0), (1, 1), (0, 0)))
    chat, cinv = apply_layer_norm(conv_valid(padded, w_conv))
    dconv = layer_norm_reverse(cot.astype(jnp.float32) * conv_gain, chat, cinv).astype(jnp.bfloat16)
    flipped = w_conv[::-1, ::-1].transpose(0, 1, 3, 2)
    spread_rows = conv_valid(jnp.pad(dconv, ((2, 2), (1, 1), (0, 0))), flipped)
    from_below = shifted_2(spread_rows[-1].astype(jnp.bfloat16), "sp", 1).astype(jnp.float32)
    from_above = shifted_2(spread_rows[0].astype(jnp.bfloat16), "sp", -1).astype(jnp.float32)
    dact = spread_rows[1:-1]
    dact = dact.at[0].add(from_below).at[-1].add(from_above)
    patches = jnp.stack(
        [
            padded[row_shift : row_shift + pixel_rows, col_shift : col_shift + pixel_cols].reshape(
                -1, LAT
            )
            for row_shift in range(3)
            for col_shift in range(3)
        ]
    )
    conv_product = jnp.einsum(
        "kpc,pd->ckd", patches, dconv.reshape(-1, LAT), preferred_element_type=jnp.float32
    )
    conv_part = (conv_product.reshape(4, 2, 4, LAT // devices, 9 * LAT) * grad_scale).astype(
        jnp.bfloat16
    )
    dlat = layer_norm_reverse(dact.reshape(-1, LAT) * lat_gain, lhat, linv).astype(jnp.bfloat16)
    lat_rows = DEC // devices
    lat_part = rounded_part(pixels, dlat).reshape(devices, lat_rows, LAT)
    lat_part = jnp.pad(lat_part, ((0, 0), (0, 16 - lat_rows), (0, 0))).reshape(4, 2, 4, 16, LAT)
    dpixels = lax.dot_general(
        dlat, w_lateral, (((1,), (1,)), ((), ())), preferred_element_type=jnp.float32
    ).astype(jnp.bfloat16)
    dup = (
        dpixels.reshape(rows_here, 2, GRID_W, 2, DEC)
        .transpose(0, 2, 1, 3, 4)
        .reshape(tokens_here, 4 * DEC)
    )
    spread_feature = jnp.pad(
        feature.reshape(tokens_here, devices, depth), ((0, 0), (0, 0), (0, ROWS_PAD - depth))
    ).reshape(tokens_here, devices * ROWS_PAD)
    dec_part = rounded_part(spread_feature, dup).reshape(4, 2, 4, ROWS_PAD, 4 * DEC)
    halfway_split = 0.5 * lax.dot_general(
        dup, deconv_full, (((1,), (1,)), ((), ())), preferred_element_type=jnp.float32
    )
    d_x1 = halfway_split.astype(jnp.bfloat16)
    dattn = lax.dot_general(
        out_full, d_x1, (((1,), (1,)), ((), ())), preferred_element_type=jnp.float32
    ).astype(jnp.bfloat16)
    projected = lax.dot_general(
        qkv_full, normalized_rows, (((0,), (1,)), ((), ())), preferred_element_type=jnp.float32
    ).reshape(3, HEADS, HEAD_PAD, tokens_here)
    scales = jnp.array([score_scale, 1.0, 1.0], jnp.float32).reshape(3, 1, 1, 1)
    projected = (projected * scales).astype(jnp.bfloat16)
    attn_heads, dqkv = attend_both_ways(
        projected, dattn.reshape(HEADS, HEAD_PAD, tokens_here)
    )
    mixed = lax.dot_general(
        attn_heads.reshape(HEADS * HEAD_PAD, tokens_here),
        out_full,
        (((0,), (0,)), ((), ())),
        preferred_element_type=jnp.float32,
    )
    x_one = (y_one.astype(jnp.float32) - mixed).astype(jnp.bfloat16)
    attn_band = attn_heads[:, :HEAD]
    spread_attn = jnp.pad(
        attn_band.reshape(devices, out_depth, tokens_here), ((0, 0), (0, 24 - out_depth), (0, 0))
    ).reshape(devices * 24, tokens_here)
    out_product = lax.dot_general(
        spread_attn, d_x1, (((1,), (0,)), ((), ())), preferred_element_type=jnp.float32
    )
    out_part = (out_product * grad_scale).astype(jnp.bfloat16).reshape(4, 2, 4, 24, -1)
    normalized_gradient = lax.dot_general(
        dqkv.reshape(3 * HEADS * HEAD_PAD, tokens_here),
        qkv_full, (((0,), (1,)), ((), ())), preferred_element_type=jnp.float32
    )
    second_input_gradient = (
        halfway_split
        + layer_norm_reverse(
            normalized_gradient * layer_norm_gain, standardized_input, inverse_deviation
        )
    ).astype(jnp.bfloat16)
    half = 2 * DEC
    dec_low, out_rows, dec_high, conv_rows, lat_sums = scatter_sums(
        [dec_part, out_part, conv_part, lat_part],
        [
            (0, 0, half, True),
            (1, 0, out_part.shape[4], False),
            (0, half, half, True),
            (2, 0, 9 * LAT, False),
            (3, 0, LAT, False),
        ],
    )
    g_deconv = jnp.concatenate([dec_low[:depth], dec_high[:depth]], axis=1)
    g_out = out_rows[:out_depth]
    g_lateral = lat_sums[:lat_rows]
    g_conv = conv_rows.reshape(conv_rows.shape[0], 3, 3, LAT).transpose(1, 2, 0, 3)
    return (x_one, d_x1, second_input_gradient, g_out, g_deconv, g_lateral, g_conv)


def solution(mesh):
    return jax.shard_map(
        per_device,
        mesh=mesh,
        in_specs=(
            P(("img", "sp"), None),
            P(("img", "sp"), None),
            P(("img", "sp"), None, None),
            P(),
            P("sp", None),
            P("sp", None),
            P("sp", None),
            P(),
            P(),
            P(),
            P(),
        ),
        out_specs=(
            P(("img", "sp"), None),
            P(("img", "sp"), None),
            P(("img", "sp"), None),
            P(("img", "sp"), None),
            P(("img", "sp"), None),
            P(("img", "sp"), None),
            P("img", None, "sp", None),
        ),
        check_vma=False,
    )
```

```python
import functools

import jax
import jax.numpy as jnp
from jax import lax
from jax.experimental import pallas as pl
from jax.experimental.pallas import tpu as pltpu
from jax.sharding import PartitionSpec as P

HEADS = 8
HEAD = 88
DEC = 384
LAT = 256
GRID_W = 64


epsilon = 1e-06
grad_scale = 0.015625


def padded_2(block, sides, width):
    for axis, dim in sides:
        count = lax.axis_size(axis)
        forward = [(i, i + 1) for i in range(count - 1)]
        backward = [(target, source) for source, target in forward]
        low = lax.ppermute(
            lax.slice_in_dim(block, block.shape[dim] - width, None, axis=dim), axis, forward
        )
        high = lax.ppermute(lax.slice_in_dim(block, 0, width, axis=dim), axis, backward)
        block = jnp.concatenate([low, block, high], axis=dim)
    return block


def shifted_2(array, axis, by):
    count = lax.axis_size(axis)
    pairs = [(i, i + by) for i in range(count) if 0 <= i + by < count]
    return lax.ppermute(array, axis, pairs)


def apply_layer_norm(values):
    centered = values - jnp.mean(values, axis=-1, keepdims=True)
    inverse = lax.rsqrt(jnp.mean(centered * centered, axis=-1, keepdims=True) + epsilon)
    return (centered * inverse, inverse)


def layer_norm_reverse(upstream, normalized_rows, inverse):
    first = jnp.mean(upstream, axis=-1, keepdims=True)
    second = jnp.mean(upstream * normalized_rows, axis=-1, keepdims=True)
    return inverse * (upstream - first - normalized_rows * second)


def conv_valid(padded, kernel):
    result = lax.conv_general_dilated(
        padded[None],
        kernel,
        (1, 1),
        "VALID",
        dimension_numbers=("NHWC", "HWIO", "NHWC"),
        preferred_element_type=jnp.float32,
    )
    return result[0]


def rounded_part(left, right):
    product = lax.dot_general(
        left, right, (((0,), (0,)), ((), ())), preferred_element_type=jnp.float32
    )
    return (product * grad_scale).astype(jnp.bfloat16)


MESH = pl.DeviceIdType.MESH
ROWS_PAD = 48
HEAD_PAD = 96
OUT_ROWS_PAD = 32
OUT_COLS_PAD = 1536


def place():
    s, i = lax.axis_index("sp"), lax.axis_index("img")
    return s // 8, (s // 4) % 2, s % 4, i // 2, i % 2


def at_sp(x, zl, y):
    return {"sp": (x * 2 + zl) * 4 + y}


def greet(targets):
    barrier = pltpu.get_barrier_semaphore()
    for target in targets:
        pl.semaphore_signal(barrier, inc=1, device_id=target, device_id_type=MESH)
    pl.semaphore_wait(barrier, len(targets))


def gather_kernel(shapes, *refs):
    count = len(shapes)
    ins, outs, shards, packs = (refs[k * count : (k + 1) * count] for k in range(4))
    send, recv, local = refs[4 * count :]
    x, zl, y, zh, core = place()
    xm, xp, xo = (x + 3) % 4, (x + 1) % 4, (x + 2) % 4
    left, right = at_sp(xm, zl, y), at_sp(xp, zl, y)
    across = (x * 2 + 1 - zl) * 4 + y
    up = {"img": ((zh + zl) % 4) * 2 + core, "sp": across}
    down = {"img": ((zh + zl + 3) % 4) * 2 + core, "sp": across}
    twin = {"img": zh * 2 + 1 - core}
    column = [at_sp(x, zl, (y + k) % 4) for k in (1, 2, 3)]
    greet(column + [left, right, up, down, twin])
    copies = {}

    def push(a, slot, src, dst, target):
        copy = pltpu.make_async_remote_copy(
            src_ref=src,
            dst_ref=dst,
            send_sem=send.at[a, slot],
            recv_sem=recv.at[a, slot],
            device_id=target,
            device_id_type=MESH,
        )
        copy.start()
        copies[a, slot] = copy

    def part(a):
        half = shapes[a][3] // 2
        return half, pl.multiple_of(core * half, 128)

    def region(a, bx, bz, lo, size):
        half, first = part(a)
        return outs[a].at[bx * 2 + bz, pl.ds(lo, size), pl.ds(first, half)]

    def forward(a, slot, bx, bz, lo, size, target):
        piece = region(a, bx, bz, lo, size)
        push(a, slot, piece, piece, target)

    for a in range(count):
        half, first = part(a)
        mine = ins[a].at[:, pl.ds(first, half)]
        for k in range(3):
            push(a, k, mine, shards[a].at[y], column[k])
        shards[a][y] = ins[a][:, pl.ds(first, half)]
    keeps = []
    for a in range(count):
        rows, per, block, _ = shapes[a]
        half, first = part(a)
        low = (block // 32) * 16
        high = block - low
        for k in range(3):
            copies[a, k].wait_recv()
        r = lax.broadcasted_iota(jnp.int32, (block, 4 * rows), 0)
        c = lax.broadcasted_iota(jnp.int32, (block, 4 * rows), 1)
        skipped = jnp.zeros_like(r)
        for k in (1, 2, 3):
            skipped += jnp.where(r >= k * per, rows - per, 0)
        pick = jnp.where(c == r + skipped, 1.0, 0.0).astype(jnp.bfloat16)
        packs[a][...] = jnp.dot(
            pick, shards[a][...].reshape(4 * rows, half), preferred_element_type=jnp.float32
        ).astype(jnp.bfloat16)
        own, whole = packs[a], region(a, x, zl, 0, block)
        keep = pltpu.make_async_copy(own, whole, local.at[a])
        keep.start()
        keeps.append(keep)
        push(a, 3, own, whole, right)
        push(a, 4, own, whole, left)
        push(a, 7, own.at[pl.ds(0, low)], region(a, x, zl, 0, low), up)
        push(a, 8, own.at[pl.ds(low, high)], region(a, x, zl, low, high), down)
        push(a, 15, own, whole, twin)

    def near(a):
        block = shapes[a][2]
        low = (block // 32) * 16
        high = block - low
        copies[a, 3].wait_recv()
        forward(a, 5, xm, zl, 0, low, right)
        forward(a, 9, xm, zl, 0, low, up)
        forward(a, 10, xm, zl, low, high, down)
        forward(a, 16, xm, zl, 0, block, twin)
        copies[a, 4].wait_recv()
        forward(a, 6, xp, zl, low, high, left)
        forward(a, 11, xp, zl, 0, low, up)
        forward(a, 12, xp, zl, low, high, down)
        forward(a, 17, xp, zl, 0, block, twin)

    def far(a):
        block = shapes[a][2]
        low = (block // 32) * 16
        high = block - low
        copies[a, 5].wait_recv()
        forward(a, 13, xo, zl, 0, low, up)
        forward(a, 18, xo, zl, 0, low, twin)
        copies[a, 6].wait_recv()
        forward(a, 14, xo, zl, low, high, down)
        forward(a, 19, xo, zl, low, high, twin)

    def deep(a):
        block = shapes[a][2]
        low = (block // 32) * 16
        high = block - low
        for n, bx in enumerate((x, xm, xp, xo)):
            copies[a, 7 + 2 * n].wait_recv()
            forward(a, 20 + 2 * n, bx, 1 - zl, 0, low, twin)
            copies[a, 8 + 2 * n].wait_recv()
            forward(a, 21 + 2 * n, bx, 1 - zl, low, high, twin)

    for step in range(count + 2):
        if step < count:
            near(step)
        if 0 <= step - 1 < count:
            far(step - 1)
        if 0 <= step - 2 < count:
            deep(step - 2)
    for a in range(count):
        for slot in range(15, 28):
            copies[a, slot].wait_recv()
    for keep in keeps:
        keep.wait()
    for copy in copies.values():
        copy.wait_send()


def gather_weights(shards, pers):
    count = len(shards)
    shapes = []
    for shard, per in zip(shards, pers):
        block = -(-4 * per // 16) * 16
        shapes.append((shard.shape[0], per, block, shard.shape[1]))
    halves = [(rows, block, width // 2) for rows, _, block, width in shapes]
    return pl.pallas_call(
        functools.partial(gather_kernel, shapes),
        out_shape=[
            jax.ShapeDtypeStruct((8, block, width), jnp.bfloat16) for _, _, block, width in shapes
        ],
        in_specs=[pl.BlockSpec(memory_space=pltpu.VMEM)] * count,
        out_specs=[pl.BlockSpec(memory_space=pl.ANY)] * count,
        scratch_shapes=[pltpu.VMEM((4, rows, half), jnp.bfloat16) for rows, _, half in halves]
        + [pltpu.VMEM((block, half), jnp.bfloat16) for _, block, half in halves]
        + [
            pltpu.SemaphoreType.DMA((count, 28)),
            pltpu.SemaphoreType.DMA((count, 28)),
            pltpu.SemaphoreType.DMA((count,)),
        ],
        compiler_params=pltpu.CompilerParams(
            collective_id=0, has_side_effects=True, vmem_limit_bytes=32 * 2**20
        ),
    )(*shards)


class Scatter:
    def __init__(self, plan, parts, buffers, send, recv, local):
        self.plan, self.parts = plan, parts
        self.land1, self.sum1, self.land2, self.sum2, self.land3 = buffers
        self.send, self.recv, self.local = send, recv, local
        self.x, self.zl, self.y, _, _ = place()
        self.row = [(self.x + k) % 4 for k in (1, 2, 3)]
        self.column = [(self.y + k) % 4 for k in (1, 2, 3)]
        self.copies, self.own = {}, {}

    def push(self, n, slot, src, dst, target):
        copy = pltpu.make_async_remote_copy(
            src_ref=src,
            dst_ref=dst,
            send_sem=self.send.at[n, slot],
            recv_sem=self.recv.at[n, slot],
            device_id=target,
            device_id_type=MESH,
        )
        copy.start()
        self.copies[n, slot] = copy

    def to_row(self, k):
        return at_sp(self.row[k], self.zl, self.y)

    def to_column(self, k):
        return at_sp(self.x, self.zl, self.column[k])

    def start(self, n):
        source, first, width, x_first = self.plan[n]
        view = self.parts[source].at[:, :, :, :, pl.ds(first, width)]
        own = view.at[self.x] if x_first else view.at[:, :, self.y]
        self.own[n] = pltpu.make_async_copy(own, self.sum1[n], self.local.at[n])
        self.own[n].start()
        for k in range(3):
            if x_first:
                self.push(n, k, view.at[self.row[k]], self.land1[n].at[k], self.to_row(k))
            else:
                self.push(n, k, view.at[:, :, self.column[k]], self.land1[n].at[k], self.to_column(k))

    def second(self, n):
        x_first = self.plan[n][3]
        sums, land = self.sum1[n], self.land1[n]
        self.own[n].wait()
        for k in range(3):
            self.copies[n, k].wait_recv()
        outer, inner = sums.shape[:2]

        def add(t, carry):
            p, q = t // inner, t % inner
            total = sums[p, q].astype(jnp.float32)
            for k in range(3):
                total += land[k, p, q].astype(jnp.float32)
            sums[p, q] = total.astype(jnp.bfloat16)
            return carry

        lax.fori_loop(0, outer * inner, add, 0)
        for k in range(3):
            if x_first:
                self.push(
                    n, 3 + k, sums.at[:, self.column[k]], self.land2[n].at[k], self.to_column(k)
                )
            else:
                self.push(n, 3 + k, sums.at[self.row[k]], self.land2[n].at[k], self.to_row(k))

    def third(self, n):
        x_first = self.plan[n][3]
        for k in range(3):
            self.copies[n, 3 + k].wait_recv()
        for p in range(2):
            own = self.sum1[n][p, self.y] if x_first else self.sum1[n][self.x, p]
            total = own.astype(jnp.float32)
            for k in range(3):
                total += self.land2[n][k, p].astype(jnp.float32)
            self.sum2[n][p] = total.astype(jnp.bfloat16)
        across = at_sp(self.x, 1 - self.zl, self.y)
        self.push(n, 6, self.sum2[n].at[1 - self.zl], self.land3[n], across)

    def finish(self, n, out):
        self.copies[n, 6].wait_recv()
        out[...] = self.sum2[n][self.zl].astype(jnp.float32) + self.land3[n][...].astype(
            jnp.float32
        )

    def settle(self):
        for copy in self.copies.values():
            copy.wait_send()


def scatter_buffers(plan, rows):
    chunks = [(rows[source], width, order) for source, _, width, order in plan]

    def ordered(*lead):
        return [
            pltpu.VMEM((*lead, *((2, 4) if order else (4, 2)), r, w), jnp.bfloat16)
            for r, w, order in chunks
        ]

    def plain(*lead):
        return [pltpu.VMEM((*lead, r, w), jnp.bfloat16) for r, w, _ in chunks]

    return [ordered(3), ordered(), plain(3, 2), plain(2), plain()]


TILE = 128
QUERY_BLOCK = 512
KEY_BLOCK = 1024


def turned(block):
    wide = block.astype(jnp.float32)
    zeros = jnp.zeros((TILE - HEAD_PAD, TILE), jnp.float32)
    return jnp.concatenate([wide, zeros], axis=0).T


def head_rows(block):
    return block.T[:HEAD_PAD].astype(jnp.bfloat16)


SUM_PLAN = [
    (0, 0, 2 * DEC, True),
    (0, 2 * DEC, 2 * DEC, False),
    (1, 0, 9 * LAT, True),
    (2, 0, LAT, True),
    (3, 0, 1408, False),
]
OUT_ROWS = 22
OUT_ROWS_STEP = 24


def attention_kernel(proj, grad, d_x1, dec_part, conv_part, lat_part, *refs):
    attn_out, dqkv_out, *sum_outs = refs[:7]
    (
        q_in,
        g_in,
        kv_in,
        key_t,
        value_t,
        key,
        value,
        query,
        cot,
        query_t,
        cot_t,
        score,
        weight,
        inverse,
        offset,
        attended,
        o_send,
        dq_send,
        d_send,
        d_land,
        d_sum,
        o_land,
        d_res,
        out_part,
    ) = refs[7:31]
    groups = [refs[31 + 5 * k : 36 + 5 * k] for k in range(5)]
    send, recv, sum_send, sum_recv, sum_local = refs[56:]
    sums = Scatter(
        SUM_PLAN, [dec_part, conv_part, lat_part, out_part], groups, sum_send, sum_recv, sum_local
    )
    x, zl, y, zh, core = place()
    m = x * 2 + zl
    plane = [(m + k) % 8 for k in range(8)]
    source = [(m + 8 - k) % 8 for k in range(8)]
    column = [(y + k) % 4 for k in range(4)]

    def at_plane(k):
        return {"sp": plane[k] * 4 + y}

    def at_column(k):
        return {"sp": m * 4 + column[k]}

    greet([at_plane(k) for k in range(1, 8)] + [at_column(k) for k in range(1, 4)])
    copies = {}

    def push(slot, src, dst, target):
        copy = pltpu.make_async_remote_copy(
            src_ref=src,
            dst_ref=dst,
            send_sem=send.at[slot],
            recv_sem=recv.at[slot],
            device_id=target,
            device_id_type=MESH,
        )
        copy.start()
        copies[slot] = copy

    kv_at, q_at, g_at, ring_at, o_at, dq_at, back_at, home_at = 0, 8, 16, 24, 48, 56, 64, 72
    for k in range(1, 8):
        push(kv_at + k, proj.at[pl.ds(1, 2), plane[k]], kv_in.at[y, m], at_plane(k))
    kv_in[y, m, 0] = proj[1, m]
    kv_in[y, m, 1] = proj[2, m]
    q_in[m] = proj[0, m]
    g_in[m] = grad[m]

    def pass_on(k):
        piece = kv_in.at[y, source[k]]
        for j in range(1, 4):
            push(ring_at + 3 * k + j - 1, piece, piece, at_column(j))

    pass_on(0)
    for k in range(1, 8):
        push(q_at + k, proj.at[0, plane[k]], q_in.at[m], at_plane(k))
    for k in range(1, 8):
        copies[kv_at + k].wait_recv()
        pass_on(k)
    for k in range(1, 8):
        push(g_at + k, grad.at[plane[k]], g_in.at[m], at_plane(k))
    for n in (0, 2, 3):
        sums.start(n)
    zero_rows = jnp.zeros((TILE - HEAD_PAD, key_t.shape[1]), jnp.bfloat16)
    key_t[HEAD_PAD:] = zero_rows
    value_t[HEAD_PAD:] = zero_rows

    def prepare(t, carry):
        at = pl.ds(pl.multiple_of(t * TILE, TILE), TILE)
        block = kv_in[t // 8, t % 8, 0]
        key_t[:HEAD_PAD, at] = block
        key[at, :] = turned(block).astype(jnp.bfloat16)
        block = kv_in[t // 8, t % 8, 1]
        value_t[:HEAD_PAD, at] = block
        value[at, :] = turned(block).astype(jnp.bfloat16)
        return carry

    def prepare_queries(t, carry):
        query[pl.ds(pl.multiple_of(t * TILE, TILE), TILE), :] = turned(q_in[t]).astype(jnp.bfloat16)
        return carry

    def prepare_cots(t, carry):
        cot[pl.ds(pl.multiple_of(t * TILE, TILE), TILE), :] = turned(g_in[t]).astype(jnp.bfloat16)
        return carry

    lax.fori_loop(y * 8, y * 8 + 8, prepare, 0)
    for k in range(1, 8):
        copies[q_at + k].wait_recv()
    lax.fori_loop(0, 8, prepare_queries, 0)
    for j in range(1, 4):
        for k in range(8):
            copies[ring_at + 3 * k + j - 1].wait_recv()
        first = ((y + 4 - j) % 4) * 8
        lax.fori_loop(first, first + 8, prepare, 0)
    sums.start(1)
    for k in range(1, 8):
        copies[g_at + k].wait_recv()
    lax.fori_loop(0, 8, prepare_cots, 0)

    tokens = key.shape[0]
    queries = query.shape[0]
    blocks = [pl.ds(c * KEY_BLOCK, KEY_BLOCK) for c in range(tokens // KEY_BLOCK)]

    def forward(i, carry):
        at = pl.ds(pl.multiple_of(i * QUERY_BLOCK, QUERY_BLOCK), QUERY_BLOCK)
        top = jnp.full((QUERY_BLOCK, 1), -jnp.inf, jnp.float32)
        for block in blocks:
            part = jnp.dot(query[at, :], key_t[:, block], preferred_element_type=jnp.float32)
            score[:, block] = part
            top = jnp.maximum(top, jnp.max(part, axis=1, keepdims=True))
        total = jnp.zeros((QUERY_BLOCK, 1), jnp.float32)
        mixed = jnp.zeros((QUERY_BLOCK, TILE), jnp.float32)
        for block in blocks:
            part = jnp.exp(score[:, block] - top)
            total += jnp.sum(part, axis=1, keepdims=True)
            rounded = part.astype(jnp.bfloat16)
            weight[at, block] = rounded
            mixed += jnp.dot(rounded, value[block, :], preferred_element_type=jnp.float32)
        inv = 1.0 / total
        mixed = mixed * inv
        attended[at, :] = mixed
        inverse[at, :] = inv
        offset[at, :] = jnp.sum(mixed * cot[at, :].astype(jnp.float32), axis=1, keepdims=True)
        return carry

    lax.fori_loop(0, queries // QUERY_BLOCK, forward, 0)
    for t in range(8):
        at = pl.ds(t * TILE, TILE)
        o_send[t] = head_rows(attended[at, :])
    for k in range(1, 8):
        push(o_at + k, o_send.at[plane[k]], o_land.at[m], at_plane(k))
    o_land[m] = o_send[m]
    for t in range(8):
        at = pl.ds(t * TILE, TILE)
        inv = inverse[at, :]
        query_t[:, at] = (query[at, :].astype(jnp.float32) * inv).T.astype(jnp.bfloat16)
        cot_t[:, at] = (cot[at, :].astype(jnp.float32) * inv).T.astype(jnp.bfloat16)

    def key_side(left, kind):
        for j in (1, 2, 3, 0):
            yy = column[j]
            at = pl.ds(pl.multiple_of(yy * 8 * TILE, 8 * TILE), 8 * TILE)
            result = jnp.dot(left[...], weight[:, at], preferred_element_type=jnp.float32)
            for t in range(8):
                d_send[kind, j, t] = result[:HEAD_PAD, t * TILE : (t + 1) * TILE].astype(
                    jnp.bfloat16
                )
            if j:
                push(back_at + 4 * kind + j, d_send.at[kind, j], d_land.at[kind, j - 1], at_column(j))

    def key_home(kind):
        for j in range(1, 4):
            copies[back_at + 4 * kind + j].wait_recv()
        for t in range(8):
            total = d_send[kind, 0, t].astype(jnp.float32)
            for j in range(3):
                total += d_land[kind, j, t].astype(jnp.float32)
            d_sum[kind, t] = total.astype(jnp.bfloat16)
        for k in range(1, 8):
            push(
                home_at + 8 * kind + k,
                d_sum.at[kind, plane[k]],
                d_res.at[kind + 1, m],
                at_plane(k),
            )
        d_res[kind + 1, m] = d_sum[kind, m]

    key_side(cot_t, 1)
    for k in range(1, 8):
        copies[o_at + k].wait_recv()
    attn_out[...] = o_land[...]
    spread = 4 * OUT_ROWS_STEP
    r = lax.broadcasted_iota(jnp.int32, (spread, HEAD_PAD), 0)
    c = lax.broadcasted_iota(jnp.int32, (spread, HEAD_PAD), 1)
    picked = c < 0
    for k in range(4):
        low, first = k * OUT_ROWS, k * OUT_ROWS_STEP
        picked |= (c - low == r - first) & (c >= low) & (c < low + OUT_ROWS) & (r >= first)
    pick = jnp.where(picked, 1.0, 0.0).astype(jnp.bfloat16)
    for t in range(8):
        rows = jnp.dot(pick, o_land[t], preferred_element_type=jnp.float32).astype(jnp.bfloat16)
        term = jnp.dot(rows, d_x1[...], preferred_element_type=jnp.float32) * grad_scale
        for k in range(4):
            out_part[t // 2, t % 2, k] = term[
                k * OUT_ROWS_STEP : (k + 1) * OUT_ROWS_STEP
            ].astype(jnp.bfloat16)
    sums.start(4)

    def backward(i, carry):
        at = pl.ds(pl.multiple_of(i * QUERY_BLOCK, QUERY_BLOCK), QUERY_BLOCK)
        query_grad = jnp.zeros((QUERY_BLOCK, TILE), jnp.float32)
        shift = offset[at, :]
        for block in blocks:
            dprob = jnp.dot(cot[at, :], value_t[:, block], preferred_element_type=jnp.float32)
            dscore = (weight[at, block].astype(jnp.float32) * (dprob - shift)).astype(jnp.bfloat16)
            weight[at, block] = dscore
            query_grad += jnp.dot(dscore, key[block, :], preferred_element_type=jnp.float32)
        attended[at, :] = query_grad * (inverse[at, :] * HEAD ** (-0.5))
        return carry

    lax.fori_loop(0, queries // QUERY_BLOCK, backward, 0)
    key_side(query_t, 0)
    for t in range(8):
        dq_send[t] = head_rows(attended[pl.ds(t * TILE, TILE), :])
    for k in range(1, 8):
        push(dq_at + k, dq_send.at[plane[k]], d_res.at[0, m], at_plane(k))
    d_res[0, m] = dq_send[m]
    for n in (0, 1, 2, 3):
        sums.second(n)
    key_home(1)
    key_home(0)
    sums.second(4)
    for n in range(5):
        sums.third(n)
    for first in (dq_at, home_at, home_at + 8):
        for k in range(1, 8):
            copies[first + k].wait_recv()
    dqkv_out[...] = d_res[...]
    for n in range(5):
        sums.finish(n, sum_outs[n])
    for copy in copies.values():
        copy.wait_send()
    sums.settle()


def attend_both_ways(proj, grad, d_x1, dec_part, conv_part, lat_part):
    rows = [part.shape[3] for part in (dec_part, conv_part, lat_part)] + [OUT_ROWS_STEP]
    groups = scatter_buffers(SUM_PLAN, rows)
    heads = grad.shape[0]
    tokens, queries = 32 * TILE, 8 * TILE
    bf16, f32 = jnp.bfloat16, jnp.float32
    block = (HEAD_PAD, TILE)
    shapes = [
        ((8, *block), bf16),
        ((8, *block), bf16),
        ((4, 8, 2, *block), bf16),
        ((TILE, tokens), bf16),
        ((TILE, tokens), bf16),
        ((tokens, TILE), bf16),
        ((tokens, TILE), bf16),
        ((queries, TILE), bf16),
        ((queries, TILE), bf16),
        ((TILE, queries), bf16),
        ((TILE, queries), bf16),
        ((QUERY_BLOCK, tokens), f32),
        ((queries, tokens), bf16),
        ((queries, 1), f32),
        ((queries, 1), f32),
        ((queries, TILE), f32),
        ((8, *block), bf16),
        ((8, *block), bf16),
        ((2, 4, 8, *block), bf16),
        ((2, 3, 8, *block), bf16),
        ((2, 8, *block), bf16),
        ((8, *block), bf16),
        ((3, 8, *block), bf16),
        ((4, 2, 4, OUT_ROWS_STEP, d_x1.shape[1]), bf16),
    ]
    sum_sems = pltpu.SemaphoreType.DMA((len(SUM_PLAN), 7))
    return pl.pallas_call(
        attention_kernel,
        out_shape=[
            jax.ShapeDtypeStruct((heads, *block), bf16),
            jax.ShapeDtypeStruct((3, heads, *block), bf16),
        ]
        + [jax.ShapeDtypeStruct((rows[source], width), f32) for source, _, width, _ in SUM_PLAN],
        in_specs=[pl.BlockSpec(memory_space=pltpu.VMEM)] * 3
        + [pl.BlockSpec(memory_space=pl.ANY)] * 3,
        out_specs=[pl.BlockSpec(memory_space=pltpu.VMEM)] * 7,
        scratch_shapes=[pltpu.VMEM(shape, kind) for shape, kind in shapes]
        + [buffer for group in groups for buffer in group]
        + [pltpu.SemaphoreType.DMA((88,)), pltpu.SemaphoreType.DMA((88,))]
        + [sum_sems, sum_sems, pltpu.SemaphoreType.DMA((len(SUM_PLAN),))],
        compiler_params=pltpu.CompilerParams(
            collective_id=2, has_side_effects=True, vmem_limit_bytes=56 * 2**20
        ),
    )(proj, grad, d_x1, dec_part, conv_part, lat_part)


def per_device(
    y_one,
    second_stream_state,
    cot,
    layer_norm_gain,
    w_qkv,
    w_out,
    w_deconv,
    w_lateral,
    lat_gain,
    w_conv,
    conv_gain,
):
    devices = lax.axis_size("sp")
    tokens_here = y_one.shape[0]
    rows_here = tokens_here // GRID_W
    score_scale = HEAD ** (-0.5)
    standardized_input, inverse_deviation = apply_layer_norm(
        second_stream_state.astype(jnp.float32)
    )
    normalized_rows = (standardized_input * layer_norm_gain).astype(jnp.bfloat16)
    depth, out_depth = w_qkv.shape[0], w_out.shape[0]
    qkv_shard = jnp.pad(
        w_qkv.reshape(depth, 3 * HEADS, HEAD),
        ((0, ROWS_PAD - depth), (0, 0), (0, HEAD_PAD - HEAD)),
    ).reshape(ROWS_PAD, 3 * HEADS * HEAD_PAD)
    out_shard = jnp.pad(
        w_out, ((0, OUT_ROWS_PAD - out_depth), (0, OUT_COLS_PAD - w_out.shape[1]))
    )
    deconv_shard = jnp.pad(w_deconv, ((0, ROWS_PAD - depth), (0, 0)))
    deconv_full, qkv_full, out_full = gather_weights(
        [deconv_shard, qkv_shard, out_shard], [depth, depth, out_depth]
    )
    deconv_full = deconv_full.reshape(devices * depth, -1)
    qkv_full = qkv_full.reshape(devices * depth, -1)
    out_full = out_full.reshape(HEADS * HEAD_PAD, -1)[:, : w_out.shape[1]]
    feature = ((y_one.astype(jnp.float32) + second_stream_state.astype(jnp.float32)) * 0.5).astype(
        jnp.bfloat16
    )
    upsampled = jnp.dot(feature, deconv_full, preferred_element_type=jnp.float32).astype(
        jnp.bfloat16
    )
    pixel_rows = 2 * rows_here
    pixel_cols = 2 * GRID_W
    pixels = (
        upsampled.reshape(rows_here, GRID_W, 2, 2, DEC)
        .transpose(0, 2, 1, 3, 4)
        .reshape(pixel_rows * pixel_cols, DEC)
    )
    lhat, linv = apply_layer_norm(jnp.dot(pixels, w_lateral, preferred_element_type=jnp.float32))
    activation = (lhat * lat_gain).astype(jnp.bfloat16).reshape(pixel_rows, pixel_cols, LAT)
    extended = padded_2(activation, (("sp", 0),), 1)
    padded = jnp.pad(extended, ((0, 0), (1, 1), (0, 0)))
    chat, cinv = apply_layer_norm(conv_valid(padded, w_conv))
    dconv = layer_norm_reverse(cot.astype(jnp.float32) * conv_gain, chat, cinv).astype(jnp.bfloat16)
    flipped = w_conv[::-1, ::-1].transpose(0, 1, 3, 2)
    spread_rows = conv_valid(jnp.pad(dconv, ((2, 2), (1, 1), (0, 0))), flipped)
    from_below = shifted_2(spread_rows[-1].astype(jnp.bfloat16), "sp", 1).astype(jnp.float32)
    from_above = shifted_2(spread_rows[0].astype(jnp.bfloat16), "sp", -1).astype(jnp.float32)
    dact = spread_rows[1:-1]
    dact = dact.at[0].add(from_below).at[-1].add(from_above)
    patches = jnp.stack(
        [
            padded[row_shift : row_shift + pixel_rows, col_shift : col_shift + pixel_cols].reshape(
                -1, LAT
            )
            for row_shift in range(3)
            for col_shift in range(3)
        ]
    )
    conv_product = jnp.einsum(
        "kpc,pd->ckd", patches, dconv.reshape(-1, LAT), preferred_element_type=jnp.float32
    )
    conv_part = (conv_product.reshape(4, 2, 4, LAT // devices, 9 * LAT) * grad_scale).astype(
        jnp.bfloat16
    )
    dlat = layer_norm_reverse(dact.reshape(-1, LAT) * lat_gain, lhat, linv).astype(jnp.bfloat16)
    lat_rows = DEC // devices
    lat_part = rounded_part(pixels, dlat).reshape(devices, lat_rows, LAT)
    lat_part = jnp.pad(lat_part, ((0, 0), (0, 16 - lat_rows), (0, 0))).reshape(4, 2, 4, 16, LAT)
    dpixels = lax.dot_general(
        dlat, w_lateral, (((1,), (1,)), ((), ())), preferred_element_type=jnp.float32
    ).astype(jnp.bfloat16)
    dup = (
        dpixels.reshape(rows_here, 2, GRID_W, 2, DEC)
        .transpose(0, 2, 1, 3, 4)
        .reshape(tokens_here, 4 * DEC)
    )
    spread_feature = jnp.pad(
        feature.reshape(tokens_here, devices, depth), ((0, 0), (0, 0), (0, ROWS_PAD - depth))
    ).reshape(tokens_here, devices * ROWS_PAD)
    dec_part = rounded_part(spread_feature, dup).reshape(4, 2, 4, ROWS_PAD, 4 * DEC)
    halfway_split = 0.5 * lax.dot_general(
        dup, deconv_full, (((1,), (1,)), ((), ())), preferred_element_type=jnp.float32
    )
    d_x1 = halfway_split.astype(jnp.bfloat16)
    dattn = lax.dot_general(
        out_full, d_x1, (((1,), (1,)), ((), ())), preferred_element_type=jnp.float32
    ).astype(jnp.bfloat16)
    projected = lax.optimization_barrier(
        jnp.dot(normalized_rows, qkv_full, preferred_element_type=jnp.float32)
    )
    projected = projected.T.reshape(3, HEADS, HEAD_PAD, tokens_here)
    scales = jnp.array([score_scale, 1.0, 1.0], jnp.float32).reshape(3, 1, 1, 1)
    projected = (projected * scales).astype(jnp.bfloat16)
    attn_heads, dqkv, dec_low, dec_high, conv_rows, lat_sums, out_rows = attend_both_ways(
        projected,
        dattn.reshape(HEADS, HEAD_PAD, tokens_here),
        d_x1,
        dec_part,
        conv_part,
        lat_part,
    )
    mixed = lax.dot_general(
        attn_heads.reshape(HEADS * HEAD_PAD, tokens_here),
        out_full,
        (((0,), (0,)), ((), ())),
        preferred_element_type=jnp.float32,
    )
    x_one = (y_one.astype(jnp.float32) - mixed).astype(jnp.bfloat16)
    normalized_gradient = lax.dot_general(
        dqkv.reshape(3 * HEADS * HEAD_PAD, tokens_here),
        qkv_full, (((0,), (1,)), ((), ())), preferred_element_type=jnp.float32
    )
    second_input_gradient = (
        halfway_split
        + layer_norm_reverse(
            normalized_gradient * layer_norm_gain, standardized_input, inverse_deviation
        )
    ).astype(jnp.bfloat16)
    g_deconv = jnp.concatenate([dec_low[:depth], dec_high[:depth]], axis=1)
    g_out = out_rows[:out_depth]
    g_lateral = lat_sums[:lat_rows]
    g_conv = conv_rows.reshape(conv_rows.shape[0], 3, 3, LAT).transpose(1, 2, 0, 3)
    return (x_one, d_x1, second_input_gradient, g_out, g_deconv, g_lateral, g_conv)


def solution(mesh):
    return jax.shard_map(
        per_device,
        mesh=mesh,
        in_specs=(
            P(("img", "sp"), None),
            P(("img", "sp"), None),
            P(("img", "sp"), None, None),
            P(),
            P("sp", None),
            P("sp", None),
            P("sp", None),
            P(),
            P(),
            P(),
            P(),
        ),
        out_specs=(
            P(("img", "sp"), None),
            P(("img", "sp"), None),
            P(("img", "sp"), None),
            P(("img", "sp"), None),
            P(("img", "sp"), None),
            P(("img", "sp"), None),
            P("img", None, "sp", None),
        ),
        check_vma=False,
    )
```

```python
import functools

import jax
import jax.numpy as jnp
from jax import lax
from jax.experimental import pallas as pl
from jax.experimental.pallas import tpu as pltpu
from jax.sharding import PartitionSpec as P

HEADS = 8
HEAD = 88
DEC = 384
LAT = 256
GRID_W = 64


epsilon = 1e-06
grad_scale = 0.015625


def apply_layer_norm(values):
    centered = values - jnp.mean(values, axis=-1, keepdims=True)
    inverse = lax.rsqrt(jnp.mean(centered * centered, axis=-1, keepdims=True) + epsilon)
    return (centered * inverse, inverse)


def layer_norm_reverse(upstream, normalized_rows, inverse):
    first = jnp.mean(upstream, axis=-1, keepdims=True)
    second = jnp.mean(upstream * normalized_rows, axis=-1, keepdims=True)
    return inverse * (upstream - first - normalized_rows * second)


MESH = pl.DeviceIdType.MESH
ROWS_PAD = 48
HEAD_PAD = 96
OUT_ROWS_PAD = 32
OUT_COLS_PAD = 1536


def place():
    s, i = lax.axis_index("sp"), lax.axis_index("img")
    return s // 8, (s // 4) % 2, s % 4, i // 2, i % 2


def at_sp(x, zl, y):
    return {"sp": (x * 2 + zl) * 4 + y}


def greet(targets):
    barrier = pltpu.get_barrier_semaphore()
    for target in targets:
        pl.semaphore_signal(barrier, inc=1, device_id=target, device_id_type=MESH)
    pl.semaphore_wait(barrier, len(targets))


def one_hot(rows, per, block):
    r = lax.broadcasted_iota(jnp.int32, (block, 4 * rows), 0)
    c = lax.broadcasted_iota(jnp.int32, (block, 4 * rows), 1)
    skipped = jnp.zeros_like(r)
    for k in (1, 2, 3):
        skipped += jnp.where(r >= k * per, rows - per, 0)
    return jnp.where(c == r + skipped, 1.0, 0.0)


def gather_kernel(shapes, *refs):
    count = len(shapes)
    ins = refs[:3]
    y_one, second, cot, w_lateral, lat_gain, w_conv, conv_gain = refs[3:10]
    qkv_out, w_out_out, half_out, d_x1_out, dec_out, conv_out, lat_out = refs[10:17]
    deconv, *rest = refs[17:]
    outs = [deconv, qkv_out, w_out_out]
    shards, packs, rest = rest[:3], rest[3:6], rest[6:]
    feature, pixels, act, dconv, cot_low, cot_high, norm_lat, dup, *sems = rest
    send, recv, local, halo_send, halo_recv = sems
    x, zl, y, zh, core = place()
    s = lax.axis_index("sp")
    below, above = {"sp": (s + 1) % 32}, {"sp": (s + 31) % 32}
    xm, xp, xo = (x + 3) % 4, (x + 1) % 4, (x + 2) % 4
    left, right = at_sp(xm, zl, y), at_sp(xp, zl, y)
    across = (x * 2 + 1 - zl) * 4 + y
    up = {"img": ((zh + zl) % 4) * 2 + core, "sp": across}
    down = {"img": ((zh + zl + 3) % 4) * 2 + core, "sp": across}
    twin = {"img": zh * 2 + 1 - core}
    column = [at_sp(x, zl, (y + k) % 4) for k in (1, 2, 3)]
    greet(column + [left, right, up, down, twin, below, above])
    copies = {}

    def push(a, slot, src, dst, target):
        copy = pltpu.make_async_remote_copy(
            src_ref=src,
            dst_ref=dst,
            send_sem=send.at[a, slot],
            recv_sem=recv.at[a, slot],
            device_id=target,
            device_id_type=MESH,
        )
        copy.start()
        copies[a, slot] = copy

    def part(a):
        half = shapes[a][3] // 2
        return half, pl.multiple_of(core * half, 128)

    def region(a, bx, bz, lo, size):
        half, first = part(a)
        return outs[a].at[bx * 2 + bz, pl.ds(lo, size), pl.ds(first, half)]

    def forward(a, slot, bx, bz, lo, size, target):
        piece = region(a, bx, bz, lo, size)
        push(a, slot, piece, piece, target)

    for a in range(count):
        half, first = part(a)
        mine = ins[a].at[:, pl.ds(first, half)]
        for k in range(3):
            push(a, k, mine, shards[a].at[y], column[k])
        shards[a][y] = ins[a][:, pl.ds(first, half)]
    keeps = []
    for a in range(count):
        rows, per, block, _ = shapes[a]
        half, first = part(a)
        low = (block // 32) * 16
        high = block - low
        for k in range(3):
            copies[a, k].wait_recv()
        pick = one_hot(rows, per, block).astype(jnp.bfloat16)
        packs[a][...] = jnp.dot(
            pick, shards[a][...].reshape(4 * rows, half), preferred_element_type=jnp.float32
        ).astype(jnp.bfloat16)
        own, whole = packs[a], region(a, x, zl, 0, block)
        keep = pltpu.make_async_copy(own, whole, local.at[a])
        keep.start()
        keeps.append(keep)
        push(a, 3, own, whole, right)
        push(a, 4, own, whole, left)
        push(a, 7, own.at[pl.ds(0, low)], region(a, x, zl, 0, low), up)
        push(a, 8, own.at[pl.ds(low, high)], region(a, x, zl, low, high), down)
        push(a, 15, own, whole, twin)

    def near(a):
        block = shapes[a][2]
        low = (block // 32) * 16
        high = block - low
        copies[a, 3].wait_recv()
        forward(a, 5, xm, zl, 0, low, right)
        forward(a, 9, xm, zl, 0, low, up)
        forward(a, 10, xm, zl, low, high, down)
        forward(a, 16, xm, zl, 0, block, twin)
        copies[a, 4].wait_recv()
        forward(a, 6, xp, zl, low, high, left)
        forward(a, 11, xp, zl, 0, low, up)
        forward(a, 12, xp, zl, low, high, down)
        forward(a, 17, xp, zl, 0, block, twin)

    def far(a):
        block = shapes[a][2]
        low = (block // 32) * 16
        high = block - low
        copies[a, 5].wait_recv()
        forward(a, 13, xo, zl, 0, low, up)
        forward(a, 18, xo, zl, 0, low, twin)
        copies[a, 6].wait_recv()
        forward(a, 14, xo, zl, low, high, down)
        forward(a, 19, xo, zl, low, high, twin)

    def deep(a):
        block = shapes[a][2]
        low = (block // 32) * 16
        high = block - low
        for n, bx in enumerate((x, xm, xp, xo)):
            copies[a, 7 + 2 * n].wait_recv()
            forward(a, 20 + 2 * n, bx, 1 - zl, 0, low, twin)
            copies[a, 8 + 2 * n].wait_recv()
            forward(a, 21 + 2 * n, bx, 1 - zl, low, high, twin)

    def twins(a):
        for slot in range(15, 28):
            copies[a, slot].wait_recv()

    row = GRID_W
    inner_rows = 4 * row
    halos = {}

    def swap_edges(ref, first):
        ends = (
            (first, pl.ds(inner_rows, row), pl.ds(0, row), below),
            (first + 1, pl.ds(row, row), pl.ds(inner_rows + row, row), above),
        )
        for slot, src_rows, dst_rows, target in ends:
            copy = pltpu.make_async_remote_copy(
                src_ref=ref.at[pl.ds(1, 2), src_rows],
                dst_ref=ref.at[pl.ds(1, 2), dst_rows],
                send_sem=halo_send.at[slot],
                recv_sem=halo_recv.at[slot],
                device_id=target,
                device_id_type=MESH,
            )
            copy.start()
            halos[slot] = copy

    def fill_sides(ref, first):
        halos[first].wait_recv()
        halos[first + 1].wait_recv()
        for b in (1, 2):
            head, tail = pl.ds(0, row), pl.ds(inner_rows + row, row)
            ref[b, head] = jnp.where(s == 0, 0.0, ref[b, head].astype(jnp.float32)).astype(
                jnp.bfloat16
            )
            ref[b, tail] = jnp.where(s == 31, 0.0, ref[b, tail].astype(jnp.float32)).astype(
                jnp.bfloat16
            )
        rows = ref.shape[1]
        at = lax.broadcasted_iota(jnp.int32, (rows, LAT), 0) % row
        moved = pltpu.roll(ref[2].astype(jnp.float32), 1, 0)
        ref[0] = jnp.where(at == 0, 0.0, moved).astype(jnp.bfloat16)
        moved = pltpu.roll(ref[1].astype(jnp.float32), rows - 1, 0)
        ref[3] = jnp.where(at == row - 1, 0.0, moved).astype(jnp.bfloat16)

    def taps():
        return [(i, j) for i in range(3) for j in range(3)]

    def upward():
        feature[...] = ((y_one[...].astype(jnp.float32) + second[...].astype(jnp.float32)) * 0.5).astype(
            jnp.bfloat16
        )
        wide = cot[...].reshape(8 * row, LAT).astype(jnp.float32)
        cot_low[...] = wide[:, : LAT // 2]
        cot_high[...] = wide[:, LAT // 2 :]
        depth = deconv.shape[0] * deconv.shape[1]
        for ab in range(4):
            plane = pl.ds(ab * DEC, DEC)
            up = jnp.dot(
                feature[...],
                deconv[:, :, plane].reshape(depth, DEC),
                preferred_element_type=jnp.float32,
            ).astype(jnp.bfloat16)
            for r in range(2):
                pixels[pl.ds((ab % 2) * inner_rows + (2 * r + ab // 2) * row, row)] = up[
                    r * row : (r + 1) * row
                ]
        lat = jnp.dot(pixels[...], w_lateral[...], preferred_element_type=jnp.float32)
        lhat, linv = apply_layer_norm(lat)
        norm_lat[...] = lhat
        scaled = (lhat * lat_gain[...]).astype(jnp.bfloat16)
        for b in range(2):
            act[1 + b, pl.ds(row, inner_rows)] = scaled[b * inner_rows : (b + 1) * inner_rows]
        swap_edges(act, 0)
        return linv

    def convolve():
        fill_sides(act, 0)
        for b in range(2):
            total = jnp.zeros((inner_rows, LAT), jnp.float32)
            for i, j in taps():
                total += jnp.dot(
                    act[b + j, pl.ds(i * row, inner_rows)],
                    w_conv[3 * i + j],
                    preferred_element_type=jnp.float32,
                )
            chat, cinv = apply_layer_norm(total)
            every = pl.ds(b, inner_rows, stride=2)
            upstream = jnp.concatenate([cot_low[every, :], cot_high[every, :]], axis=1)
            upstream = upstream * conv_gain[...]
            dconv[1 + b, pl.ds(row, inner_rows)] = layer_norm_reverse(upstream, chat, cinv).astype(
                jnp.bfloat16
            )
        swap_edges(dconv, 2)

    def downward(linv):
        fill_sides(dconv, 2)
        for b in range(2):
            total = jnp.zeros((inner_rows, LAT), jnp.float32)
            for i, j in taps():
                total += lax.dot_general(
                    dconv[b - j + 2, pl.ds((2 - i) * row, inner_rows)],
                    w_conv[3 * i + j],
                    (((1,), (1,)), ((), ())),
                    preferred_element_type=jnp.float32,
                )
            here = slice(b * inner_rows, (b + 1) * inner_rows)
            dlat = layer_norm_reverse(
                total * lat_gain[...], norm_lat[pl.ds(b * inner_rows, inner_rows)], linv[here]
            ).astype(jnp.bfloat16)
            term = jnp.dot(
                pixels[pl.ds(b * inner_rows, inner_rows)].astype(jnp.float32).T.astype(jnp.bfloat16),
                dlat,
                preferred_element_type=jnp.float32,
            )
            lat_term = term if b == 0 else lat_term + term
            dpixels = lax.dot_general(
                dlat, w_lateral[...], (((1,), (1,)), ((), ())), preferred_element_type=jnp.float32
            ).astype(jnp.bfloat16)
            for line in range(4):
                r, a = line // 2, line % 2
                dup[pl.ds(r * row, row), pl.ds((2 * a + b) * DEC, DEC)] = dpixels[
                    line * row : (line + 1) * row
                ]
        lat_out[...] = (lat_term * grad_scale).astype(jnp.bfloat16)
        depth = deconv.shape[0] * deconv.shape[1]
        half = 0.5 * lax.dot_general(
            dup[...],
            deconv[...].reshape(depth, 4 * DEC),
            (((1,), (1,)), ((), ())),
            preferred_element_type=jnp.float32,
        )
        half_out[...] = half
        d_x1_out[...] = half.astype(jnp.bfloat16)

    def conv_term():
        turned_grads = [
            dconv[1 + b, pl.ds(row, inner_rows)].astype(jnp.float32).T.astype(jnp.bfloat16)
            for b in range(2)
        ]
        for i, j in taps():
            total = jnp.zeros((LAT, LAT), jnp.float32)
            for b in range(2):
                total += jnp.dot(
                    turned_grads[b],
                    act[b + j, pl.ds(i * row, inner_rows)],
                    preferred_element_type=jnp.float32,
                )
            conv_out[:, pl.ds((3 * i + j) * LAT, LAT)] = (total.T * grad_scale).astype(jnp.bfloat16)

    def deconv_term():
        rows, per, block, _ = shapes[0]
        wide = feature[...].astype(jnp.float32).T
        pick = one_hot(rows, per, block).T.astype(jnp.bfloat16)
        for g in range(8):
            group = jnp.dot(
                pick,
                wide[g * block : (g + 1) * block].astype(jnp.bfloat16),
                preferred_element_type=jnp.float32,
            ).astype(jnp.bfloat16)
            term = jnp.dot(group, dup[...], preferred_element_type=jnp.float32) * grad_scale
            dec_out[pl.ds(g * 4 * rows, 4 * rows)] = term.astype(jnp.bfloat16)

    near(0)
    near(1)
    far(0)
    deep(0)
    twins(0)
    keeps[0].wait()
    linv = upward()
    far(1)
    near(2)
    convolve()
    far(2)
    downward(linv)
    deep(1)
    conv_term()
    deep(2)
    deconv_term()
    twins(1)
    twins(2)
    for keep in keeps[1:]:
        keep.wait()
    for copy in list(copies.values()) + list(halos.values()):
        copy.wait_send()


def gather_and_pyramid(shards, pers, *others):
    count = len(shards)
    shapes = []
    for shard, per in zip(shards, pers):
        block = -(-4 * per // 16) * 16
        shapes.append((shard.shape[0], per, block, shard.shape[1]))
    halves = [(rows, block, width // 2) for rows, _, block, width in shapes]
    tokens, features = others[0].shape
    bf16, f32 = jnp.bfloat16, jnp.float32
    full = [jax.ShapeDtypeStruct((8, block, width), bf16) for _, _, block, width in shapes]
    pixel_count = 4 * tokens
    return pl.pallas_call(
        functools.partial(gather_kernel, shapes),
        out_shape=full[1:]
        + [
            jax.ShapeDtypeStruct((tokens, features), f32),
            jax.ShapeDtypeStruct((tokens, features), bf16),
            jax.ShapeDtypeStruct((32 * ROWS_PAD, 4 * DEC), bf16),
            jax.ShapeDtypeStruct((LAT, 9 * LAT), bf16),
            jax.ShapeDtypeStruct((DEC, LAT), bf16),
        ],
        in_specs=[pl.BlockSpec(memory_space=pltpu.VMEM)] * (count + len(others)),
        out_specs=[pl.BlockSpec(memory_space=pl.ANY)] * (count - 1)
        + [pl.BlockSpec(memory_space=pltpu.VMEM)] * 5,
        scratch_shapes=[pltpu.VMEM(full[0].shape, bf16)]
        + [pltpu.VMEM((4, rows, half), bf16) for rows, _, half in halves]
        + [pltpu.VMEM((block, half), bf16) for _, block, half in halves]
        + [
            pltpu.VMEM((tokens, features), bf16),
            pltpu.VMEM((pixel_count, DEC), bf16),
            pltpu.VMEM((4, 6 * GRID_W, LAT), bf16),
            pltpu.VMEM((4, 6 * GRID_W, LAT), bf16),
            pltpu.VMEM((pixel_count, LAT // 2), f32),
            pltpu.VMEM((pixel_count, LAT // 2), f32),
            pltpu.VMEM((pixel_count, LAT), f32),
            pltpu.VMEM((tokens, 4 * DEC), bf16),
            pltpu.SemaphoreType.DMA((count, 28)),
            pltpu.SemaphoreType.DMA((count, 28)),
            pltpu.SemaphoreType.DMA((count,)),
            pltpu.SemaphoreType.DMA((4,)),
            pltpu.SemaphoreType.DMA((4,)),
        ],
        compiler_params=pltpu.CompilerParams(
            collective_id=0, has_side_effects=True, vmem_limit_bytes=56 * 2**20
        ),
    )(*shards, *others)


class Scatter:
    def __init__(self, plan, parts, buffers, send, recv, local):
        self.plan, self.parts = plan, parts
        self.land1, self.sum1, self.land2, self.sum2, self.land3 = buffers
        self.send, self.recv, self.local = send, recv, local
        self.x, self.zl, self.y, _, _ = place()
        self.row = [(self.x + k) % 4 for k in (1, 2, 3)]
        self.column = [(self.y + k) % 4 for k in (1, 2, 3)]
        self.copies, self.own = {}, {}

    def push(self, n, slot, src, dst, target):
        copy = pltpu.make_async_remote_copy(
            src_ref=src,
            dst_ref=dst,
            send_sem=self.send.at[n, slot],
            recv_sem=self.recv.at[n, slot],
            device_id=target,
            device_id_type=MESH,
        )
        copy.start()
        self.copies[n, slot] = copy

    def to_row(self, k):
        return at_sp(self.row[k], self.zl, self.y)

    def to_column(self, k):
        return at_sp(self.x, self.zl, self.column[k])

    def start(self, n):
        source, first, width, x_first = self.plan[n]
        view = self.parts[source].at[:, :, :, :, pl.ds(first, width)]
        own = view.at[self.x] if x_first else view.at[:, :, self.y]
        self.own[n] = pltpu.make_async_copy(own, self.sum1[n], self.local.at[n])
        self.own[n].start()
        for k in range(3):
            if x_first:
                self.push(n, k, view.at[self.row[k]], self.land1[n].at[k], self.to_row(k))
            else:
                self.push(n, k, view.at[:, :, self.column[k]], self.land1[n].at[k], self.to_column(k))

    def second(self, n):
        x_first = self.plan[n][3]
        sums, land = self.sum1[n], self.land1[n]
        self.own[n].wait()
        for k in range(3):
            self.copies[n, k].wait_recv()
        outer, inner = sums.shape[:2]

        def add(t, carry):
            p, q = t // inner, t % inner
            total = sums[p, q].astype(jnp.float32)
            for k in range(3):
                total += land[k, p, q].astype(jnp.float32)
            sums[p, q] = total.astype(jnp.bfloat16)
            return carry

        lax.fori_loop(0, outer * inner, add, 0)
        for k in range(3):
            if x_first:
                self.push(
                    n, 3 + k, sums.at[:, self.column[k]], self.land2[n].at[k], self.to_column(k)
                )
            else:
                self.push(n, 3 + k, sums.at[self.row[k]], self.land2[n].at[k], self.to_row(k))

    def third(self, n):
        x_first = self.plan[n][3]
        for k in range(3):
            self.copies[n, 3 + k].wait_recv()
        for p in range(2):
            own = self.sum1[n][p, self.y] if x_first else self.sum1[n][self.x, p]
            total = own.astype(jnp.float32)
            for k in range(3):
                total += self.land2[n][k, p].astype(jnp.float32)
            self.sum2[n][p] = total.astype(jnp.bfloat16)
        across = at_sp(self.x, 1 - self.zl, self.y)
        self.push(n, 6, self.sum2[n].at[1 - self.zl], self.land3[n], across)

    def finish(self, n, out):
        self.copies[n, 6].wait_recv()
        out[...] = self.sum2[n][self.zl].astype(jnp.float32) + self.land3[n][...].astype(
            jnp.float32
        )

    def settle(self):
        for copy in self.copies.values():
            copy.wait_send()


def scatter_buffers(plan, rows):
    chunks = [(rows[source], width, order) for source, _, width, order in plan]

    def ordered(*lead):
        return [
            pltpu.VMEM((*lead, *((2, 4) if order else (4, 2)), r, w), jnp.bfloat16)
            for r, w, order in chunks
        ]

    def plain(*lead):
        return [pltpu.VMEM((*lead, r, w), jnp.bfloat16) for r, w, _ in chunks]

    return [ordered(3), ordered(), plain(3, 2), plain(2), plain()]


TILE = 128
QUERY_BLOCK = 512
KEY_BLOCK = 1024


def turned(block):
    wide = block.astype(jnp.float32)
    zeros = jnp.zeros((TILE - HEAD_PAD, TILE), jnp.float32)
    return jnp.concatenate([wide, zeros], axis=0).T


def head_rows(block):
    return block.T[:HEAD_PAD].astype(jnp.bfloat16)


SUM_PLAN = [
    (0, 0, 2 * DEC, True),
    (0, 2 * DEC, 2 * DEC, False),
    (1, 0, 9 * LAT, True),
    (2, 0, LAT, True),
    (3, 0, 1408, False),
]
OUT_ROWS = 22
OUT_ROWS_STEP = 24


def attention_kernel(proj, grad, d_x1, dec_part, conv_part, lat_part, *refs):
    attn_out, dqkv_out, *sum_outs = refs[:7]
    (
        q_in,
        g_in,
        kv_in,
        key_t,
        value_t,
        key,
        value,
        query,
        cot,
        query_t,
        cot_t,
        score,
        weight,
        inverse,
        offset,
        attended,
        o_send,
        dq_send,
        d_send,
        d_land,
        d_sum,
        o_land,
        d_res,
        out_part,
    ) = refs[7:31]
    groups = [refs[31 + 5 * k : 36 + 5 * k] for k in range(5)]
    send, recv, sum_send, sum_recv, sum_local = refs[56:]
    sums = Scatter(
        SUM_PLAN, [dec_part, conv_part, lat_part, out_part], groups, sum_send, sum_recv, sum_local
    )
    x, zl, y, zh, core = place()
    m = x * 2 + zl
    plane = [(m + k) % 8 for k in range(8)]
    source = [(m + 8 - k) % 8 for k in range(8)]
    column = [(y + k) % 4 for k in range(4)]

    def at_plane(k):
        return {"sp": plane[k] * 4 + y}

    def at_column(k):
        return {"sp": m * 4 + column[k]}

    greet([at_plane(k) for k in range(1, 8)] + [at_column(k) for k in range(1, 4)])
    copies = {}

    def push(slot, src, dst, target):
        copy = pltpu.make_async_remote_copy(
            src_ref=src,
            dst_ref=dst,
            send_sem=send.at[slot],
            recv_sem=recv.at[slot],
            device_id=target,
            device_id_type=MESH,
        )
        copy.start()
        copies[slot] = copy

    kv_at, q_at, g_at, ring_at, o_at, dq_at, back_at, home_at = 0, 8, 16, 24, 48, 56, 64, 72
    for k in range(1, 8):
        push(kv_at + k, proj.at[pl.ds(1, 2), plane[k]], kv_in.at[y, m], at_plane(k))
    kv_in[y, m, 0] = proj[1, m]
    kv_in[y, m, 1] = proj[2, m]
    q_in[m] = proj[0, m]
    g_in[m] = grad[m]

    def pass_on(k):
        piece = kv_in.at[y, source[k]]
        for j in range(1, 4):
            push(ring_at + 3 * k + j - 1, piece, piece, at_column(j))

    pass_on(0)
    for k in range(1, 8):
        push(q_at + k, proj.at[0, plane[k]], q_in.at[m], at_plane(k))
    for k in range(1, 8):
        copies[kv_at + k].wait_recv()
        pass_on(k)
    for k in range(1, 8):
        push(g_at + k, grad.at[plane[k]], g_in.at[m], at_plane(k))
    for n in (0, 2, 3):
        sums.start(n)
    zero_rows = jnp.zeros((TILE - HEAD_PAD, key_t.shape[1]), jnp.bfloat16)
    key_t[HEAD_PAD:] = zero_rows
    value_t[HEAD_PAD:] = zero_rows

    def prepare(t, carry):
        at = pl.ds(pl.multiple_of(t * TILE, TILE), TILE)
        block = kv_in[t // 8, t % 8, 0]
        key_t[:HEAD_PAD, at] = block
        key[at, :] = turned(block).astype(jnp.bfloat16)
        block = kv_in[t // 8, t % 8, 1]
        value_t[:HEAD_PAD, at] = block
        value[at, :] = turned(block).astype(jnp.bfloat16)
        return carry

    def prepare_queries(t, carry):
        query[pl.ds(pl.multiple_of(t * TILE, TILE), TILE), :] = turned(q_in[t]).astype(jnp.bfloat16)
        return carry

    def prepare_cots(t, carry):
        cot[pl.ds(pl.multiple_of(t * TILE, TILE), TILE), :] = turned(g_in[t]).astype(jnp.bfloat16)
        return carry

    lax.fori_loop(y * 8, y * 8 + 8, prepare, 0)
    for k in range(1, 8):
        copies[q_at + k].wait_recv()
    lax.fori_loop(0, 8, prepare_queries, 0)
    for j in range(1, 4):
        for k in range(8):
            copies[ring_at + 3 * k + j - 1].wait_recv()
        first = ((y + 4 - j) % 4) * 8
        lax.fori_loop(first, first + 8, prepare, 0)
    sums.start(1)
    for k in range(1, 8):
        copies[g_at + k].wait_recv()
    lax.fori_loop(0, 8, prepare_cots, 0)

    tokens = key.shape[0]
    queries = query.shape[0]
    blocks = [pl.ds(c * KEY_BLOCK, KEY_BLOCK) for c in range(tokens // KEY_BLOCK)]

    def forward(i, carry):
        at = pl.ds(pl.multiple_of(i * QUERY_BLOCK, QUERY_BLOCK), QUERY_BLOCK)
        top = jnp.full((QUERY_BLOCK, 1), -jnp.inf, jnp.float32)
        for block in blocks:
            part = jnp.dot(query[at, :], key_t[:, block], preferred_element_type=jnp.float32)
            score[:, block] = part
            top = jnp.maximum(top, jnp.max(part, axis=1, keepdims=True))
        total = jnp.zeros((QUERY_BLOCK, 1), jnp.float32)
        mixed = jnp.zeros((QUERY_BLOCK, TILE), jnp.float32)
        for block in blocks:
            part = jnp.exp(score[:, block] - top)
            total += jnp.sum(part, axis=1, keepdims=True)
            rounded = part.astype(jnp.bfloat16)
            weight[at, block] = rounded
            mixed += jnp.dot(rounded, value[block, :], preferred_element_type=jnp.float32)
        inv = 1.0 / total
        mixed = mixed * inv
        attended[at, :] = mixed
        inverse[at, :] = inv
        offset[at, :] = jnp.sum(mixed * cot[at, :].astype(jnp.float32), axis=1, keepdims=True)
        return carry

    lax.fori_loop(0, queries // QUERY_BLOCK, forward, 0)
    for t in range(8):
        at = pl.ds(t * TILE, TILE)
        o_send[t] = head_rows(attended[at, :])
    for k in range(1, 8):
        push(o_at + k, o_send.at[plane[k]], o_land.at[m], at_plane(k))
    o_land[m] = o_send[m]
    for t in range(8):
        at = pl.ds(t * TILE, TILE)
        inv = inverse[at, :]
        query_t[:, at] = (query[at, :].astype(jnp.float32) * inv).T.astype(jnp.bfloat16)
        cot_t[:, at] = (cot[at, :].astype(jnp.float32) * inv).T.astype(jnp.bfloat16)

    def key_side(left, kind):
        for j in (1, 2, 3, 0):
            yy = column[j]
            at = pl.ds(pl.multiple_of(yy * 8 * TILE, 8 * TILE), 8 * TILE)
            result = jnp.dot(left[...], weight[:, at], preferred_element_type=jnp.float32)
            for t in range(8):
                d_send[kind, j, t] = result[:HEAD_PAD, t * TILE : (t + 1) * TILE].astype(
                    jnp.bfloat16
                )
            if j:
                push(back_at + 4 * kind + j, d_send.at[kind, j], d_land.at[kind, j - 1], at_column(j))

    def key_home(kind):
        for j in range(1, 4):
            copies[back_at + 4 * kind + j].wait_recv()
        for t in range(8):
            total = d_send[kind, 0, t].astype(jnp.float32)
            for j in range(3):
                total += d_land[kind, j, t].astype(jnp.float32)
            d_sum[kind, t] = total.astype(jnp.bfloat16)
        for k in range(1, 8):
            push(
                home_at + 8 * kind + k,
                d_sum.at[kind, plane[k]],
                d_res.at[kind + 1, m],
                at_plane(k),
            )
        d_res[kind + 1, m] = d_sum[kind, m]

    key_side(cot_t, 1)
    for k in range(1, 8):
        copies[o_at + k].wait_recv()
    attn_out[...] = o_land[...]
    spread = 4 * OUT_ROWS_STEP
    r = lax.broadcasted_iota(jnp.int32, (spread, HEAD_PAD), 0)
    c = lax.broadcasted_iota(jnp.int32, (spread, HEAD_PAD), 1)
    picked = c < 0
    for k in range(4):
        low, first = k * OUT_ROWS, k * OUT_ROWS_STEP
        picked |= (c - low == r - first) & (c >= low) & (c < low + OUT_ROWS) & (r >= first)
    pick = jnp.where(picked, 1.0, 0.0).astype(jnp.bfloat16)
    for t in range(8):
        rows = jnp.dot(pick, o_land[t], preferred_element_type=jnp.float32).astype(jnp.bfloat16)
        term = jnp.dot(rows, d_x1[...], preferred_element_type=jnp.float32) * grad_scale
        for k in range(4):
            out_part[t // 2, t % 2, k] = term[
                k * OUT_ROWS_STEP : (k + 1) * OUT_ROWS_STEP
            ].astype(jnp.bfloat16)
    sums.start(4)

    def backward(i, carry):
        at = pl.ds(pl.multiple_of(i * QUERY_BLOCK, QUERY_BLOCK), QUERY_BLOCK)
        query_grad = jnp.zeros((QUERY_BLOCK, TILE), jnp.float32)
        shift = offset[at, :]
        for block in blocks:
            dprob = jnp.dot(cot[at, :], value_t[:, block], preferred_element_type=jnp.float32)
            dscore = (weight[at, block].astype(jnp.float32) * (dprob - shift)).astype(jnp.bfloat16)
            weight[at, block] = dscore
            query_grad += jnp.dot(dscore, key[block, :], preferred_element_type=jnp.float32)
        attended[at, :] = query_grad * (inverse[at, :] * HEAD ** (-0.5))
        return carry

    lax.fori_loop(0, queries // QUERY_BLOCK, backward, 0)
    key_side(query_t, 0)
    for t in range(8):
        dq_send[t] = head_rows(attended[pl.ds(t * TILE, TILE), :])
    for k in range(1, 8):
        push(dq_at + k, dq_send.at[plane[k]], d_res.at[0, m], at_plane(k))
    d_res[0, m] = dq_send[m]
    for n in (0, 1, 2, 3):
        sums.second(n)
    key_home(1)
    key_home(0)
    sums.second(4)
    for n in range(5):
        sums.third(n)
    for first in (dq_at, home_at, home_at + 8):
        for k in range(1, 8):
            copies[first + k].wait_recv()
    dqkv_out[...] = d_res[...]
    for n in range(5):
        sums.finish(n, sum_outs[n])
    for copy in copies.values():
        copy.wait_send()
    sums.settle()


def attend_both_ways(proj, grad, d_x1, dec_part, conv_part, lat_part):
    rows = [part.shape[3] for part in (dec_part, conv_part, lat_part)] + [OUT_ROWS_STEP]
    groups = scatter_buffers(SUM_PLAN, rows)
    heads = grad.shape[0]
    tokens, queries = 32 * TILE, 8 * TILE
    bf16, f32 = jnp.bfloat16, jnp.float32
    block = (HEAD_PAD, TILE)
    shapes = [
        ((8, *block), bf16),
        ((8, *block), bf16),
        ((4, 8, 2, *block), bf16),
        ((TILE, tokens), bf16),
        ((TILE, tokens), bf16),
        ((tokens, TILE), bf16),
        ((tokens, TILE), bf16),
        ((queries, TILE), bf16),
        ((queries, TILE), bf16),
        ((TILE, queries), bf16),
        ((TILE, queries), bf16),
        ((QUERY_BLOCK, tokens), f32),
        ((queries, tokens), bf16),
        ((queries, 1), f32),
        ((queries, 1), f32),
        ((queries, TILE), f32),
        ((8, *block), bf16),
        ((8, *block), bf16),
        ((2, 4, 8, *block), bf16),
        ((2, 3, 8, *block), bf16),
        ((2, 8, *block), bf16),
        ((8, *block), bf16),
        ((3, 8, *block), bf16),
        ((4, 2, 4, OUT_ROWS_STEP, d_x1.shape[1]), bf16),
    ]
    sum_sems = pltpu.SemaphoreType.DMA((len(SUM_PLAN), 7))
    return pl.pallas_call(
        attention_kernel,
        out_shape=[
            jax.ShapeDtypeStruct((heads, *block), bf16),
            jax.ShapeDtypeStruct((3, heads, *block), bf16),
        ]
        + [jax.ShapeDtypeStruct((rows[source], width), f32) for source, _, width, _ in SUM_PLAN],
        in_specs=[pl.BlockSpec(memory_space=pltpu.VMEM)] * 3
        + [pl.BlockSpec(memory_space=pl.ANY)] * 3,
        out_specs=[pl.BlockSpec(memory_space=pltpu.VMEM)] * 7,
        scratch_shapes=[pltpu.VMEM(shape, kind) for shape, kind in shapes]
        + [buffer for group in groups for buffer in group]
        + [pltpu.SemaphoreType.DMA((88,)), pltpu.SemaphoreType.DMA((88,))]
        + [sum_sems, sum_sems, pltpu.SemaphoreType.DMA((len(SUM_PLAN),))],
        compiler_params=pltpu.CompilerParams(
            collective_id=2, has_side_effects=True, vmem_limit_bytes=56 * 2**20
        ),
    )(proj, grad, d_x1, dec_part, conv_part, lat_part)


def per_device(
    y_one,
    second_stream_state,
    cot,
    layer_norm_gain,
    w_qkv,
    w_out,
    w_deconv,
    w_lateral,
    lat_gain,
    w_conv,
    conv_gain,
):
    devices = lax.axis_size("sp")
    tokens_here = y_one.shape[0]
    score_scale = HEAD ** (-0.5)
    standardized_input, inverse_deviation = apply_layer_norm(
        second_stream_state.astype(jnp.float32)
    )
    normalized_rows = (standardized_input * layer_norm_gain).astype(jnp.bfloat16)
    depth, out_depth = w_qkv.shape[0], w_out.shape[0]
    qkv_shard = jnp.pad(
        w_qkv.reshape(depth, 3 * HEADS, HEAD),
        ((0, ROWS_PAD - depth), (0, 0), (0, HEAD_PAD - HEAD)),
    ).reshape(ROWS_PAD, 3 * HEADS * HEAD_PAD)
    out_shard = jnp.pad(
        w_out, ((0, OUT_ROWS_PAD - out_depth), (0, OUT_COLS_PAD - w_out.shape[1]))
    )
    deconv_shard = jnp.pad(w_deconv, ((0, ROWS_PAD - depth), (0, 0)))
    qkv_full, out_full, halfway_split, d_x1, dec_part, conv_part, lat_part = gather_and_pyramid(
        [deconv_shard, qkv_shard, out_shard],
        [depth, depth, out_depth],
        y_one,
        second_stream_state,
        cot,
        w_lateral,
        lat_gain[None],
        w_conv.reshape(9, LAT, LAT),
        conv_gain[None],
    )
    dec_part = dec_part.reshape(4, 2, 4, ROWS_PAD, 4 * DEC)
    conv_part = conv_part.reshape(4, 2, 4, LAT // devices, 9 * LAT)
    lat_rows = DEC // devices
    lat_part = jnp.pad(
        lat_part.reshape(devices, lat_rows, LAT), ((0, 0), (0, 16 - lat_rows), (0, 0))
    ).reshape(4, 2, 4, 16, LAT)
    qkv_full = qkv_full.reshape(devices * depth, -1)
    out_full = out_full.reshape(HEADS * HEAD_PAD, -1)[:, : w_out.shape[1]]
    dattn = lax.dot_general(
        out_full, d_x1, (((1,), (1,)), ((), ())), preferred_element_type=jnp.float32
    ).astype(jnp.bfloat16)
    projected = lax.optimization_barrier(
        jnp.dot(normalized_rows, qkv_full, preferred_element_type=jnp.float32)
    )
    projected = projected.T.reshape(3, HEADS, HEAD_PAD, tokens_here)
    scales = jnp.array([score_scale, 1.0, 1.0], jnp.float32).reshape(3, 1, 1, 1)
    projected = (projected * scales).astype(jnp.bfloat16)
    attn_heads, dqkv, dec_low, dec_high, conv_rows, lat_sums, out_rows = attend_both_ways(
        projected,
        dattn.reshape(HEADS, HEAD_PAD, tokens_here),
        d_x1,
        dec_part,
        conv_part,
        lat_part,
    )
    mixed = lax.dot_general(
        attn_heads.reshape(HEADS * HEAD_PAD, tokens_here),
        out_full,
        (((0,), (0,)), ((), ())),
        preferred_element_type=jnp.float32,
    )
    x_one = (y_one.astype(jnp.float32) - mixed).astype(jnp.bfloat16)
    normalized_gradient = lax.dot_general(
        dqkv.reshape(3 * HEADS * HEAD_PAD, tokens_here),
        qkv_full, (((0,), (1,)), ((), ())), preferred_element_type=jnp.float32
    )
    second_input_gradient = (
        halfway_split
        + layer_norm_reverse(
            normalized_gradient * layer_norm_gain, standardized_input, inverse_deviation
        )
    ).astype(jnp.bfloat16)
    g_deconv = jnp.concatenate([dec_low[:depth], dec_high[:depth]], axis=1)
    g_out = out_rows[:out_depth]
    g_lateral = lat_sums[:lat_rows]
    g_conv = conv_rows.reshape(conv_rows.shape[0], 3, 3, LAT).transpose(1, 2, 0, 3)
    return (x_one, d_x1, second_input_gradient, g_out, g_deconv, g_lateral, g_conv)


def solution(mesh):
    return jax.shard_map(
        per_device,
        mesh=mesh,
        in_specs=(
            P(("img", "sp"), None),
            P(("img", "sp"), None),
            P(("img", "sp"), None, None),
            P(),
            P("sp", None),
            P("sp", None),
            P("sp", None),
            P(),
            P(),
            P(),
            P(),
        ),
        out_specs=(
            P(("img", "sp"), None),
            P(("img", "sp"), None),
            P(("img", "sp"), None),
            P(("img", "sp"), None),
            P(("img", "sp"), None),
            P(("img", "sp"), None),
            P("img", None, "sp", None),
        ),
        check_vma=False,
    )
```

```python
import functools

import jax
import jax.numpy as jnp
from jax import lax
from jax.experimental import pallas as pl
from jax.experimental.pallas import tpu as pltpu
from jax.sharding import PartitionSpec as P

HEADS = 8
HEAD = 88
DEC = 384
LAT = 256
GRID_W = 64


epsilon = 1e-06
grad_scale = 0.015625


def apply_layer_norm(values):
    centered = values - jnp.mean(values, axis=-1, keepdims=True)
    inverse = lax.rsqrt(jnp.mean(centered * centered, axis=-1, keepdims=True) + epsilon)
    return (centered * inverse, inverse)


def layer_norm_reverse(upstream, normalized_rows, inverse):
    first = jnp.mean(upstream, axis=-1, keepdims=True)
    second = jnp.mean(upstream * normalized_rows, axis=-1, keepdims=True)
    return inverse * (upstream - first - normalized_rows * second)


MESH = pl.DeviceIdType.MESH
ROWS_PAD = 48
HEAD_PAD = 96
OUT_ROWS_PAD = 32
OUT_COLS_PAD = 1536


def place():
    s, i = lax.axis_index("sp"), lax.axis_index("img")
    return s // 8, (s // 4) % 2, s % 4, i // 2, i % 2


def at_sp(x, zl, y):
    return {"sp": (x * 2 + zl) * 4 + y}


def greet(targets):
    barrier = pltpu.get_barrier_semaphore()
    for target in targets:
        pl.semaphore_signal(barrier, inc=1, device_id=target, device_id_type=MESH)
    pl.semaphore_wait(barrier, len(targets))


def one_hot(rows, per, block):
    r = lax.broadcasted_iota(jnp.int32, (block, 4 * rows), 0)
    c = lax.broadcasted_iota(jnp.int32, (block, 4 * rows), 1)
    skipped = jnp.zeros_like(r)
    for k in (1, 2, 3):
        skipped += jnp.where(r >= k * per, rows - per, 0)
    return jnp.where(c == r + skipped, 1.0, 0.0)


def gather_kernel(shapes, *refs):
    count = len(shapes)
    ins = refs[:3]
    y_one, second, cot, w_lateral, lat_gain, w_conv, conv_gain = refs[3:10]
    qkv_out, w_out_out, half_out, d_x1_out, dec_out, conv_out, lat_out = refs[10:17]
    deconv, *rest = refs[17:]
    outs = [deconv, qkv_out, w_out_out]
    shards, packs, rest = rest[:3], rest[3:6], rest[6:]
    feature, pixels, act, dconv, cot_low, cot_high, norm_lat, dup, *sems = rest
    send, recv, local, halo_send, halo_recv = sems
    x, zl, y, zh, core = place()
    s = lax.axis_index("sp")
    below, above = {"sp": (s + 1) % 32}, {"sp": (s + 31) % 32}
    xm, xp, xo = (x + 3) % 4, (x + 1) % 4, (x + 2) % 4
    left, right = at_sp(xm, zl, y), at_sp(xp, zl, y)
    across = (x * 2 + 1 - zl) * 4 + y
    up = {"img": ((zh + zl) % 4) * 2 + core, "sp": across}
    down = {"img": ((zh + zl + 3) % 4) * 2 + core, "sp": across}
    twin = {"img": zh * 2 + 1 - core}
    column = [at_sp(x, zl, (y + k) % 4) for k in (1, 2, 3)]
    greet(column + [left, right, up, down, twin, below, above])
    copies = {}

    def push(a, slot, src, dst, target):
        copy = pltpu.make_async_remote_copy(
            src_ref=src,
            dst_ref=dst,
            send_sem=send.at[a, slot],
            recv_sem=recv.at[a, slot],
            device_id=target,
            device_id_type=MESH,
        )
        copy.start()
        copies[a, slot] = copy

    def part(a):
        half = shapes[a][3] // 2
        return half, pl.multiple_of(core * half, 128)

    def region(a, bx, bz, lo, size):
        half, first = part(a)
        return outs[a].at[bx * 2 + bz, pl.ds(lo, size), pl.ds(first, half)]

    def forward(a, slot, bx, bz, lo, size, target):
        piece = region(a, bx, bz, lo, size)
        push(a, slot, piece, piece, target)

    for a in range(count):
        half, first = part(a)
        mine = ins[a].at[:, pl.ds(first, half)]
        for k in range(3):
            push(a, k, mine, shards[a].at[y], column[k])
        shards[a][y] = ins[a][:, pl.ds(first, half)]
    keeps = []
    for a in range(count):
        rows, per, block, _ = shapes[a]
        half, first = part(a)
        low = (block // 32) * 16
        high = block - low
        for k in range(3):
            copies[a, k].wait_recv()
        pick = one_hot(rows, per, block).astype(jnp.bfloat16)
        packs[a][...] = jnp.dot(
            pick, shards[a][...].reshape(4 * rows, half), preferred_element_type=jnp.float32
        ).astype(jnp.bfloat16)
        own, whole = packs[a], region(a, x, zl, 0, block)
        keep = pltpu.make_async_copy(own, whole, local.at[a])
        keep.start()
        keeps.append(keep)
        push(a, 3, own, whole, right)
        push(a, 4, own, whole, left)
        push(a, 7, own.at[pl.ds(0, low)], region(a, x, zl, 0, low), up)
        push(a, 8, own.at[pl.ds(low, high)], region(a, x, zl, low, high), down)
        push(a, 15, own, whole, twin)

    def near(a):
        block = shapes[a][2]
        low = (block // 32) * 16
        high = block - low
        copies[a, 3].wait_recv()
        forward(a, 5, xm, zl, 0, low, right)
        forward(a, 9, xm, zl, 0, low, up)
        forward(a, 10, xm, zl, low, high, down)
        forward(a, 16, xm, zl, 0, block, twin)
        copies[a, 4].wait_recv()
        forward(a, 6, xp, zl, low, high, left)
        forward(a, 11, xp, zl, 0, low, up)
        forward(a, 12, xp, zl, low, high, down)
        forward(a, 17, xp, zl, 0, block, twin)

    def far(a):
        block = shapes[a][2]
        low = (block // 32) * 16
        high = block - low
        copies[a, 5].wait_recv()
        forward(a, 13, xo, zl, 0, low, up)
        forward(a, 18, xo, zl, 0, low, twin)
        copies[a, 6].wait_recv()
        forward(a, 14, xo, zl, low, high, down)
        forward(a, 19, xo, zl, low, high, twin)

    def deep(a):
        block = shapes[a][2]
        low = (block // 32) * 16
        high = block - low
        for n, bx in enumerate((x, xm, xp, xo)):
            copies[a, 7 + 2 * n].wait_recv()
            forward(a, 20 + 2 * n, bx, 1 - zl, 0, low, twin)
            copies[a, 8 + 2 * n].wait_recv()
            forward(a, 21 + 2 * n, bx, 1 - zl, low, high, twin)

    def twins(a):
        for slot in range(15, 28):
            copies[a, slot].wait_recv()

    row = GRID_W
    inner_rows = 4 * row
    halos = {}

    def swap_edges(ref, first):
        ends = (
            (first, pl.ds(inner_rows, row), pl.ds(0, row), below),
            (first + 1, pl.ds(row, row), pl.ds(inner_rows + row, row), above),
        )
        for slot, src_rows, dst_rows, target in ends:
            copy = pltpu.make_async_remote_copy(
                src_ref=ref.at[pl.ds(1, 2), src_rows],
                dst_ref=ref.at[pl.ds(1, 2), dst_rows],
                send_sem=halo_send.at[slot],
                recv_sem=halo_recv.at[slot],
                device_id=target,
                device_id_type=MESH,
            )
            copy.start()
            halos[slot] = copy

    def fill_sides(ref, first):
        halos[first].wait_recv()
        halos[first + 1].wait_recv()
        for b in (1, 2):
            head, tail = pl.ds(0, row), pl.ds(inner_rows + row, row)
            ref[b, head] = jnp.where(s == 0, 0.0, ref[b, head].astype(jnp.float32)).astype(
                jnp.bfloat16
            )
            ref[b, tail] = jnp.where(s == 31, 0.0, ref[b, tail].astype(jnp.float32)).astype(
                jnp.bfloat16
            )
        rows = ref.shape[1]
        at = lax.broadcasted_iota(jnp.int32, (rows, LAT), 0) % row
        moved = pltpu.roll(ref[2].astype(jnp.float32), 1, 0)
        ref[0] = jnp.where(at == 0, 0.0, moved).astype(jnp.bfloat16)
        moved = pltpu.roll(ref[1].astype(jnp.float32), rows - 1, 0)
        ref[3] = jnp.where(at == row - 1, 0.0, moved).astype(jnp.bfloat16)

    def taps():
        return [(i, j) for i in range(3) for j in range(3)]

    def upward():
        feature[...] = ((y_one[...].astype(jnp.float32) + second[...].astype(jnp.float32)) * 0.5).astype(
            jnp.bfloat16
        )
        wide = cot[...].reshape(8 * row, LAT).astype(jnp.float32)
        cot_low[...] = wide[:, : LAT // 2]
        cot_high[...] = wide[:, LAT // 2 :]
        depth = deconv.shape[0] * deconv.shape[1]
        for ab in range(4):
            plane = pl.ds(ab * DEC, DEC)
            up = jnp.dot(
                feature[...],
                deconv[:, :, plane].reshape(depth, DEC),
                preferred_element_type=jnp.float32,
            ).astype(jnp.bfloat16)
            for r in range(2):
                pixels[pl.ds((ab % 2) * inner_rows + (2 * r + ab // 2) * row, row)] = up[
                    r * row : (r + 1) * row
                ]
        lat = jnp.dot(pixels[...], w_lateral[...], preferred_element_type=jnp.float32)
        lhat, linv = apply_layer_norm(lat)
        norm_lat[...] = lhat
        scaled = (lhat * lat_gain[...]).astype(jnp.bfloat16)
        for b in range(2):
            act[1 + b, pl.ds(row, inner_rows)] = scaled[b * inner_rows : (b + 1) * inner_rows]
        swap_edges(act, 0)
        return linv

    def convolve():
        fill_sides(act, 0)
        for b in range(2):
            total = jnp.zeros((inner_rows, LAT), jnp.float32)
            for i, j in taps():
                total += jnp.dot(
                    act[b + j, pl.ds(i * row, inner_rows)],
                    w_conv[3 * i + j],
                    preferred_element_type=jnp.float32,
                )
            chat, cinv = apply_layer_norm(total)
            every = pl.ds(b, inner_rows, stride=2)
            upstream = jnp.concatenate([cot_low[every, :], cot_high[every, :]], axis=1)
            upstream = upstream * conv_gain[...]
            dconv[1 + b, pl.ds(row, inner_rows)] = layer_norm_reverse(upstream, chat, cinv).astype(
                jnp.bfloat16
            )
        swap_edges(dconv, 2)

    def downward(linv):
        fill_sides(dconv, 2)
        for b in range(2):
            total = jnp.zeros((inner_rows, LAT), jnp.float32)
            for i, j in taps():
                total += lax.dot_general(
                    dconv[b - j + 2, pl.ds((2 - i) * row, inner_rows)],
                    w_conv[3 * i + j],
                    (((1,), (1,)), ((), ())),
                    preferred_element_type=jnp.float32,
                )
            here = slice(b * inner_rows, (b + 1) * inner_rows)
            dlat = layer_norm_reverse(
                total * lat_gain[...], norm_lat[pl.ds(b * inner_rows, inner_rows)], linv[here]
            ).astype(jnp.bfloat16)
            term = jnp.dot(
                pixels[pl.ds(b * inner_rows, inner_rows)].astype(jnp.float32).T.astype(jnp.bfloat16),
                dlat,
                preferred_element_type=jnp.float32,
            )
            lat_term = term if b == 0 else lat_term + term
            dpixels = lax.dot_general(
                dlat, w_lateral[...], (((1,), (1,)), ((), ())), preferred_element_type=jnp.float32
            ).astype(jnp.bfloat16)
            for line in range(4):
                r, a = line // 2, line % 2
                dup[pl.ds(r * row, row), pl.ds((2 * a + b) * DEC, DEC)] = dpixels[
                    line * row : (line + 1) * row
                ]
        lat_out[...] = (lat_term * grad_scale).astype(jnp.bfloat16)
        depth = deconv.shape[0] * deconv.shape[1]
        half = 0.5 * lax.dot_general(
            dup[...],
            deconv[...].reshape(depth, 4 * DEC),
            (((1,), (1,)), ((), ())),
            preferred_element_type=jnp.float32,
        )
        half_out[...] = half
        d_x1_out[...] = half.astype(jnp.bfloat16)

    def conv_term():
        turned_grads = [
            dconv[1 + b, pl.ds(row, inner_rows)].astype(jnp.float32).T.astype(jnp.bfloat16)
            for b in range(2)
        ]
        for i, j in taps():
            total = jnp.zeros((LAT, LAT), jnp.float32)
            for b in range(2):
                total += jnp.dot(
                    turned_grads[b],
                    act[b + j, pl.ds(i * row, inner_rows)],
                    preferred_element_type=jnp.float32,
                )
            conv_out[:, pl.ds((3 * i + j) * LAT, LAT)] = (total.T * grad_scale).astype(jnp.bfloat16)

    def deconv_term():
        rows, per, block, _ = shapes[0]
        wide = feature[...].astype(jnp.float32).T
        pick = one_hot(rows, per, block).T.astype(jnp.bfloat16)
        for g in range(8):
            group = jnp.dot(
                pick,
                wide[g * block : (g + 1) * block].astype(jnp.bfloat16),
                preferred_element_type=jnp.float32,
            ).astype(jnp.bfloat16)
            term = jnp.dot(group, dup[...], preferred_element_type=jnp.float32) * grad_scale
            dec_out[pl.ds(g * 4 * rows, 4 * rows)] = term.astype(jnp.bfloat16)

    near(0)
    near(1)
    far(0)
    deep(0)
    twins(0)
    keeps[0].wait()
    linv = upward()
    far(1)
    near(2)
    convolve()
    far(2)
    downward(linv)
    deep(1)
    conv_term()
    deep(2)
    deconv_term()
    twins(1)
    twins(2)
    for keep in keeps[1:]:
        keep.wait()
    for copy in list(copies.values()) + list(halos.values()):
        copy.wait_send()


def gather_and_pyramid(shards, pers, *others):
    count = len(shards)
    shapes = []
    for shard, per in zip(shards, pers):
        block = -(-4 * per // 16) * 16
        shapes.append((shard.shape[0], per, block, shard.shape[1]))
    halves = [(rows, block, width // 2) for rows, _, block, width in shapes]
    tokens, features = others[0].shape
    bf16, f32 = jnp.bfloat16, jnp.float32
    full = [jax.ShapeDtypeStruct((8, block, width), bf16) for _, _, block, width in shapes]
    pixel_count = 4 * tokens
    return pl.pallas_call(
        functools.partial(gather_kernel, shapes),
        out_shape=full[1:]
        + [
            jax.ShapeDtypeStruct((tokens, features), f32),
            jax.ShapeDtypeStruct((tokens, features), bf16),
            jax.ShapeDtypeStruct((32 * ROWS_PAD, 4 * DEC), bf16),
            jax.ShapeDtypeStruct((LAT, 9 * LAT), bf16),
            jax.ShapeDtypeStruct((DEC, LAT), bf16),
        ],
        in_specs=[pl.BlockSpec(memory_space=pltpu.VMEM)] * (count + len(others)),
        out_specs=[pl.BlockSpec(memory_space=pl.ANY)] * (count - 1)
        + [pl.BlockSpec(memory_space=pltpu.VMEM)] * 5,
        scratch_shapes=[pltpu.VMEM(full[0].shape, bf16)]
        + [pltpu.VMEM((4, rows, half), bf16) for rows, _, half in halves]
        + [pltpu.VMEM((block, half), bf16) for _, block, half in halves]
        + [
            pltpu.VMEM((tokens, features), bf16),
            pltpu.VMEM((pixel_count, DEC), bf16),
            pltpu.VMEM((4, 6 * GRID_W, LAT), bf16),
            pltpu.VMEM((4, 6 * GRID_W, LAT), bf16),
            pltpu.VMEM((pixel_count, LAT // 2), f32),
            pltpu.VMEM((pixel_count, LAT // 2), f32),
            pltpu.VMEM((pixel_count, LAT), f32),
            pltpu.VMEM((tokens, 4 * DEC), bf16),
            pltpu.SemaphoreType.DMA((count, 28)),
            pltpu.SemaphoreType.DMA((count, 28)),
            pltpu.SemaphoreType.DMA((count,)),
            pltpu.SemaphoreType.DMA((4,)),
            pltpu.SemaphoreType.DMA((4,)),
        ],
        compiler_params=pltpu.CompilerParams(
            collective_id=0, has_side_effects=True, vmem_limit_bytes=56 * 2**20
        ),
    )(*shards, *others)


AXES = {"x": 4, "z": 2, "y": 4}


def leads(order):
    left = list(AXES)
    sizes = []
    for axis in order:
        left = [name for name in left if name != axis]
        sizes.append([AXES[name] for name in left])
    return sizes


class Scatter:
    def __init__(self, plan, parts, buffers, send, recv, local):
        self.plan, self.parts = plan, parts
        self.land = [buffers[0], buffers[2], buffers[4]]
        self.sums = [buffers[1], buffers[3]]
        self.send, self.recv, self.local = send, recv, local
        x, zl, y, _, _ = place()
        self.me = {"x": x, "z": zl, "y": y}
        self.peers = {
            "x": [(x + k) % 4 for k in (1, 2, 3)],
            "y": [(y + k) % 4 for k in (1, 2, 3)],
            "z": [1 - zl],
        }
        self.copies, self.own = {}, {}

    def take(self, n, step, view, where):
        order = self.plan[n][3]
        left = [name for name in AXES if name not in order[:step]]
        lead = [slice(None)] * left.index(order[step])
        return view.at[(*lead, where)]

    def ship(self, n, step, view):
        axis = self.plan[n][3][step]
        for k, peer in enumerate(self.peers[axis]):
            at = dict(self.me)
            at[axis] = peer
            copy = pltpu.make_async_remote_copy(
                src_ref=self.take(n, step, view, peer),
                dst_ref=self.land[step][n].at[k],
                send_sem=self.send.at[n, 3 * step + k],
                recv_sem=self.recv.at[n, 3 * step + k],
                device_id=at_sp(at["x"], at["z"], at["y"]),
                device_id_type=MESH,
            )
            copy.start()
            self.copies[n, step, k] = copy

    def arrived(self, n, step):
        count = len(self.peers[self.plan[n][3][step]])
        for k in range(count):
            self.copies[n, step, k].wait_recv()
        return count

    def start(self, n):
        source, first, width, order = self.plan[n]
        view = self.parts[source].at[:, :, :, :, pl.ds(first, width)]
        own = self.take(n, 0, view, self.me[order[0]])
        self.own[n] = pltpu.make_async_copy(own, self.sums[0][n], self.local.at[n])
        self.own[n].start()
        self.ship(n, 0, view)

    def second(self, n):
        sums, land = self.sums[0][n], self.land[0][n]
        self.own[n].wait()
        count = self.arrived(n, 0)
        outer, inner = sums.shape[:2]

        def add(t, carry):
            p, q = t // inner, t % inner
            total = sums[p, q].astype(jnp.float32)
            for k in range(count):
                total += land[k, p, q].astype(jnp.float32)
            sums[p, q] = total.astype(jnp.bfloat16)
            return carry

        lax.fori_loop(0, outer * inner, add, 0)
        self.ship(n, 1, sums)

    def third(self, n):
        land, sums = self.land[1][n], self.sums[1][n]
        order = self.plan[n][3]
        count = self.arrived(n, 1)
        own = self.take(n, 1, self.sums[0][n], self.me[order[1]])
        for p in range(sums.shape[0]):
            total = own[p].astype(jnp.float32)
            for k in range(count):
                total += land[k, p].astype(jnp.float32)
            sums[p] = total.astype(jnp.bfloat16)
        self.ship(n, 2, sums)

    def finish(self, n, out):
        count = self.arrived(n, 2)
        total = self.sums[1][n][self.me[self.plan[n][3][2]]].astype(jnp.float32)
        for k in range(count):
            total += self.land[2][n][k].astype(jnp.float32)
        out[...] = total

    def settle(self):
        for copy in self.copies.values():
            copy.wait_send()


def scatter_buffers(plan, rows):
    groups = [[], [], [], [], []]
    for source, _, width, order in plan:
        sizes = leads(order)
        for step in range(3):
            peers = AXES[order[step]] - 1
            tail = (rows[source], width)
            groups[2 * step].append(pltpu.VMEM((peers, *sizes[step], *tail), jnp.bfloat16))
            if step < 2:
                groups[2 * step + 1].append(pltpu.VMEM((*sizes[step], *tail), jnp.bfloat16))
    return groups


TILE = 128
QUERY_BLOCK = 512
KEY_BLOCK = 1024


def turned(block):
    wide = block.astype(jnp.float32)
    zeros = jnp.zeros((TILE - HEAD_PAD, TILE), jnp.float32)
    return jnp.concatenate([wide, zeros], axis=0).T


def head_rows(block):
    return block.T[:HEAD_PAD].astype(jnp.bfloat16)


SUM_PLAN = [
    (0, 0, 2 * DEC, "xyz"),
    (0, 2 * DEC, 2 * DEC, "zxy"),
    (1, 0, 9 * LAT, "zxy"),
    (2, 0, LAT, "zxy"),
    (3, 0, 1408, "yxz"),
]
OUT_ROWS = 22
OUT_ROWS_STEP = 24


def attention_kernel(proj, grad, d_x1, dec_part, conv_part, lat_part, *refs):
    attn_out, dqkv_out, *sum_outs = refs[:7]
    (
        q_in,
        g_in,
        kv_in,
        key_t,
        value_t,
        key,
        value,
        query,
        cot,
        query_t,
        cot_t,
        score,
        weight,
        inverse,
        offset,
        attended,
        o_send,
        dq_send,
        d_send,
        d_land,
        d_sum,
        o_land,
        d_res,
        out_part,
    ) = refs[7:31]
    groups = [refs[31 + 5 * k : 36 + 5 * k] for k in range(5)]
    send, recv, sum_send, sum_recv, sum_local = refs[56:]
    sums = Scatter(
        SUM_PLAN, [dec_part, conv_part, lat_part, out_part], groups, sum_send, sum_recv, sum_local
    )
    x, zl, y, zh, core = place()
    m = x * 2 + zl
    plane = [(m + k) % 8 for k in range(8)]
    source = [(m + 8 - k) % 8 for k in range(8)]
    column = [(y + k) % 4 for k in range(4)]

    def at_plane(k):
        return {"sp": plane[k] * 4 + y}

    def at_column(k):
        return {"sp": m * 4 + column[k]}

    greet([at_plane(k) for k in range(1, 8)] + [at_column(k) for k in range(1, 4)])
    copies = {}

    def push(slot, src, dst, target):
        copy = pltpu.make_async_remote_copy(
            src_ref=src,
            dst_ref=dst,
            send_sem=send.at[slot],
            recv_sem=recv.at[slot],
            device_id=target,
            device_id_type=MESH,
        )
        copy.start()
        copies[slot] = copy

    kv_at, q_at, g_at, ring_at, o_at, dq_at, back_at, home_at = 0, 8, 16, 24, 48, 56, 64, 72
    for k in range(1, 8):
        push(kv_at + k, proj.at[pl.ds(1, 2), plane[k]], kv_in.at[y, m], at_plane(k))
    kv_in[y, m, 0] = proj[1, m]
    kv_in[y, m, 1] = proj[2, m]
    q_in[m] = proj[0, m]
    g_in[m] = grad[m]

    def pass_on(k):
        piece = kv_in.at[y, source[k]]
        for j in range(1, 4):
            push(ring_at + 3 * k + j - 1, piece, piece, at_column(j))

    pass_on(0)
    for k in range(1, 8):
        push(q_at + k, proj.at[0, plane[k]], q_in.at[m], at_plane(k))
    for k in range(1, 8):
        copies[kv_at + k].wait_recv()
        pass_on(k)
    for k in range(1, 8):
        push(g_at + k, grad.at[plane[k]], g_in.at[m], at_plane(k))
    for n in (0, 1, 2, 3):
        sums.start(n)
    zero_rows = jnp.zeros((TILE - HEAD_PAD, key_t.shape[1]), jnp.bfloat16)
    key_t[HEAD_PAD:] = zero_rows
    value_t[HEAD_PAD:] = zero_rows

    def prepare(t, carry):
        at = pl.ds(pl.multiple_of(t * TILE, TILE), TILE)
        block = kv_in[t // 8, t % 8, 0]
        key_t[:HEAD_PAD, at] = block
        key[at, :] = turned(block).astype(jnp.bfloat16)
        block = kv_in[t // 8, t % 8, 1]
        value_t[:HEAD_PAD, at] = block
        value[at, :] = turned(block).astype(jnp.bfloat16)
        return carry

    def prepare_queries(t, carry):
        query[pl.ds(pl.multiple_of(t * TILE, TILE), TILE), :] = turned(q_in[t]).astype(jnp.bfloat16)
        return carry

    def prepare_cots(t, carry):
        cot[pl.ds(pl.multiple_of(t * TILE, TILE), TILE), :] = turned(g_in[t]).astype(jnp.bfloat16)
        return carry

    lax.fori_loop(y * 8, y * 8 + 8, prepare, 0)
    for k in range(1, 8):
        copies[q_at + k].wait_recv()
    lax.fori_loop(0, 8, prepare_queries, 0)
    for j in range(1, 4):
        for k in range(8):
            copies[ring_at + 3 * k + j - 1].wait_recv()
        first = ((y + 4 - j) % 4) * 8
        lax.fori_loop(first, first + 8, prepare, 0)
    for k in range(1, 8):
        copies[g_at + k].wait_recv()
    lax.fori_loop(0, 8, prepare_cots, 0)

    tokens = key.shape[0]
    queries = query.shape[0]
    blocks = [pl.ds(c * KEY_BLOCK, KEY_BLOCK) for c in range(tokens // KEY_BLOCK)]

    def forward(i, carry):
        at = pl.ds(pl.multiple_of(i * QUERY_BLOCK, QUERY_BLOCK), QUERY_BLOCK)
        top = jnp.full((QUERY_BLOCK, 1), -jnp.inf, jnp.float32)
        for block in blocks:
            part = jnp.dot(query[at, :], key_t[:, block], preferred_element_type=jnp.float32)
            score[:, block] = part
            top = jnp.maximum(top, jnp.max(part, axis=1, keepdims=True))
        total = jnp.zeros((QUERY_BLOCK, 1), jnp.float32)
        mixed = jnp.zeros((QUERY_BLOCK, TILE), jnp.float32)
        for block in blocks:
            part = jnp.exp(score[:, block] - top)
            total += jnp.sum(part, axis=1, keepdims=True)
            rounded = part.astype(jnp.bfloat16)
            weight[at, block] = rounded
            mixed += jnp.dot(rounded, value[block, :], preferred_element_type=jnp.float32)
        inv = 1.0 / total
        mixed = mixed * inv
        attended[at, :] = mixed
        inverse[at, :] = inv
        offset[at, :] = jnp.sum(mixed * cot[at, :].astype(jnp.float32), axis=1, keepdims=True)
        return carry

    lax.fori_loop(0, queries // QUERY_BLOCK, forward, 0)
    for t in range(8):
        at = pl.ds(t * TILE, TILE)
        o_send[t] = head_rows(attended[at, :])
    for k in range(1, 8):
        push(o_at + k, o_send.at[plane[k]], o_land.at[m], at_plane(k))
    o_land[m] = o_send[m]
    for t in range(8):
        at = pl.ds(t * TILE, TILE)
        inv = inverse[at, :]
        query_t[:, at] = (query[at, :].astype(jnp.float32) * inv).T.astype(jnp.bfloat16)
        cot_t[:, at] = (cot[at, :].astype(jnp.float32) * inv).T.astype(jnp.bfloat16)

    def key_side(left, kind):
        for j in (1, 2, 3, 0):
            yy = column[j]
            at = pl.ds(pl.multiple_of(yy * 8 * TILE, 8 * TILE), 8 * TILE)
            result = jnp.dot(left[...], weight[:, at], preferred_element_type=jnp.float32)
            for t in range(8):
                d_send[kind, j, t] = result[:HEAD_PAD, t * TILE : (t + 1) * TILE].astype(
                    jnp.bfloat16
                )
            if j:
                push(back_at + 4 * kind + j, d_send.at[kind, j], d_land.at[kind, j - 1], at_column(j))

    def key_home(kind):
        for j in range(1, 4):
            copies[back_at + 4 * kind + j].wait_recv()
        for t in range(8):
            total = d_send[kind, 0, t].astype(jnp.float32)
            for j in range(3):
                total += d_land[kind, j, t].astype(jnp.float32)
            d_sum[kind, t] = total.astype(jnp.bfloat16)
        for k in range(1, 8):
            push(
                home_at + 8 * kind + k,
                d_sum.at[kind, plane[k]],
                d_res.at[kind + 1, m],
                at_plane(k),
            )
        d_res[kind + 1, m] = d_sum[kind, m]

    key_side(cot_t, 1)
    for k in range(1, 8):
        copies[o_at + k].wait_recv()
    attn_out[...] = o_land[...]
    spread = 4 * OUT_ROWS_STEP
    r = lax.broadcasted_iota(jnp.int32, (spread, HEAD_PAD), 0)
    c = lax.broadcasted_iota(jnp.int32, (spread, HEAD_PAD), 1)
    picked = c < 0
    for k in range(4):
        low, first = k * OUT_ROWS, k * OUT_ROWS_STEP
        picked |= (c - low == r - first) & (c >= low) & (c < low + OUT_ROWS) & (r >= first)
    pick = jnp.where(picked, 1.0, 0.0).astype(jnp.bfloat16)
    for t in range(8):
        rows = jnp.dot(pick, o_land[t], preferred_element_type=jnp.float32).astype(jnp.bfloat16)
        term = jnp.dot(rows, d_x1[...], preferred_element_type=jnp.float32) * grad_scale
        for k in range(4):
            out_part[t // 2, t % 2, k] = term[
                k * OUT_ROWS_STEP : (k + 1) * OUT_ROWS_STEP
            ].astype(jnp.bfloat16)
    sums.start(4)

    def backward(i, carry):
        at = pl.ds(pl.multiple_of(i * QUERY_BLOCK, QUERY_BLOCK), QUERY_BLOCK)
        query_grad = jnp.zeros((QUERY_BLOCK, TILE), jnp.float32)
        shift = offset[at, :]
        for block in blocks:
            dprob = jnp.dot(cot[at, :], value_t[:, block], preferred_element_type=jnp.float32)
            dscore = (weight[at, block].astype(jnp.float32) * (dprob - shift)).astype(jnp.bfloat16)
            weight[at, block] = dscore
            query_grad += jnp.dot(dscore, key[block, :], preferred_element_type=jnp.float32)
        attended[at, :] = query_grad * (inverse[at, :] * HEAD ** (-0.5))
        return carry

    for i in range(queries // QUERY_BLOCK):
        backward(i, 0)
        if i == 0:
            key_home(1)
            sums.second(3)
            sums.second(2)
    key_side(query_t, 0)
    for t in range(8):
        dq_send[t] = head_rows(attended[pl.ds(t * TILE, TILE), :])
    for k in range(1, 8):
        push(dq_at + k, dq_send.at[plane[k]], d_res.at[0, m], at_plane(k))
    d_res[0, m] = dq_send[m]
    sums.second(0)
    sums.second(1)
    sums.third(3)
    sums.third(2)
    key_home(0)
    sums.second(4)
    for n in (0, 1, 4):
        sums.third(n)
    for first in (dq_at, home_at, home_at + 8):
        for k in range(1, 8):
            copies[first + k].wait_recv()
    dqkv_out[...] = d_res[...]
    for n in range(5):
        sums.finish(n, sum_outs[n])
    for copy in copies.values():
        copy.wait_send()
    sums.settle()


def attend_both_ways(proj, grad, d_x1, dec_part, conv_part, lat_part):
    rows = [part.shape[3] for part in (dec_part, conv_part, lat_part)] + [OUT_ROWS_STEP]
    groups = scatter_buffers(SUM_PLAN, rows)
    heads = grad.shape[0]
    tokens, queries = 32 * TILE, 8 * TILE
    bf16, f32 = jnp.bfloat16, jnp.float32
    block = (HEAD_PAD, TILE)
    shapes = [
        ((8, *block), bf16),
        ((8, *block), bf16),
        ((4, 8, 2, *block), bf16),
        ((TILE, tokens), bf16),
        ((TILE, tokens), bf16),
        ((tokens, TILE), bf16),
        ((tokens, TILE), bf16),
        ((queries, TILE), bf16),
        ((queries, TILE), bf16),
        ((TILE, queries), bf16),
        ((TILE, queries), bf16),
        ((QUERY_BLOCK, tokens), f32),
        ((queries, tokens), bf16),
        ((queries, 1), f32),
        ((queries, 1), f32),
        ((queries, TILE), f32),
        ((8, *block), bf16),
        ((8, *block), bf16),
        ((2, 4, 8, *block), bf16),
        ((2, 3, 8, *block), bf16),
        ((2, 8, *block), bf16),
        ((8, *block), bf16),
        ((3, 8, *block), bf16),
        ((4, 2, 4, OUT_ROWS_STEP, d_x1.shape[1]), bf16),
    ]
    sum_sems = pltpu.SemaphoreType.DMA((len(SUM_PLAN), 9))
    return pl.pallas_call(
        attention_kernel,
        out_shape=[
            jax.ShapeDtypeStruct((heads, *block), bf16),
            jax.ShapeDtypeStruct((3, heads, *block), bf16),
        ]
        + [jax.ShapeDtypeStruct((rows[source], width), f32) for source, _, width, _ in SUM_PLAN],
        in_specs=[pl.BlockSpec(memory_space=pltpu.VMEM)] * 3
        + [pl.BlockSpec(memory_space=pl.ANY)] * 3,
        out_specs=[pl.BlockSpec(memory_space=pltpu.VMEM)] * 7,
        scratch_shapes=[pltpu.VMEM(shape, kind) for shape, kind in shapes]
        + [buffer for group in groups for buffer in group]
        + [pltpu.SemaphoreType.DMA((88,)), pltpu.SemaphoreType.DMA((88,))]
        + [sum_sems, sum_sems, pltpu.SemaphoreType.DMA((len(SUM_PLAN),))],
        compiler_params=pltpu.CompilerParams(
            collective_id=2, has_side_effects=True, vmem_limit_bytes=56 * 2**20
        ),
    )(proj, grad, d_x1, dec_part, conv_part, lat_part)


def per_device(
    y_one,
    second_stream_state,
    cot,
    layer_norm_gain,
    w_qkv,
    w_out,
    w_deconv,
    w_lateral,
    lat_gain,
    w_conv,
    conv_gain,
):
    devices = lax.axis_size("sp")
    tokens_here = y_one.shape[0]
    score_scale = HEAD ** (-0.5)
    standardized_input, inverse_deviation = apply_layer_norm(
        second_stream_state.astype(jnp.float32)
    )
    normalized_rows = (standardized_input * layer_norm_gain).astype(jnp.bfloat16)
    depth, out_depth = w_qkv.shape[0], w_out.shape[0]
    qkv_shard = jnp.pad(
        w_qkv.reshape(depth, 3 * HEADS, HEAD),
        ((0, ROWS_PAD - depth), (0, 0), (0, HEAD_PAD - HEAD)),
    ).reshape(ROWS_PAD, 3 * HEADS * HEAD_PAD)
    out_shard = jnp.pad(
        w_out, ((0, OUT_ROWS_PAD - out_depth), (0, OUT_COLS_PAD - w_out.shape[1]))
    )
    deconv_shard = jnp.pad(w_deconv, ((0, ROWS_PAD - depth), (0, 0)))
    qkv_full, out_full, halfway_split, d_x1, dec_part, conv_part, lat_part = gather_and_pyramid(
        [deconv_shard, qkv_shard, out_shard],
        [depth, depth, out_depth],
        y_one,
        second_stream_state,
        cot,
        w_lateral,
        lat_gain[None],
        w_conv.reshape(9, LAT, LAT),
        conv_gain[None],
    )
    dec_part = dec_part.reshape(4, 2, 4, ROWS_PAD, 4 * DEC)
    conv_part = conv_part.reshape(4, 2, 4, LAT // devices, 9 * LAT)
    lat_rows = DEC // devices
    lat_part = jnp.pad(
        lat_part.reshape(devices, lat_rows, LAT), ((0, 0), (0, 16 - lat_rows), (0, 0))
    ).reshape(4, 2, 4, 16, LAT)
    qkv_full = qkv_full.reshape(devices * depth, -1)
    out_full = out_full.reshape(HEADS * HEAD_PAD, -1)[:, : w_out.shape[1]]
    dattn = lax.dot_general(
        out_full, d_x1, (((1,), (1,)), ((), ())), preferred_element_type=jnp.float32
    ).astype(jnp.bfloat16)
    projected = lax.optimization_barrier(
        jnp.dot(normalized_rows, qkv_full, preferred_element_type=jnp.float32)
    )
    projected = projected.T.reshape(3, HEADS, HEAD_PAD, tokens_here)
    scales = jnp.array([score_scale, 1.0, 1.0], jnp.float32).reshape(3, 1, 1, 1)
    projected = (projected * scales).astype(jnp.bfloat16)
    attn_heads, dqkv, dec_low, dec_high, conv_rows, lat_sums, out_rows = attend_both_ways(
        projected,
        dattn.reshape(HEADS, HEAD_PAD, tokens_here),
        d_x1,
        dec_part,
        conv_part,
        lat_part,
    )
    mixed = lax.dot_general(
        attn_heads.reshape(HEADS * HEAD_PAD, tokens_here),
        out_full,
        (((0,), (0,)), ((), ())),
        preferred_element_type=jnp.float32,
    )
    x_one = (y_one.astype(jnp.float32) - mixed).astype(jnp.bfloat16)
    normalized_gradient = lax.dot_general(
        dqkv.reshape(3 * HEADS * HEAD_PAD, tokens_here),
        qkv_full, (((0,), (1,)), ((), ())), preferred_element_type=jnp.float32
    )
    second_input_gradient = (
        halfway_split
        + layer_norm_reverse(
            normalized_gradient * layer_norm_gain, standardized_input, inverse_deviation
        )
    ).astype(jnp.bfloat16)
    g_deconv = jnp.concatenate([dec_low[:depth], dec_high[:depth]], axis=1)
    g_out = out_rows[:out_depth]
    g_lateral = lat_sums[:lat_rows]
    g_conv = conv_rows.reshape(conv_rows.shape[0], 3, 3, LAT).transpose(1, 2, 0, 3)
    return (x_one, d_x1, second_input_gradient, g_out, g_deconv, g_lateral, g_conv)


def solution(mesh):
    return jax.shard_map(
        per_device,
        mesh=mesh,
        in_specs=(
            P(("img", "sp"), None),
            P(("img", "sp"), None),
            P(("img", "sp"), None, None),
            P(),
            P("sp", None),
            P("sp", None),
            P("sp", None),
            P(),
            P(),
            P(),
            P(),
        ),
        out_specs=(
            P(("img", "sp"), None),
            P(("img", "sp"), None),
            P(("img", "sp"), None),
            P(("img", "sp"), None),
            P(("img", "sp"), None),
            P(("img", "sp"), None),
            P("img", None, "sp", None),
        ),
        check_vma=False,
    )
```

```python
import functools

import jax
import jax.numpy as jnp
from jax import lax
from jax.experimental import pallas as pl
from jax.experimental.pallas import tpu as pltpu
from jax.sharding import PartitionSpec as P

HEADS = 8
HEAD = 88
DEC = 384
LAT = 256
GRID_W = 64


epsilon = 1e-06
grad_scale = 0.015625


def apply_layer_norm(values):
    centered = values - jnp.mean(values, axis=-1, keepdims=True)
    inverse = lax.rsqrt(jnp.mean(centered * centered, axis=-1, keepdims=True) + epsilon)
    return (centered * inverse, inverse)


def layer_norm_reverse(upstream, normalized_rows, inverse):
    first = jnp.mean(upstream, axis=-1, keepdims=True)
    second = jnp.mean(upstream * normalized_rows, axis=-1, keepdims=True)
    return inverse * (upstream - first - normalized_rows * second)


MESH = pl.DeviceIdType.MESH
ROWS_PAD = 48
HEAD_PAD = 96
OUT_ROWS_PAD = 32
OUT_COLS_PAD = 1536


def place():
    s, i = lax.axis_index("sp"), lax.axis_index("img")
    return s // 8, (s // 4) % 2, s % 4, i // 2, i % 2


def at_sp(x, zl, y):
    return {"sp": (x * 2 + zl) * 4 + y}


def greet(targets):
    barrier = pltpu.get_barrier_semaphore()
    for target in targets:
        pl.semaphore_signal(barrier, inc=1, device_id=target, device_id_type=MESH)
    pl.semaphore_wait(barrier, len(targets))


def one_hot(rows, per, block):
    r = lax.broadcasted_iota(jnp.int32, (block, 4 * rows), 0)
    c = lax.broadcasted_iota(jnp.int32, (block, 4 * rows), 1)
    skipped = jnp.zeros_like(r)
    for k in (1, 2, 3):
        skipped += jnp.where(r >= k * per, rows - per, 0)
    return jnp.where(c == r + skipped, 1.0, 0.0)


def gather_kernel(shapes, *refs):
    count = len(shapes)
    ins = refs[:3]
    y_one, second, cot, w_lateral, lat_gain, w_conv, conv_gain = refs[3:10]
    qkv_out, w_out_out, half_out, d_x1_out, dec_out, conv_out, lat_out = refs[10:17]
    deconv, *rest = refs[17:]
    outs = [deconv, qkv_out, w_out_out]
    shards, packs, rest = rest[:3], rest[3:6], rest[6:]
    feature, pixels, act, dconv, cot_low, cot_high, norm_lat, dup, *sems = rest
    send, recv, local, halo_send, halo_recv = sems
    x, zl, y, zh, core = place()
    s = lax.axis_index("sp")
    below, above = {"sp": (s + 1) % 32}, {"sp": (s + 31) % 32}
    xm, xp, xo = (x + 3) % 4, (x + 1) % 4, (x + 2) % 4
    left, right = at_sp(xm, zl, y), at_sp(xp, zl, y)
    across = (x * 2 + 1 - zl) * 4 + y
    up = {"img": ((zh + zl) % 4) * 2 + core, "sp": across}
    down = {"img": ((zh + zl + 3) % 4) * 2 + core, "sp": across}
    twin = {"img": zh * 2 + 1 - core}
    column = [at_sp(x, zl, (y + k) % 4) for k in (1, 2, 3)]
    greet(column + [left, right, up, down, twin, below, above])
    copies = {}

    def push(a, slot, src, dst, target):
        copy = pltpu.make_async_remote_copy(
            src_ref=src,
            dst_ref=dst,
            send_sem=send.at[a, slot],
            recv_sem=recv.at[a, slot],
            device_id=target,
            device_id_type=MESH,
        )
        copy.start()
        copies[a, slot] = copy

    def part(a):
        half = shapes[a][3] // 2
        return half, pl.multiple_of(core * half, 128)

    def region(a, bx, bz, lo, size):
        half, first = part(a)
        return outs[a].at[bx * 2 + bz, pl.ds(lo, size), pl.ds(first, half)]

    def forward(a, slot, bx, bz, lo, size, target):
        piece = region(a, bx, bz, lo, size)
        push(a, slot, piece, piece, target)

    for a in range(count):
        half, first = part(a)
        mine = ins[a].at[:, pl.ds(first, half)]
        for k in range(3):
            push(a, k, mine, shards[a].at[y], column[k])
        shards[a][y] = ins[a][:, pl.ds(first, half)]
    keeps = {}

    def pack(a):
        rows, per, block, _ = shapes[a]
        half, first = part(a)
        low = (block // 32) * 16
        high = block - low
        for k in range(3):
            copies[a, k].wait_recv()
        pick = one_hot(rows, per, block).astype(jnp.bfloat16)
        packs[a][...] = jnp.dot(
            pick, shards[a][...].reshape(4 * rows, half), preferred_element_type=jnp.float32
        ).astype(jnp.bfloat16)
        own, whole = packs[a], region(a, x, zl, 0, block)
        keep = pltpu.make_async_copy(own, whole, local.at[a])
        keep.start()
        keeps[a] = keep
        push(a, 3, own, whole, right)
        push(a, 4, own, whole, left)
        push(a, 7, own.at[pl.ds(0, low)], region(a, x, zl, 0, low), up)
        push(a, 8, own.at[pl.ds(low, high)], region(a, x, zl, low, high), down)
        push(a, 15, own, whole, twin)

    def near(a):
        block = shapes[a][2]
        low = (block // 32) * 16
        high = block - low
        copies[a, 3].wait_recv()
        forward(a, 5, xm, zl, 0, low, right)
        forward(a, 9, xm, zl, 0, low, up)
        forward(a, 10, xm, zl, low, high, down)
        forward(a, 16, xm, zl, 0, block, twin)
        copies[a, 4].wait_recv()
        forward(a, 6, xp, zl, low, high, left)
        forward(a, 11, xp, zl, 0, low, up)
        forward(a, 12, xp, zl, low, high, down)
        forward(a, 17, xp, zl, 0, block, twin)

    def far(a):
        block = shapes[a][2]
        low = (block // 32) * 16
        high = block - low
        copies[a, 5].wait_recv()
        forward(a, 13, xo, zl, 0, low, up)
        forward(a, 18, xo, zl, 0, low, twin)
        copies[a, 6].wait_recv()
        forward(a, 14, xo, zl, low, high, down)
        forward(a, 19, xo, zl, low, high, twin)

    def deep(a):
        block = shapes[a][2]
        low = (block // 32) * 16
        high = block - low
        for n, bx in enumerate((x, xm, xp, xo)):
            copies[a, 7 + 2 * n].wait_recv()
            forward(a, 20 + 2 * n, bx, 1 - zl, 0, low, twin)
            copies[a, 8 + 2 * n].wait_recv()
            forward(a, 21 + 2 * n, bx, 1 - zl, low, high, twin)

    def twins(a):
        for slot in range(15, 28):
            copies[a, slot].wait_recv()

    row = GRID_W
    inner_rows = 4 * row
    halos = {}

    def swap_edges(ref, first):
        ends = (
            (first, pl.ds(inner_rows, row), pl.ds(0, row), below),
            (first + 1, pl.ds(row, row), pl.ds(inner_rows + row, row), above),
        )
        for slot, src_rows, dst_rows, target in ends:
            copy = pltpu.make_async_remote_copy(
                src_ref=ref.at[pl.ds(1, 2), src_rows],
                dst_ref=ref.at[pl.ds(1, 2), dst_rows],
                send_sem=halo_send.at[slot],
                recv_sem=halo_recv.at[slot],
                device_id=target,
                device_id_type=MESH,
            )
            copy.start()
            halos[slot] = copy

    def fill_sides(ref, first):
        halos[first].wait_recv()
        halos[first + 1].wait_recv()
        for b in (1, 2):
            head, tail = pl.ds(0, row), pl.ds(inner_rows + row, row)
            ref[b, head] = jnp.where(s == 0, 0.0, ref[b, head].astype(jnp.float32)).astype(
                jnp.bfloat16
            )
            ref[b, tail] = jnp.where(s == 31, 0.0, ref[b, tail].astype(jnp.float32)).astype(
                jnp.bfloat16
            )
        rows = ref.shape[1]
        at = lax.broadcasted_iota(jnp.int32, (rows, LAT), 0) % row
        moved = pltpu.roll(ref[2].astype(jnp.float32), 1, 0)
        ref[0] = jnp.where(at == 0, 0.0, moved).astype(jnp.bfloat16)
        moved = pltpu.roll(ref[1].astype(jnp.float32), rows - 1, 0)
        ref[3] = jnp.where(at == row - 1, 0.0, moved).astype(jnp.bfloat16)

    def taps():
        return [(i, j) for i in range(3) for j in range(3)]

    def upward():
        feature[...] = ((y_one[...].astype(jnp.float32) + second[...].astype(jnp.float32)) * 0.5).astype(
            jnp.bfloat16
        )
        wide = cot[...].reshape(8 * row, LAT).astype(jnp.float32)
        cot_low[...] = wide[:, : LAT // 2]
        cot_high[...] = wide[:, LAT // 2 :]
        depth = deconv.shape[0] * deconv.shape[1]
        for ab in range(4):
            plane = pl.ds(ab * DEC, DEC)
            up = jnp.dot(
                feature[...],
                deconv[:, :, plane].reshape(depth, DEC),
                preferred_element_type=jnp.float32,
            ).astype(jnp.bfloat16)
            for r in range(2):
                pixels[pl.ds((ab % 2) * inner_rows + (2 * r + ab // 2) * row, row)] = up[
                    r * row : (r + 1) * row
                ]
        lat = jnp.dot(pixels[...], w_lateral[...], preferred_element_type=jnp.float32)
        lhat, linv = apply_layer_norm(lat)
        norm_lat[...] = lhat
        scaled = (lhat * lat_gain[...]).astype(jnp.bfloat16)
        for b in range(2):
            act[1 + b, pl.ds(row, inner_rows)] = scaled[b * inner_rows : (b + 1) * inner_rows]
        swap_edges(act, 0)
        return linv

    def convolve():
        fill_sides(act, 0)
        for b in range(2):
            total = jnp.zeros((inner_rows, LAT), jnp.float32)
            for i, j in taps():
                total += jnp.dot(
                    act[b + j, pl.ds(i * row, inner_rows)],
                    w_conv[3 * i + j],
                    preferred_element_type=jnp.float32,
                )
            chat, cinv = apply_layer_norm(total)
            every = pl.ds(b, inner_rows, stride=2)
            upstream = jnp.concatenate([cot_low[every, :], cot_high[every, :]], axis=1)
            upstream = upstream * conv_gain[...]
            dconv[1 + b, pl.ds(row, inner_rows)] = layer_norm_reverse(upstream, chat, cinv).astype(
                jnp.bfloat16
            )
        swap_edges(dconv, 2)

    def downward(linv):
        fill_sides(dconv, 2)
        for b in range(2):
            total = jnp.zeros((inner_rows, LAT), jnp.float32)
            for i, j in taps():
                total += lax.dot_general(
                    dconv[b - j + 2, pl.ds((2 - i) * row, inner_rows)],
                    w_conv[3 * i + j],
                    (((1,), (1,)), ((), ())),
                    preferred_element_type=jnp.float32,
                )
            here = slice(b * inner_rows, (b + 1) * inner_rows)
            dlat = layer_norm_reverse(
                total * lat_gain[...], norm_lat[pl.ds(b * inner_rows, inner_rows)], linv[here]
            ).astype(jnp.bfloat16)
            term = jnp.dot(
                pixels[pl.ds(b * inner_rows, inner_rows)].astype(jnp.float32).T.astype(jnp.bfloat16),
                dlat,
                preferred_element_type=jnp.float32,
            )
            lat_term = term if b == 0 else lat_term + term
            dpixels = lax.dot_general(
                dlat, w_lateral[...], (((1,), (1,)), ((), ())), preferred_element_type=jnp.float32
            ).astype(jnp.bfloat16)
            for line in range(4):
                r, a = line // 2, line % 2
                dup[pl.ds(r * row, row), pl.ds((2 * a + b) * DEC, DEC)] = dpixels[
                    line * row : (line + 1) * row
                ]
        lat_out[...] = (lat_term * grad_scale).astype(jnp.bfloat16)
        depth = deconv.shape[0] * deconv.shape[1]
        half = 0.5 * lax.dot_general(
            dup[...],
            deconv[...].reshape(depth, 4 * DEC),
            (((1,), (1,)), ((), ())),
            preferred_element_type=jnp.float32,
        )
        half_out[...] = half
        d_x1_out[...] = half.astype(jnp.bfloat16)

    def conv_term():
        turned_grads = [
            dconv[1 + b, pl.ds(row, inner_rows)].astype(jnp.float32).T.astype(jnp.bfloat16)
            for b in range(2)
        ]
        for i, j in taps():
            total = jnp.zeros((LAT, LAT), jnp.float32)
            for b in range(2):
                total += jnp.dot(
                    turned_grads[b],
                    act[b + j, pl.ds(i * row, inner_rows)],
                    preferred_element_type=jnp.float32,
                )
            conv_out[:, pl.ds((3 * i + j) * LAT, LAT)] = (total.T * grad_scale).astype(jnp.bfloat16)

    def deconv_term():
        rows, per, block, _ = shapes[0]
        wide = feature[...].astype(jnp.float32).T
        pick = one_hot(rows, per, block).T.astype(jnp.bfloat16)
        for g in range(8):
            group = jnp.dot(
                pick,
                wide[g * block : (g + 1) * block].astype(jnp.bfloat16),
                preferred_element_type=jnp.float32,
            ).astype(jnp.bfloat16)
            term = jnp.dot(group, dup[...], preferred_element_type=jnp.float32) * grad_scale
            dec_out[pl.ds(g * 4 * rows, 4 * rows)] = term.astype(jnp.bfloat16)

    pack(0)
    near(0)
    pack(1)
    far(0)
    pack(2)
    near(1)
    deep(0)
    twins(0)
    keeps[0].wait()
    linv = upward()
    far(1)
    near(2)
    convolve()
    far(2)
    downward(linv)
    deep(1)
    conv_term()
    deep(2)
    deconv_term()
    twins(1)
    twins(2)
    for a in range(1, count):
        keeps[a].wait()
    for copy in list(copies.values()) + list(halos.values()):
        copy.wait_send()


def gather_and_pyramid(shards, pers, *others):
    count = len(shards)
    shapes = []
    for shard, per in zip(shards, pers):
        block = -(-4 * per // 16) * 16
        shapes.append((shard.shape[0], per, block, shard.shape[1]))
    halves = [(rows, block, width // 2) for rows, _, block, width in shapes]
    tokens, features = others[0].shape
    bf16, f32 = jnp.bfloat16, jnp.float32
    full = [jax.ShapeDtypeStruct((8, block, width), bf16) for _, _, block, width in shapes]
    pixel_count = 4 * tokens
    return pl.pallas_call(
        functools.partial(gather_kernel, shapes),
        out_shape=full[1:]
        + [
            jax.ShapeDtypeStruct((tokens, features), f32),
            jax.ShapeDtypeStruct((tokens, features), bf16),
            jax.ShapeDtypeStruct((32 * ROWS_PAD, 4 * DEC), bf16),
            jax.ShapeDtypeStruct((LAT, 9 * LAT), bf16),
            jax.ShapeDtypeStruct((DEC, LAT), bf16),
        ],
        in_specs=[pl.BlockSpec(memory_space=pltpu.VMEM)] * (count + len(others)),
        out_specs=[pl.BlockSpec(memory_space=pl.ANY)] * (count - 1)
        + [pl.BlockSpec(memory_space=pltpu.VMEM)] * 5,
        scratch_shapes=[pltpu.VMEM(full[0].shape, bf16)]
        + [pltpu.VMEM((4, rows, half), bf16) for rows, _, half in halves]
        + [pltpu.VMEM((block, half), bf16) for _, block, half in halves]
        + [
            pltpu.VMEM((tokens, features), bf16),
            pltpu.VMEM((pixel_count, DEC), bf16),
            pltpu.VMEM((4, 6 * GRID_W, LAT), bf16),
            pltpu.VMEM((4, 6 * GRID_W, LAT), bf16),
            pltpu.VMEM((pixel_count, LAT // 2), f32),
            pltpu.VMEM((pixel_count, LAT // 2), f32),
            pltpu.VMEM((pixel_count, LAT), f32),
            pltpu.VMEM((tokens, 4 * DEC), bf16),
            pltpu.SemaphoreType.DMA((count, 28)),
            pltpu.SemaphoreType.DMA((count, 28)),
            pltpu.SemaphoreType.DMA((count,)),
            pltpu.SemaphoreType.DMA((4,)),
            pltpu.SemaphoreType.DMA((4,)),
        ],
        compiler_params=pltpu.CompilerParams(
            collective_id=0, has_side_effects=True, vmem_limit_bytes=56 * 2**20
        ),
    )(*shards, *others)


AXES = {"x": 4, "z": 2, "y": 4}


def leads(order):
    left = list(AXES)
    sizes = []
    for axis in order:
        left = [name for name in left if name != axis]
        sizes.append([AXES[name] for name in left])
    return sizes


class Scatter:
    def __init__(self, plan, parts, buffers, send, recv, local):
        self.plan, self.parts = plan, parts
        self.land = [buffers[0], buffers[2], buffers[4]]
        self.sums = [buffers[1], buffers[3]]
        self.send, self.recv, self.local = send, recv, local
        x, zl, y, _, _ = place()
        self.me = {"x": x, "z": zl, "y": y}
        self.peers = {
            "x": [(x + k) % 4 for k in (1, 2, 3)],
            "y": [(y + k) % 4 for k in (1, 2, 3)],
            "z": [1 - zl],
        }
        self.copies, self.own = {}, {}

    def take(self, n, step, view, where):
        order = self.plan[n][3]
        left = [name for name in AXES if name not in order[:step]]
        lead = [slice(None)] * left.index(order[step])
        return view.at[(*lead, where)]

    def ship(self, n, step, view):
        axis = self.plan[n][3][step]
        for k, peer in enumerate(self.peers[axis]):
            at = dict(self.me)
            at[axis] = peer
            copy = pltpu.make_async_remote_copy(
                src_ref=self.take(n, step, view, peer),
                dst_ref=self.land[step][n].at[k],
                send_sem=self.send.at[n, 3 * step + k],
                recv_sem=self.recv.at[n, 3 * step + k],
                device_id=at_sp(at["x"], at["z"], at["y"]),
                device_id_type=MESH,
            )
            copy.start()
            self.copies[n, step, k] = copy

    def arrived(self, n, step):
        count = len(self.peers[self.plan[n][3][step]])
        for k in range(count):
            self.copies[n, step, k].wait_recv()
        return count

    def start(self, n):
        source, first, width, order = self.plan[n]
        view = self.parts[source].at[:, :, :, :, pl.ds(first, width)]
        own = self.take(n, 0, view, self.me[order[0]])
        self.own[n] = pltpu.make_async_copy(own, self.sums[0][n], self.local.at[n])
        self.own[n].start()
        self.ship(n, 0, view)

    def second(self, n):
        sums, land = self.sums[0][n], self.land[0][n]
        self.own[n].wait()
        count = self.arrived(n, 0)
        outer, inner = sums.shape[:2]

        def add(t, carry):
            p, q = t // inner, t % inner
            total = sums[p, q].astype(jnp.float32)
            for k in range(count):
                total += land[k, p, q].astype(jnp.float32)
            sums[p, q] = total.astype(jnp.bfloat16)
            return carry

        lax.fori_loop(0, outer * inner, add, 0)
        self.ship(n, 1, sums)

    def third(self, n):
        land, sums = self.land[1][n], self.sums[1][n]
        order = self.plan[n][3]
        count = self.arrived(n, 1)
        own = self.take(n, 1, self.sums[0][n], self.me[order[1]])
        for p in range(sums.shape[0]):
            total = own[p].astype(jnp.float32)
            for k in range(count):
                total += land[k, p].astype(jnp.float32)
            sums[p] = total.astype(jnp.bfloat16)
        self.ship(n, 2, sums)

    def finish(self, n, out):
        count = self.arrived(n, 2)
        total = self.sums[1][n][self.me[self.plan[n][3][2]]].astype(jnp.float32)
        for k in range(count):
            total += self.land[2][n][k].astype(jnp.float32)
        out[...] = total

    def settle(self):
        for copy in self.copies.values():
            copy.wait_send()


def scatter_buffers(plan, rows):
    groups = [[], [], [], [], []]
    for source, _, width, order in plan:
        sizes = leads(order)
        for step in range(3):
            peers = AXES[order[step]] - 1
            tail = (rows[source], width)
            groups[2 * step].append(pltpu.VMEM((peers, *sizes[step], *tail), jnp.bfloat16))
            if step < 2:
                groups[2 * step + 1].append(pltpu.VMEM((*sizes[step], *tail), jnp.bfloat16))
    return groups


TILE = 128
QUERY_BLOCK = 512
KEY_BLOCK = 1024


def turned(block):
    wide = block.astype(jnp.float32)
    zeros = jnp.zeros((TILE - HEAD_PAD, TILE), jnp.float32)
    return jnp.concatenate([wide, zeros], axis=0).T


def head_rows(block):
    return block.T[:HEAD_PAD].astype(jnp.bfloat16)


SUM_PLAN = [
    (0, 0, 2 * DEC, "xyz"),
    (0, 2 * DEC, 2 * DEC, "zxy"),
    (1, 0, 9 * LAT, "zxy"),
    (2, 0, LAT, "zxy"),
    (3, 0, 768, "yxz"),
    (3, 768, 640, "xyz"),
]
OUT_ROWS = 22
OUT_ROWS_STEP = 24


def attention_kernel(proj, grad, d_x1, dec_part, conv_part, lat_part, *refs):
    attn_out, dqkv_out, *sum_outs = refs[:8]
    (
        q_in,
        g_in,
        kv_in,
        key_t,
        value_t,
        key,
        value,
        query,
        cot,
        query_t,
        cot_t,
        score,
        weight,
        inverse,
        offset,
        attended,
        o_send,
        dq_send,
        d_send,
        d_land,
        d_sum,
        o_land,
        d_res,
        out_part,
    ) = refs[8:32]
    chunks = len(SUM_PLAN)
    groups = [refs[32 + chunks * k : 32 + chunks * (k + 1)] for k in range(5)]
    send, recv, sum_send, sum_recv, sum_local = refs[32 + 5 * chunks :]
    sums = Scatter(
        SUM_PLAN, [dec_part, conv_part, lat_part, out_part], groups, sum_send, sum_recv, sum_local
    )
    x, zl, y, zh, core = place()
    m = x * 2 + zl
    plane = [(m + k) % 8 for k in range(8)]
    source = [(m + 8 - k) % 8 for k in range(8)]
    column = [(y + k) % 4 for k in range(4)]

    def at_plane(k):
        return {"sp": plane[k] * 4 + y}

    def at_column(k):
        return {"sp": m * 4 + column[k]}

    greet([at_plane(k) for k in range(1, 8)] + [at_column(k) for k in range(1, 4)])
    copies = {}

    def push(slot, src, dst, target):
        copy = pltpu.make_async_remote_copy(
            src_ref=src,
            dst_ref=dst,
            send_sem=send.at[slot],
            recv_sem=recv.at[slot],
            device_id=target,
            device_id_type=MESH,
        )
        copy.start()
        copies[slot] = copy

    for n in (0, 1, 2, 3):
        sums.start(n)
    kv_at, q_at, g_at, ring_at, o_at, dq_at, back_at, home_at = 0, 8, 16, 24, 48, 56, 64, 72
    for k in range(1, 8):
        push(kv_at + k, proj.at[pl.ds(1, 2), plane[k]], kv_in.at[y, m], at_plane(k))
    kv_in[y, m, 0] = proj[1, m]
    kv_in[y, m, 1] = proj[2, m]
    q_in[m] = proj[0, m]
    g_in[m] = grad[m]

    def pass_on(k):
        piece = kv_in.at[y, source[k]]
        for j in range(1, 4):
            push(ring_at + 3 * k + j - 1, piece, piece, at_column(j))

    pass_on(0)
    for k in range(1, 8):
        push(q_at + k, proj.at[0, plane[k]], q_in.at[m], at_plane(k))
    for k in range(1, 8):
        copies[kv_at + k].wait_recv()
        pass_on(k)
    for k in range(1, 8):
        push(g_at + k, grad.at[plane[k]], g_in.at[m], at_plane(k))
    zero_rows = jnp.zeros((TILE - HEAD_PAD, key_t.shape[1]), jnp.bfloat16)
    key_t[HEAD_PAD:] = zero_rows
    value_t[HEAD_PAD:] = zero_rows

    def prepare(t, carry):
        at = pl.ds(pl.multiple_of(t * TILE, TILE), TILE)
        block = kv_in[t // 8, t % 8, 0]
        key_t[:HEAD_PAD, at] = block
        key[at, :] = turned(block).astype(jnp.bfloat16)
        block = kv_in[t // 8, t % 8, 1]
        value_t[:HEAD_PAD, at] = block
        value[at, :] = turned(block).astype(jnp.bfloat16)
        return carry

    def prepare_queries(t, carry):
        query[pl.ds(pl.multiple_of(t * TILE, TILE), TILE), :] = turned(q_in[t]).astype(jnp.bfloat16)
        return carry

    def prepare_cots(t, carry):
        cot[pl.ds(pl.multiple_of(t * TILE, TILE), TILE), :] = turned(g_in[t]).astype(jnp.bfloat16)
        return carry

    lax.fori_loop(y * 8, y * 8 + 8, prepare, 0)
    for k in range(1, 8):
        copies[q_at + k].wait_recv()
    lax.fori_loop(0, 8, prepare_queries, 0)
    for j in range(1, 4):
        for k in range(8):
            copies[ring_at + 3 * k + j - 1].wait_recv()
        first = ((y + 4 - j) % 4) * 8
        lax.fori_loop(first, first + 8, prepare, 0)
    for k in range(1, 8):
        copies[g_at + k].wait_recv()
    lax.fori_loop(0, 8, prepare_cots, 0)

    tokens = key.shape[0]
    queries = query.shape[0]
    blocks = [pl.ds(c * KEY_BLOCK, KEY_BLOCK) for c in range(tokens // KEY_BLOCK)]

    def forward(i, carry):
        at = pl.ds(pl.multiple_of(i * QUERY_BLOCK, QUERY_BLOCK), QUERY_BLOCK)
        top = jnp.full((QUERY_BLOCK, 1), -jnp.inf, jnp.float32)
        for block in blocks:
            part = jnp.dot(query[at, :], key_t[:, block], preferred_element_type=jnp.float32)
            score[:, block] = part
            top = jnp.maximum(top, jnp.max(part, axis=1, keepdims=True))
        total = jnp.zeros((QUERY_BLOCK, 1), jnp.float32)
        mixed = jnp.zeros((QUERY_BLOCK, TILE), jnp.float32)
        for block in blocks:
            part = jnp.exp(score[:, block] - top)
            total += jnp.sum(part, axis=1, keepdims=True)
            rounded = part.astype(jnp.bfloat16)
            weight[at, block] = rounded
            mixed += jnp.dot(rounded, value[block, :], preferred_element_type=jnp.float32)
        inv = 1.0 / total
        mixed = mixed * inv
        attended[at, :] = mixed
        inverse[at, :] = inv
        offset[at, :] = jnp.sum(mixed * cot[at, :].astype(jnp.float32), axis=1, keepdims=True)
        return carry

    for n in (3, 2, 0, 1):
        sums.second(n)
    lax.fori_loop(0, queries // QUERY_BLOCK, forward, 0)
    for t in range(8):
        at = pl.ds(t * TILE, TILE)
        o_send[t] = head_rows(attended[at, :])
    for k in range(1, 8):
        push(o_at + k, o_send.at[plane[k]], o_land.at[m], at_plane(k))
    o_land[m] = o_send[m]
    for t in range(8):
        at = pl.ds(t * TILE, TILE)
        inv = inverse[at, :]
        query_t[:, at] = (query[at, :].astype(jnp.float32) * inv).T.astype(jnp.bfloat16)
        cot_t[:, at] = (cot[at, :].astype(jnp.float32) * inv).T.astype(jnp.bfloat16)

    def key_side(left, kind):
        for j in (1, 2, 3, 0):
            yy = column[j]
            at = pl.ds(pl.multiple_of(yy * 8 * TILE, 8 * TILE), 8 * TILE)
            result = jnp.dot(left[...], weight[:, at], preferred_element_type=jnp.float32)
            for t in range(8):
                d_send[kind, j, t] = result[:HEAD_PAD, t * TILE : (t + 1) * TILE].astype(
                    jnp.bfloat16
                )
            if j:
                push(back_at + 4 * kind + j, d_send.at[kind, j], d_land.at[kind, j - 1], at_column(j))

    def key_home(kind):
        for j in range(1, 4):
            copies[back_at + 4 * kind + j].wait_recv()
        for t in range(8):
            total = d_send[kind, 0, t].astype(jnp.float32)
            for j in range(3):
                total += d_land[kind, j, t].astype(jnp.float32)
            d_sum[kind, t] = total.astype(jnp.bfloat16)
        for k in range(1, 8):
            push(
                home_at + 8 * kind + k,
                d_sum.at[kind, plane[k]],
                d_res.at[kind + 1, m],
                at_plane(k),
            )
        d_res[kind + 1, m] = d_sum[kind, m]

    key_side(cot_t, 1)
    for n in (3, 2, 0, 1):
        sums.third(n)
    for k in range(1, 8):
        copies[o_at + k].wait_recv()
    attn_out[...] = o_land[...]
    spread = 4 * OUT_ROWS_STEP
    r = lax.broadcasted_iota(jnp.int32, (spread, HEAD_PAD), 0)
    c = lax.broadcasted_iota(jnp.int32, (spread, HEAD_PAD), 1)
    picked = c < 0
    for k in range(4):
        low, first = k * OUT_ROWS, k * OUT_ROWS_STEP
        picked |= (c - low == r - first) & (c >= low) & (c < low + OUT_ROWS) & (r >= first)
    pick = jnp.where(picked, 1.0, 0.0).astype(jnp.bfloat16)
    for t in range(8):
        rows = jnp.dot(pick, o_land[t], preferred_element_type=jnp.float32).astype(jnp.bfloat16)
        term = jnp.dot(rows, d_x1[...], preferred_element_type=jnp.float32) * grad_scale
        for k in range(4):
            out_part[t // 2, t % 2, k] = term[
                k * OUT_ROWS_STEP : (k + 1) * OUT_ROWS_STEP
            ].astype(jnp.bfloat16)
    sums.start(4)
    sums.start(5)

    def backward(i, carry):
        at = pl.ds(pl.multiple_of(i * QUERY_BLOCK, QUERY_BLOCK), QUERY_BLOCK)
        query_grad = jnp.zeros((QUERY_BLOCK, TILE), jnp.float32)
        shift = offset[at, :]
        for block in blocks:
            dprob = jnp.dot(cot[at, :], value_t[:, block], preferred_element_type=jnp.float32)
            dscore = (weight[at, block].astype(jnp.float32) * (dprob - shift)).astype(jnp.bfloat16)
            weight[at, block] = dscore
            query_grad += jnp.dot(dscore, key[block, :], preferred_element_type=jnp.float32)
        attended[at, :] = query_grad * (inverse[at, :] * HEAD ** (-0.5))
        return carry

    for i in range(queries // QUERY_BLOCK):
        backward(i, 0)
        if i == 0:
            key_home(1)
    key_side(query_t, 0)
    for t in range(8):
        dq_send[t] = head_rows(attended[pl.ds(t * TILE, TILE), :])
    for k in range(1, 8):
        push(dq_at + k, dq_send.at[plane[k]], d_res.at[0, m], at_plane(k))
    d_res[0, m] = dq_send[m]
    sums.second(4)
    sums.second(5)
    key_home(0)
    sums.third(4)
    sums.third(5)
    for first in (dq_at, home_at, home_at + 8):
        for k in range(1, 8):
            copies[first + k].wait_recv()
    dqkv_out[...] = d_res[...]
    for n in range(chunks):
        sums.finish(n, sum_outs[n])
    for copy in copies.values():
        copy.wait_send()
    sums.settle()


def attend_both_ways(proj, grad, d_x1, dec_part, conv_part, lat_part):
    rows = [part.shape[3] for part in (dec_part, conv_part, lat_part)] + [OUT_ROWS_STEP]
    groups = scatter_buffers(SUM_PLAN, rows)
    heads = grad.shape[0]
    tokens, queries = 32 * TILE, 8 * TILE
    bf16, f32 = jnp.bfloat16, jnp.float32
    block = (HEAD_PAD, TILE)
    shapes = [
        ((8, *block), bf16),
        ((8, *block), bf16),
        ((4, 8, 2, *block), bf16),
        ((TILE, tokens), bf16),
        ((TILE, tokens), bf16),
        ((tokens, TILE), bf16),
        ((tokens, TILE), bf16),
        ((queries, TILE), bf16),
        ((queries, TILE), bf16),
        ((TILE, queries), bf16),
        ((TILE, queries), bf16),
        ((QUERY_BLOCK, tokens), f32),
        ((queries, tokens), bf16),
        ((queries, 1), f32),
        ((queries, 1), f32),
        ((queries, TILE), f32),
        ((8, *block), bf16),
        ((8, *block), bf16),
        ((2, 4, 8, *block), bf16),
        ((2, 3, 8, *block), bf16),
        ((2, 8, *block), bf16),
        ((8, *block), bf16),
        ((3, 8, *block), bf16),
        ((4, 2, 4, OUT_ROWS_STEP, d_x1.shape[1]), bf16),
    ]
    sum_sems = pltpu.SemaphoreType.DMA((len(SUM_PLAN), 9))
    return pl.pallas_call(
        attention_kernel,
        out_shape=[
            jax.ShapeDtypeStruct((heads, *block), bf16),
            jax.ShapeDtypeStruct((3, heads, *block), bf16),
        ]
        + [jax.ShapeDtypeStruct((rows[source], width), f32) for source, _, width, _ in SUM_PLAN],
        in_specs=[pl.BlockSpec(memory_space=pltpu.VMEM)] * 3
        + [pl.BlockSpec(memory_space=pl.ANY)] * 3,
        out_specs=[pl.BlockSpec(memory_space=pltpu.VMEM)] * 8,
        scratch_shapes=[pltpu.VMEM(shape, kind) for shape, kind in shapes]
        + [buffer for group in groups for buffer in group]
        + [pltpu.SemaphoreType.DMA((88,)), pltpu.SemaphoreType.DMA((88,))]
        + [sum_sems, sum_sems, pltpu.SemaphoreType.DMA((len(SUM_PLAN),))],
        compiler_params=pltpu.CompilerParams(
            collective_id=2, has_side_effects=True, vmem_limit_bytes=56 * 2**20
        ),
    )(proj, grad, d_x1, dec_part, conv_part, lat_part)


def per_device(
    y_one,
    second_stream_state,
    cot,
    layer_norm_gain,
    w_qkv,
    w_out,
    w_deconv,
    w_lateral,
    lat_gain,
    w_conv,
    conv_gain,
):
    devices = lax.axis_size("sp")
    tokens_here = y_one.shape[0]
    score_scale = HEAD ** (-0.5)
    standardized_input, inverse_deviation = apply_layer_norm(
        second_stream_state.astype(jnp.float32)
    )
    normalized_rows = (standardized_input * layer_norm_gain).astype(jnp.bfloat16)
    depth, out_depth = w_qkv.shape[0], w_out.shape[0]
    qkv_shard = jnp.pad(
        w_qkv.reshape(depth, 3 * HEADS, HEAD),
        ((0, ROWS_PAD - depth), (0, 0), (0, HEAD_PAD - HEAD)),
    ).reshape(ROWS_PAD, 3 * HEADS * HEAD_PAD)
    out_shard = jnp.pad(
        w_out, ((0, OUT_ROWS_PAD - out_depth), (0, OUT_COLS_PAD - w_out.shape[1]))
    )
    deconv_shard = jnp.pad(w_deconv, ((0, ROWS_PAD - depth), (0, 0)))
    qkv_full, out_full, halfway_split, d_x1, dec_part, conv_part, lat_part = gather_and_pyramid(
        [deconv_shard, qkv_shard, out_shard],
        [depth, depth, out_depth],
        y_one,
        second_stream_state,
        cot,
        w_lateral,
        lat_gain[None],
        w_conv.reshape(9, LAT, LAT),
        conv_gain[None],
    )
    dec_part = dec_part.reshape(4, 2, 4, ROWS_PAD, 4 * DEC)
    conv_part = conv_part.reshape(4, 2, 4, LAT // devices, 9 * LAT)
    lat_rows = DEC // devices
    lat_part = jnp.pad(
        lat_part.reshape(devices, lat_rows, LAT), ((0, 0), (0, 16 - lat_rows), (0, 0))
    ).reshape(4, 2, 4, 16, LAT)
    qkv_full = qkv_full.reshape(devices * depth, -1)
    out_full = out_full.reshape(HEADS * HEAD_PAD, -1)[:, : w_out.shape[1]]
    dattn = lax.dot_general(
        out_full, d_x1, (((1,), (1,)), ((), ())), preferred_element_type=jnp.float32
    ).astype(jnp.bfloat16)
    projected = lax.optimization_barrier(
        jnp.dot(normalized_rows, qkv_full, preferred_element_type=jnp.float32)
    )
    projected = projected.T.reshape(3, HEADS, HEAD_PAD, tokens_here)
    scales = jnp.array([score_scale, 1.0, 1.0], jnp.float32).reshape(3, 1, 1, 1)
    projected = (projected * scales).astype(jnp.bfloat16)
    attn_heads, dqkv, *summed = attend_both_ways(
        projected,
        dattn.reshape(HEADS, HEAD_PAD, tokens_here),
        d_x1,
        dec_part,
        conv_part,
        lat_part,
    )
    dec_low, dec_high, conv_rows, lat_sums, out_low, out_high = summed
    mixed = lax.dot_general(
        attn_heads.reshape(HEADS * HEAD_PAD, tokens_here),
        out_full,
        (((0,), (0,)), ((), ())),
        preferred_element_type=jnp.float32,
    )
    x_one = (y_one.astype(jnp.float32) - mixed).astype(jnp.bfloat16)
    normalized_gradient = lax.dot_general(
        dqkv.reshape(3 * HEADS * HEAD_PAD, tokens_here),
        qkv_full, (((0,), (1,)), ((), ())), preferred_element_type=jnp.float32
    )
    second_input_gradient = (
        halfway_split
        + layer_norm_reverse(
            normalized_gradient * layer_norm_gain, standardized_input, inverse_deviation
        )
    ).astype(jnp.bfloat16)
    g_deconv = jnp.concatenate([dec_low[:depth], dec_high[:depth]], axis=1)
    g_out = jnp.concatenate([out_low[:out_depth], out_high[:out_depth]], axis=1)
    g_lateral = lat_sums[:lat_rows]
    g_conv = conv_rows.reshape(conv_rows.shape[0], 3, 3, LAT).transpose(1, 2, 0, 3)
    return (x_one, d_x1, second_input_gradient, g_out, g_deconv, g_lateral, g_conv)


def solution(mesh):
    return jax.shard_map(
        per_device,
        mesh=mesh,
        in_specs=(
            P(("img", "sp"), None),
            P(("img", "sp"), None),
            P(("img", "sp"), None, None),
            P(),
            P("sp", None),
            P("sp", None),
            P("sp", None),
            P(),
            P(),
            P(),
            P(),
        ),
        out_specs=(
            P(("img", "sp"), None),
            P(("img", "sp"), None),
            P(("img", "sp"), None),
            P(("img", "sp"), None),
            P(("img", "sp"), None),
            P(("img", "sp"), None),
            P("img", None, "sp", None),
        ),
        check_vma=False,
    )
```

```python
import functools

import jax
import jax.numpy as jnp
from jax import lax
from jax.experimental import pallas as pl
from jax.experimental.pallas import tpu as pltpu
from jax.sharding import PartitionSpec as P

HEADS = 8
HEAD = 88
DEC = 384
LAT = 256
GRID_W = 64


epsilon = 1e-06
grad_scale = 0.015625


def apply_layer_norm(values):
    centered = values - jnp.mean(values, axis=-1, keepdims=True)
    inverse = lax.rsqrt(jnp.mean(centered * centered, axis=-1, keepdims=True) + epsilon)
    return (centered * inverse, inverse)


def layer_norm_reverse(upstream, normalized_rows, inverse):
    first = jnp.mean(upstream, axis=-1, keepdims=True)
    second = jnp.mean(upstream * normalized_rows, axis=-1, keepdims=True)
    return inverse * (upstream - first - normalized_rows * second)


MESH = pl.DeviceIdType.MESH
ROWS_PAD = 48
HEAD_PAD = 96
OUT_ROWS_PAD = 32
OUT_COLS_PAD = 1536


def place():
    s, i = lax.axis_index("sp"), lax.axis_index("img")
    return s // 8, (s // 4) % 2, s % 4, i // 2, i % 2


def at_sp(x, zl, y):
    return {"sp": (x * 2 + zl) * 4 + y}


def greet(targets):
    barrier = pltpu.get_barrier_semaphore()
    for target in targets:
        pl.semaphore_signal(barrier, inc=1, device_id=target, device_id_type=MESH)
    pl.semaphore_wait(barrier, len(targets))


def one_hot(rows, per, block):
    r = lax.broadcasted_iota(jnp.int32, (block, 4 * rows), 0)
    c = lax.broadcasted_iota(jnp.int32, (block, 4 * rows), 1)
    skipped = jnp.zeros_like(r)
    for k in (1, 2, 3):
        skipped += jnp.where(r >= k * per, rows - per, 0)
    return jnp.where(c == r + skipped, 1.0, 0.0)


def gather_kernel(shapes, *refs):
    count = len(shapes)
    ins = refs[:3]
    y_one, second, cot, w_lateral, lat_gain, w_conv, conv_gain = refs[3:10]
    qkv_out, w_out_out, half_out, d_x1_out, dec_out, conv_out, lat_out = refs[10:17]
    deconv, *rest = refs[17:]
    outs = [deconv, qkv_out, w_out_out]
    shards, packs, rest = rest[:3], rest[3:6], rest[6:]
    feature, pixels, act, dconv, cot_low, cot_high, norm_lat, dup, *sems = rest
    send, recv, local, halo_send, halo_recv = sems
    x, zl, y, zh, core = place()
    s = lax.axis_index("sp")
    below, above = {"sp": (s + 1) % 32}, {"sp": (s + 31) % 32}
    xm, xp, xo = (x + 3) % 4, (x + 1) % 4, (x + 2) % 4
    left, right = at_sp(xm, zl, y), at_sp(xp, zl, y)
    across = (x * 2 + 1 - zl) * 4 + y
    up = {"img": ((zh + zl) % 4) * 2 + core, "sp": across}
    down = {"img": ((zh + zl + 3) % 4) * 2 + core, "sp": across}
    twin = {"img": zh * 2 + 1 - core}
    column = [at_sp(x, zl, (y + k) % 4) for k in (1, 2, 3)]
    greet(column + [left, right, up, down, twin, below, above])
    copies = {}

    def push(a, slot, src, dst, target):
        copy = pltpu.make_async_remote_copy(
            src_ref=src,
            dst_ref=dst,
            send_sem=send.at[a, slot],
            recv_sem=recv.at[a, slot],
            device_id=target,
            device_id_type=MESH,
        )
        copy.start()
        copies[a, slot] = copy

    def part(a):
        half = shapes[a][3] // 2
        return half, pl.multiple_of(core * half, 128)

    def region(a, bx, bz, lo, size):
        half, first = part(a)
        return outs[a].at[bx * 2 + bz, pl.ds(lo, size), pl.ds(first, half)]

    def forward(a, slot, bx, bz, lo, size, target):
        piece = region(a, bx, bz, lo, size)
        push(a, slot, piece, piece, target)

    for a in range(count):
        half, first = part(a)
        mine = ins[a].at[:, pl.ds(first, half)]
        for k in range(3):
            push(a, k, mine, shards[a].at[y], column[k])
        shards[a][y] = ins[a][:, pl.ds(first, half)]
    keeps = {}

    def pack(a):
        rows, per, block, _ = shapes[a]
        half, first = part(a)
        low = (block // 32) * 16
        high = block - low
        for k in range(3):
            copies[a, k].wait_recv()
        pick = one_hot(rows, per, block).astype(jnp.bfloat16)
        packs[a][...] = jnp.dot(
            pick, shards[a][...].reshape(4 * rows, half), preferred_element_type=jnp.float32
        ).astype(jnp.bfloat16)
        own, whole = packs[a], region(a, x, zl, 0, block)
        keep = pltpu.make_async_copy(own, whole, local.at[a])
        keep.start()
        keeps[a] = keep
        push(a, 3, own, whole, right)
        push(a, 4, own, whole, left)
        push(a, 7, own.at[pl.ds(0, low)], region(a, x, zl, 0, low), up)
        push(a, 8, own.at[pl.ds(low, high)], region(a, x, zl, low, high), down)
        push(a, 15, own, whole, twin)

    def near(a):
        block = shapes[a][2]
        low = (block // 32) * 16
        high = block - low
        copies[a, 3].wait_recv()
        forward(a, 5, xm, zl, 0, low, right)
        forward(a, 9, xm, zl, 0, low, up)
        forward(a, 10, xm, zl, low, high, down)
        forward(a, 16, xm, zl, 0, block, twin)
        copies[a, 4].wait_recv()
        forward(a, 6, xp, zl, low, high, left)
        forward(a, 11, xp, zl, 0, low, up)
        forward(a, 12, xp, zl, low, high, down)
        forward(a, 17, xp, zl, 0, block, twin)

    def far(a):
        block = shapes[a][2]
        low = (block // 32) * 16
        high = block - low
        copies[a, 5].wait_recv()
        forward(a, 13, xo, zl, 0, low, up)
        forward(a, 18, xo, zl, 0, low, twin)
        copies[a, 6].wait_recv()
        forward(a, 14, xo, zl, low, high, down)
        forward(a, 19, xo, zl, low, high, twin)

    def deep(a):
        block = shapes[a][2]
        low = (block // 32) * 16
        high = block - low
        for n, bx in enumerate((x, xm, xp, xo)):
            copies[a, 7 + 2 * n].wait_recv()
            forward(a, 20 + 2 * n, bx, 1 - zl, 0, low, twin)
            copies[a, 8 + 2 * n].wait_recv()
            forward(a, 21 + 2 * n, bx, 1 - zl, low, high, twin)

    def twins(a):
        for slot in range(15, 28):
            copies[a, slot].wait_recv()

    row = GRID_W
    inner_rows = 4 * row
    halos = {}

    def swap_edges(ref, first):
        ends = (
            (first, pl.ds(inner_rows, row), pl.ds(0, row), below),
            (first + 1, pl.ds(row, row), pl.ds(inner_rows + row, row), above),
        )
        for slot, src_rows, dst_rows, target in ends:
            copy = pltpu.make_async_remote_copy(
                src_ref=ref.at[pl.ds(1, 2), src_rows],
                dst_ref=ref.at[pl.ds(1, 2), dst_rows],
                send_sem=halo_send.at[slot],
                recv_sem=halo_recv.at[slot],
                device_id=target,
                device_id_type=MESH,
            )
            copy.start()
            halos[slot] = copy

    def fill_sides(ref, first):
        halos[first].wait_recv()
        halos[first + 1].wait_recv()
        for b in (1, 2):
            head, tail = pl.ds(0, row), pl.ds(inner_rows + row, row)
            ref[b, head] = jnp.where(s == 0, 0.0, ref[b, head].astype(jnp.float32)).astype(
                jnp.bfloat16
            )
            ref[b, tail] = jnp.where(s == 31, 0.0, ref[b, tail].astype(jnp.float32)).astype(
                jnp.bfloat16
            )
        rows = ref.shape[1]
        at = lax.broadcasted_iota(jnp.int32, (rows, LAT), 0) % row
        moved = pltpu.roll(ref[2].astype(jnp.float32), 1, 0)
        ref[0] = jnp.where(at == 0, 0.0, moved).astype(jnp.bfloat16)
        moved = pltpu.roll(ref[1].astype(jnp.float32), rows - 1, 0)
        ref[3] = jnp.where(at == row - 1, 0.0, moved).astype(jnp.bfloat16)

    def taps():
        return [(i, j) for i in range(3) for j in range(3)]

    def upward():
        feature[...] = ((y_one[...].astype(jnp.float32) + second[...].astype(jnp.float32)) * 0.5).astype(
            jnp.bfloat16
        )
        wide = cot[...].reshape(8 * row, LAT).astype(jnp.float32)
        cot_low[...] = wide[:, : LAT // 2]
        cot_high[...] = wide[:, LAT // 2 :]
        depth = deconv.shape[0] * deconv.shape[1]
        for ab in range(4):
            plane = pl.ds(ab * DEC, DEC)
            up = jnp.dot(
                feature[...],
                deconv[:, :, plane].reshape(depth, DEC),
                preferred_element_type=jnp.float32,
            ).astype(jnp.bfloat16)
            for r in range(2):
                pixels[pl.ds((ab % 2) * inner_rows + (2 * r + ab // 2) * row, row)] = up[
                    r * row : (r + 1) * row
                ]
        lat = jnp.dot(pixels[...], w_lateral[...], preferred_element_type=jnp.float32)
        lhat, linv = apply_layer_norm(lat)
        norm_lat[...] = lhat
        scaled = (lhat * lat_gain[...]).astype(jnp.bfloat16)
        for b in range(2):
            act[1 + b, pl.ds(row, inner_rows)] = scaled[b * inner_rows : (b + 1) * inner_rows]
        swap_edges(act, 0)
        return linv

    def convolve():
        fill_sides(act, 0)
        for b in range(2):
            total = jnp.zeros((inner_rows, LAT), jnp.float32)
            for i, j in taps():
                total += jnp.dot(
                    act[b + j, pl.ds(i * row, inner_rows)],
                    w_conv[3 * i + j],
                    preferred_element_type=jnp.float32,
                )
            chat, cinv = apply_layer_norm(total)
            every = pl.ds(b, inner_rows, stride=2)
            upstream = jnp.concatenate([cot_low[every, :], cot_high[every, :]], axis=1)
            upstream = upstream * conv_gain[...]
            dconv[1 + b, pl.ds(row, inner_rows)] = layer_norm_reverse(upstream, chat, cinv).astype(
                jnp.bfloat16
            )
        swap_edges(dconv, 2)

    def downward(linv):
        fill_sides(dconv, 2)
        for b in range(2):
            total = jnp.zeros((inner_rows, LAT), jnp.float32)
            for i, j in taps():
                total += lax.dot_general(
                    dconv[b - j + 2, pl.ds((2 - i) * row, inner_rows)],
                    w_conv[3 * i + j],
                    (((1,), (1,)), ((), ())),
                    preferred_element_type=jnp.float32,
                )
            here = slice(b * inner_rows, (b + 1) * inner_rows)
            dlat = layer_norm_reverse(
                total * lat_gain[...], norm_lat[pl.ds(b * inner_rows, inner_rows)], linv[here]
            ).astype(jnp.bfloat16)
            term = jnp.dot(
                pixels[pl.ds(b * inner_rows, inner_rows)].astype(jnp.float32).T.astype(jnp.bfloat16),
                dlat,
                preferred_element_type=jnp.float32,
            )
            lat_term = term if b == 0 else lat_term + term
            dpixels = lax.dot_general(
                dlat, w_lateral[...], (((1,), (1,)), ((), ())), preferred_element_type=jnp.float32
            ).astype(jnp.bfloat16)
            for line in range(4):
                r, a = line // 2, line % 2
                dup[pl.ds(r * row, row), pl.ds((2 * a + b) * DEC, DEC)] = dpixels[
                    line * row : (line + 1) * row
                ]
        lat_out[...] = (lat_term * grad_scale).astype(jnp.bfloat16)
        depth = deconv.shape[0] * deconv.shape[1]
        half = 0.5 * lax.dot_general(
            dup[...],
            deconv[...].reshape(depth, 4 * DEC),
            (((1,), (1,)), ((), ())),
            preferred_element_type=jnp.float32,
        )
        half_out[...] = half
        d_x1_out[...] = half.astype(jnp.bfloat16)

    def conv_term():
        turned_grads = [
            dconv[1 + b, pl.ds(row, inner_rows)].astype(jnp.float32).T.astype(jnp.bfloat16)
            for b in range(2)
        ]
        for i, j in taps():
            total = jnp.zeros((LAT, LAT), jnp.float32)
            for b in range(2):
                total += jnp.dot(
                    turned_grads[b],
                    act[b + j, pl.ds(i * row, inner_rows)],
                    preferred_element_type=jnp.float32,
                )
            conv_out[:, pl.ds((3 * i + j) * LAT, LAT)] = (total.T * grad_scale).astype(jnp.bfloat16)

    def deconv_term():
        rows, per, block, _ = shapes[0]
        wide = feature[...].astype(jnp.float32).T
        pick = one_hot(rows, per, block).T.astype(jnp.bfloat16)
        for g in range(8):
            group = jnp.dot(
                pick,
                wide[g * block : (g + 1) * block].astype(jnp.bfloat16),
                preferred_element_type=jnp.float32,
            ).astype(jnp.bfloat16)
            term = jnp.dot(group, dup[...], preferred_element_type=jnp.float32) * grad_scale
            dec_out[pl.ds(g * 4 * rows, 4 * rows)] = term.astype(jnp.bfloat16)

    pack(0)
    near(0)
    pack(1)
    far(0)
    pack(2)
    near(1)
    deep(0)
    twins(0)
    keeps[0].wait()
    linv = upward()
    far(1)
    near(2)
    convolve()
    far(2)
    downward(linv)
    deep(1)
    conv_term()
    deep(2)
    deconv_term()
    twins(1)
    twins(2)
    for a in range(1, count):
        keeps[a].wait()
    for copy in list(copies.values()) + list(halos.values()):
        copy.wait_send()


def gather_and_pyramid(shards, pers, *others):
    count = len(shards)
    shapes = []
    for shard, per in zip(shards, pers):
        block = -(-4 * per // 16) * 16
        shapes.append((shard.shape[0], per, block, shard.shape[1]))
    halves = [(rows, block, width // 2) for rows, _, block, width in shapes]
    tokens, features = others[0].shape
    bf16, f32 = jnp.bfloat16, jnp.float32
    full = [jax.ShapeDtypeStruct((8, block, width), bf16) for _, _, block, width in shapes]
    pixel_count = 4 * tokens
    return pl.pallas_call(
        functools.partial(gather_kernel, shapes),
        out_shape=full[1:]
        + [
            jax.ShapeDtypeStruct((tokens, features), f32),
            jax.ShapeDtypeStruct((tokens, features), bf16),
            jax.ShapeDtypeStruct((32 * ROWS_PAD, 4 * DEC), bf16),
            jax.ShapeDtypeStruct((LAT, 9 * LAT), bf16),
            jax.ShapeDtypeStruct((DEC, LAT), bf16),
        ],
        in_specs=[pl.BlockSpec(memory_space=pltpu.VMEM)] * (count + len(others)),
        out_specs=[pl.BlockSpec(memory_space=pl.ANY)] * (count - 1)
        + [pl.BlockSpec(memory_space=pltpu.VMEM)] * 5,
        scratch_shapes=[pltpu.VMEM(full[0].shape, bf16)]
        + [pltpu.VMEM((4, rows, half), bf16) for rows, _, half in halves]
        + [pltpu.VMEM((block, half), bf16) for _, block, half in halves]
        + [
            pltpu.VMEM((tokens, features), bf16),
            pltpu.VMEM((pixel_count, DEC), bf16),
            pltpu.VMEM((4, 6 * GRID_W, LAT), bf16),
            pltpu.VMEM((4, 6 * GRID_W, LAT), bf16),
            pltpu.VMEM((pixel_count, LAT // 2), f32),
            pltpu.VMEM((pixel_count, LAT // 2), f32),
            pltpu.VMEM((pixel_count, LAT), f32),
            pltpu.VMEM((tokens, 4 * DEC), bf16),
            pltpu.SemaphoreType.DMA((count, 28)),
            pltpu.SemaphoreType.DMA((count, 28)),
            pltpu.SemaphoreType.DMA((count,)),
            pltpu.SemaphoreType.DMA((4,)),
            pltpu.SemaphoreType.DMA((4,)),
        ],
        compiler_params=pltpu.CompilerParams(
            collective_id=0, has_side_effects=True, vmem_limit_bytes=56 * 2**20
        ),
    )(*shards, *others)


AXES = {"x": 4, "z": 2, "y": 4}


def leads(order):
    left = list(AXES)
    sizes = []
    for axis in order:
        left = [name for name in left if name != axis]
        sizes.append([AXES[name] for name in left])
    return sizes


class Scatter:
    def __init__(self, plan, parts, buffers, send, recv, local):
        self.plan, self.parts = plan, parts
        self.land = [buffers[0], buffers[2], buffers[4]]
        self.sums = [buffers[1], buffers[3]]
        self.send, self.recv, self.local = send, recv, local
        x, zl, y, _, _ = place()
        self.me = {"x": x, "z": zl, "y": y}
        self.peers = {
            "x": [(x + k) % 4 for k in (1, 2, 3)],
            "y": [(y + k) % 4 for k in (1, 2, 3)],
            "z": [1 - zl],
        }
        self.copies, self.own = {}, {}

    def take(self, n, step, view, where):
        order = self.plan[n][3]
        left = [name for name in AXES if name not in order[:step]]
        lead = [slice(None)] * left.index(order[step])
        return view.at[(*lead, where)]

    def ship(self, n, step, view):
        axis = self.plan[n][3][step]
        for k, peer in enumerate(self.peers[axis]):
            at = dict(self.me)
            at[axis] = peer
            copy = pltpu.make_async_remote_copy(
                src_ref=self.take(n, step, view, peer),
                dst_ref=self.land[step][n].at[k],
                send_sem=self.send.at[n, 3 * step + k],
                recv_sem=self.recv.at[n, 3 * step + k],
                device_id=at_sp(at["x"], at["z"], at["y"]),
                device_id_type=MESH,
            )
            copy.start()
            self.copies[n, step, k] = copy

    def arrived(self, n, step):
        count = len(self.peers[self.plan[n][3][step]])
        for k in range(count):
            self.copies[n, step, k].wait_recv()
        return count

    def start(self, n):
        source, first, width, order = self.plan[n]
        view = self.parts[source].at[:, :, :, :, pl.ds(first, width)]
        own = self.take(n, 0, view, self.me[order[0]])
        self.own[n] = pltpu.make_async_copy(own, self.sums[0][n], self.local.at[n])
        self.own[n].start()
        self.ship(n, 0, view)

    def second(self, n):
        sums, land = self.sums[0][n], self.land[0][n]
        self.own[n].wait()
        count = self.arrived(n, 0)
        outer, inner = sums.shape[:2]

        def add(t, carry):
            p, q = t // inner, t % inner
            total = sums[p, q].astype(jnp.float32)
            for k in range(count):
                total += land[k, p, q].astype(jnp.float32)
            sums[p, q] = total.astype(jnp.bfloat16)
            return carry

        lax.fori_loop(0, outer * inner, add, 0)
        self.ship(n, 1, sums)

    def third(self, n):
        land, sums = self.land[1][n], self.sums[1][n]
        order = self.plan[n][3]
        count = self.arrived(n, 1)
        own = self.take(n, 1, self.sums[0][n], self.me[order[1]])
        for p in range(sums.shape[0]):
            total = own[p].astype(jnp.float32)
            for k in range(count):
                total += land[k, p].astype(jnp.float32)
            sums[p] = total.astype(jnp.bfloat16)
        self.ship(n, 2, sums)

    def finish(self, n, out):
        count = self.arrived(n, 2)
        total = self.sums[1][n][self.me[self.plan[n][3][2]]].astype(jnp.float32)
        for k in range(count):
            total += self.land[2][n][k].astype(jnp.float32)
        out[...] = total

    def settle(self):
        for copy in self.copies.values():
            copy.wait_send()


def scatter_buffers(plan, rows):
    groups = [[], [], [], [], []]
    for source, _, width, order in plan:
        sizes = leads(order)
        for step in range(3):
            peers = AXES[order[step]] - 1
            tail = (rows[source], width)
            groups[2 * step].append(pltpu.VMEM((peers, *sizes[step], *tail), jnp.bfloat16))
            if step < 2:
                groups[2 * step + 1].append(pltpu.VMEM((*sizes[step], *tail), jnp.bfloat16))
    return groups


TILE = 128
QUERY_BLOCK = 512
KEY_BLOCK = 1024


def turned(block):
    wide = block.astype(jnp.float32)
    zeros = jnp.zeros((TILE - HEAD_PAD, TILE), jnp.float32)
    return jnp.concatenate([wide, zeros], axis=0).T


def head_rows(block):
    return block.T[:HEAD_PAD].astype(jnp.bfloat16)


SUM_PLAN = [
    (0, 0, 2 * DEC, "xyz"),
    (0, 2 * DEC, 2 * DEC, "zxy"),
    (1, 0, 9 * LAT, "zxy"),
    (2, 0, LAT, "zxy"),
    (3, 0, 768, "yxz"),
    (3, 768, 640, "xyz"),
]
OUT_ROWS = 22
OUT_ROWS_STEP = 24


def attention_kernel(proj, grad, d_x1, dec_part, conv_part, lat_part, *refs):
    attn_out, dqkv_out, *sum_outs = refs[:8]
    (
        q_in,
        g_in,
        kv_in,
        key_t,
        value_t,
        key,
        value,
        query,
        cot,
        query_t,
        cot_t,
        score,
        weight,
        inverse,
        offset,
        attended,
        o_send,
        dq_send,
        d_send,
        d_land,
        d_sum,
        o_land,
        d_res,
        out_part,
    ) = refs[8:32]
    chunks = len(SUM_PLAN)
    groups = [refs[32 + chunks * k : 32 + chunks * (k + 1)] for k in range(5)]
    send, recv, sum_send, sum_recv, sum_local = refs[32 + 5 * chunks :]
    sums = Scatter(
        SUM_PLAN, [dec_part, conv_part, lat_part, out_part], groups, sum_send, sum_recv, sum_local
    )
    x, zl, y, zh, core = place()
    m = x * 2 + zl
    plane = [(m + k) % 8 for k in range(8)]
    source = [(m + 8 - k) % 8 for k in range(8)]
    column = [(y + k) % 4 for k in range(4)]

    def at_plane(k):
        return {"sp": plane[k] * 4 + y}

    def at_column(k):
        return {"sp": m * 4 + column[k]}

    greet([at_plane(k) for k in range(1, 8)] + [at_column(k) for k in range(1, 4)])
    copies = {}

    def push(slot, src, dst, target):
        copy = pltpu.make_async_remote_copy(
            src_ref=src,
            dst_ref=dst,
            send_sem=send.at[slot],
            recv_sem=recv.at[slot],
            device_id=target,
            device_id_type=MESH,
        )
        copy.start()
        copies[slot] = copy

    kv_at, q_at, g_at, ring_at, o_at, dq_at, back_at, home_at = 0, 8, 16, 24, 48, 56, 64, 72
    for k in range(1, 8):
        push(kv_at + k, proj.at[pl.ds(1, 2), plane[k]], kv_in.at[y, m], at_plane(k))
    kv_in[y, m, 0] = proj[1, m]
    kv_in[y, m, 1] = proj[2, m]
    q_in[m] = proj[0, m]
    g_in[m] = grad[m]

    def pass_on(k):
        piece = kv_in.at[y, source[k]]
        for j in range(1, 4):
            push(ring_at + 3 * k + j - 1, piece, piece, at_column(j))

    pass_on(0)
    for k in range(1, 8):
        push(q_at + k, proj.at[0, plane[k]], q_in.at[m], at_plane(k))
    for k in range(1, 8):
        copies[kv_at + k].wait_recv()
        pass_on(k)
    for k in range(1, 8):
        push(g_at + k, grad.at[plane[k]], g_in.at[m], at_plane(k))
    for n in (0, 1, 2, 3):
        sums.start(n)
    zero_rows = jnp.zeros((TILE - HEAD_PAD, key_t.shape[1]), jnp.bfloat16)
    key_t[HEAD_PAD:] = zero_rows
    value_t[HEAD_PAD:] = zero_rows

    def prepare(t, carry):
        at = pl.ds(pl.multiple_of(t * TILE, TILE), TILE)
        block = kv_in[t // 8, t % 8, 0]
        key_t[:HEAD_PAD, at] = block
        key[at, :] = turned(block).astype(jnp.bfloat16)
        block = kv_in[t // 8, t % 8, 1]
        value_t[:HEAD_PAD, at] = block
        value[at, :] = turned(block).astype(jnp.bfloat16)
        return carry

    def prepare_queries(t, carry):
        query[pl.ds(pl.multiple_of(t * TILE, TILE), TILE), :] = turned(q_in[t]).astype(jnp.bfloat16)
        return carry

    def prepare_cots(t, carry):
        cot[pl.ds(pl.multiple_of(t * TILE, TILE), TILE), :] = turned(g_in[t]).astype(jnp.bfloat16)
        return carry

    lax.fori_loop(y * 8, y * 8 + 8, prepare, 0)
    for k in range(1, 8):
        copies[q_at + k].wait_recv()
    lax.fori_loop(0, 8, prepare_queries, 0)
    for j in range(1, 4):
        for k in range(8):
            copies[ring_at + 3 * k + j - 1].wait_recv()
        first = ((y + 4 - j) % 4) * 8
        lax.fori_loop(first, first + 8, prepare, 0)
    for k in range(1, 8):
        copies[g_at + k].wait_recv()
    lax.fori_loop(0, 8, prepare_cots, 0)

    tokens = key.shape[0]
    queries = query.shape[0]
    blocks = [pl.ds(c * KEY_BLOCK, KEY_BLOCK) for c in range(tokens // KEY_BLOCK)]

    def forward(i, carry):
        at = pl.ds(pl.multiple_of(i * QUERY_BLOCK, QUERY_BLOCK), QUERY_BLOCK)
        top = jnp.full((QUERY_BLOCK, 1), -jnp.inf, jnp.float32)
        for block in blocks:
            part = jnp.dot(query[at, :], key_t[:, block], preferred_element_type=jnp.float32)
            score[:, block] = part
            top = jnp.maximum(top, jnp.max(part, axis=1, keepdims=True))
        total = jnp.zeros((QUERY_BLOCK, 1), jnp.float32)
        mixed = jnp.zeros((QUERY_BLOCK, TILE), jnp.float32)
        for block in blocks:
            part = jnp.exp(score[:, block] - top)
            total += jnp.sum(part, axis=1, keepdims=True)
            rounded = part.astype(jnp.bfloat16)
            weight[at, block] = rounded
            mixed += jnp.dot(rounded, value[block, :], preferred_element_type=jnp.float32)
        inv = 1.0 / total
        mixed = mixed * inv
        attended[at, :] = mixed
        inverse[at, :] = inv
        offset[at, :] = jnp.sum(mixed * cot[at, :].astype(jnp.float32), axis=1, keepdims=True)
        return carry

    lax.fori_loop(0, queries // QUERY_BLOCK, forward, 0)
    for t in range(8):
        at = pl.ds(t * TILE, TILE)
        o_send[t] = head_rows(attended[at, :])
    for k in range(1, 8):
        push(o_at + k, o_send.at[plane[k]], o_land.at[m], at_plane(k))
    o_land[m] = o_send[m]
    for t in range(8):
        at = pl.ds(t * TILE, TILE)
        inv = inverse[at, :]
        query_t[:, at] = (query[at, :].astype(jnp.float32) * inv).T.astype(jnp.bfloat16)
        cot_t[:, at] = (cot[at, :].astype(jnp.float32) * inv).T.astype(jnp.bfloat16)

    def key_side(left, kind):
        for j in (1, 2, 3, 0):
            yy = column[j]
            at = pl.ds(pl.multiple_of(yy * 8 * TILE, 8 * TILE), 8 * TILE)
            result = jnp.dot(left[...], weight[:, at], preferred_element_type=jnp.float32)
            for t in range(8):
                d_send[kind, j, t] = result[:HEAD_PAD, t * TILE : (t + 1) * TILE].astype(
                    jnp.bfloat16
                )
            if j:
                push(back_at + 4 * kind + j, d_send.at[kind, j], d_land.at[kind, j - 1], at_column(j))

    def key_home(kind):
        for j in range(1, 4):
            copies[back_at + 4 * kind + j].wait_recv()
        for t in range(8):
            total = d_send[kind, 0, t].astype(jnp.float32)
            for j in range(3):
                total += d_land[kind, j, t].astype(jnp.float32)
            d_sum[kind, t] = total.astype(jnp.bfloat16)
        for k in range(1, 8):
            push(
                home_at + 8 * kind + k,
                d_sum.at[kind, plane[k]],
                d_res.at[kind + 1, m],
                at_plane(k),
            )
        d_res[kind + 1, m] = d_sum[kind, m]

    key_side(cot_t, 1)
    for k in range(1, 8):
        copies[o_at + k].wait_recv()
    attn_out[...] = o_land[...]
    spread = 4 * OUT_ROWS_STEP
    r = lax.broadcasted_iota(jnp.int32, (spread, HEAD_PAD), 0)
    c = lax.broadcasted_iota(jnp.int32, (spread, HEAD_PAD), 1)
    picked = c < 0
    for k in range(4):
        low, first = k * OUT_ROWS, k * OUT_ROWS_STEP
        picked |= (c - low == r - first) & (c >= low) & (c < low + OUT_ROWS) & (r >= first)
    pick = jnp.where(picked, 1.0, 0.0).astype(jnp.bfloat16)
    for t in range(8):
        rows = jnp.dot(pick, o_land[t], preferred_element_type=jnp.float32).astype(jnp.bfloat16)
        term = jnp.dot(rows, d_x1[...], preferred_element_type=jnp.float32) * grad_scale
        for k in range(4):
            out_part[t // 2, t % 2, k] = term[
                k * OUT_ROWS_STEP : (k + 1) * OUT_ROWS_STEP
            ].astype(jnp.bfloat16)
    sums.start(4)
    sums.start(5)
    for n in (3, 2, 0, 1):
        sums.second(n)

    def backward(i, carry):
        at = pl.ds(pl.multiple_of(i * QUERY_BLOCK, QUERY_BLOCK), QUERY_BLOCK)
        query_grad = jnp.zeros((QUERY_BLOCK, TILE), jnp.float32)
        shift = offset[at, :]
        for block in blocks:
            dprob = jnp.dot(cot[at, :], value_t[:, block], preferred_element_type=jnp.float32)
            dscore = (weight[at, block].astype(jnp.float32) * (dprob - shift)).astype(jnp.bfloat16)
            weight[at, block] = dscore
            query_grad += jnp.dot(dscore, key[block, :], preferred_element_type=jnp.float32)
        attended[at, :] = query_grad * (inverse[at, :] * HEAD ** (-0.5))
        return carry

    for i in range(queries // QUERY_BLOCK):
        backward(i, 0)
        if i == 0:
            key_home(1)
    key_side(query_t, 0)
    for t in range(8):
        dq_send[t] = head_rows(attended[pl.ds(t * TILE, TILE), :])
    for k in range(1, 8):
        push(dq_at + k, dq_send.at[plane[k]], d_res.at[0, m], at_plane(k))
    d_res[0, m] = dq_send[m]
    key_home(0)
    for n in (3, 2, 0, 1):
        sums.third(n)
    sums.second(4)
    sums.second(5)
    sums.third(4)
    sums.third(5)
    for first in (dq_at, home_at, home_at + 8):
        for k in range(1, 8):
            copies[first + k].wait_recv()
    dqkv_out[...] = d_res[...]
    for n in range(chunks):
        sums.finish(n, sum_outs[n])
    for copy in copies.values():
        copy.wait_send()
    sums.settle()


def attend_both_ways(proj, grad, d_x1, dec_part, conv_part, lat_part):
    rows = [part.shape[3] for part in (dec_part, conv_part, lat_part)] + [OUT_ROWS_STEP]
    groups = scatter_buffers(SUM_PLAN, rows)
    heads = grad.shape[0]
    tokens, queries = 32 * TILE, 8 * TILE
    bf16, f32 = jnp.bfloat16, jnp.float32
    block = (HEAD_PAD, TILE)
    shapes = [
        ((8, *block), bf16),
        ((8, *block), bf16),
        ((4, 8, 2, *block), bf16),
        ((TILE, tokens), bf16),
        ((TILE, tokens), bf16),
        ((tokens, TILE), bf16),
        ((tokens, TILE), bf16),
        ((queries, TILE), bf16),
        ((queries, TILE), bf16),
        ((TILE, queries), bf16),
        ((TILE, queries), bf16),
        ((QUERY_BLOCK, tokens), f32),
        ((queries, tokens), bf16),
        ((queries, 1), f32),
        ((queries, 1), f32),
        ((queries, TILE), f32),
        ((8, *block), bf16),
        ((8, *block), bf16),
        ((2, 4, 8, *block), bf16),
        ((2, 3, 8, *block), bf16),
        ((2, 8, *block), bf16),
        ((8, *block), bf16),
        ((3, 8, *block), bf16),
        ((4, 2, 4, OUT_ROWS_STEP, d_x1.shape[1]), bf16),
    ]
    sum_sems = pltpu.SemaphoreType.DMA((len(SUM_PLAN), 9))
    return pl.pallas_call(
        attention_kernel,
        out_shape=[
            jax.ShapeDtypeStruct((heads, *block), bf16),
            jax.ShapeDtypeStruct((3, heads, *block), bf16),
        ]
        + [jax.ShapeDtypeStruct((rows[source], width), f32) for source, _, width, _ in SUM_PLAN],
        in_specs=[pl.BlockSpec(memory_space=pltpu.VMEM)] * 3
        + [pl.BlockSpec(memory_space=pl.ANY)] * 3,
        out_specs=[pl.BlockSpec(memory_space=pltpu.VMEM)] * 8,
        scratch_shapes=[pltpu.VMEM(shape, kind) for shape, kind in shapes]
        + [buffer for group in groups for buffer in group]
        + [pltpu.SemaphoreType.DMA((88,)), pltpu.SemaphoreType.DMA((88,))]
        + [sum_sems, sum_sems, pltpu.SemaphoreType.DMA((len(SUM_PLAN),))],
        compiler_params=pltpu.CompilerParams(
            collective_id=2, has_side_effects=True, vmem_limit_bytes=56 * 2**20
        ),
    )(proj, grad, d_x1, dec_part, conv_part, lat_part)


def per_device(
    y_one,
    second_stream_state,
    cot,
    layer_norm_gain,
    w_qkv,
    w_out,
    w_deconv,
    w_lateral,
    lat_gain,
    w_conv,
    conv_gain,
):
    devices = lax.axis_size("sp")
    tokens_here = y_one.shape[0]
    score_scale = HEAD ** (-0.5)
    standardized_input, inverse_deviation = apply_layer_norm(
        second_stream_state.astype(jnp.float32)
    )
    normalized_rows = (standardized_input * layer_norm_gain).astype(jnp.bfloat16)
    depth, out_depth = w_qkv.shape[0], w_out.shape[0]
    qkv_shard = jnp.pad(
        w_qkv.reshape(depth, 3 * HEADS, HEAD),
        ((0, ROWS_PAD - depth), (0, 0), (0, HEAD_PAD - HEAD)),
    ).reshape(ROWS_PAD, 3 * HEADS * HEAD_PAD)
    out_shard = jnp.pad(
        w_out, ((0, OUT_ROWS_PAD - out_depth), (0, OUT_COLS_PAD - w_out.shape[1]))
    )
    deconv_shard = jnp.pad(w_deconv, ((0, ROWS_PAD - depth), (0, 0)))
    qkv_full, out_full, halfway_split, d_x1, dec_part, conv_part, lat_part = gather_and_pyramid(
        [deconv_shard, qkv_shard, out_shard],
        [depth, depth, out_depth],
        y_one,
        second_stream_state,
        cot,
        w_lateral,
        lat_gain[None],
        w_conv.reshape(9, LAT, LAT),
        conv_gain[None],
    )
    dec_part = dec_part.reshape(4, 2, 4, ROWS_PAD, 4 * DEC)
    conv_part = conv_part.reshape(4, 2, 4, LAT // devices, 9 * LAT)
    lat_rows = DEC // devices
    lat_part = jnp.pad(
        lat_part.reshape(devices, lat_rows, LAT), ((0, 0), (0, 16 - lat_rows), (0, 0))
    ).reshape(4, 2, 4, 16, LAT)
    qkv_full = qkv_full.reshape(devices * depth, -1)
    out_full = out_full.reshape(HEADS * HEAD_PAD, -1)[:, : w_out.shape[1]]
    dattn = lax.dot_general(
        out_full, d_x1, (((1,), (1,)), ((), ())), preferred_element_type=jnp.float32
    ).astype(jnp.bfloat16)
    projected = lax.optimization_barrier(
        jnp.dot(normalized_rows, qkv_full, preferred_element_type=jnp.float32)
    )
    projected = projected.T.reshape(3, HEADS, HEAD_PAD, tokens_here)
    scales = jnp.array([score_scale, 1.0, 1.0], jnp.float32).reshape(3, 1, 1, 1)
    projected = (projected * scales).astype(jnp.bfloat16)
    attn_heads, dqkv, *summed = attend_both_ways(
        projected,
        dattn.reshape(HEADS, HEAD_PAD, tokens_here),
        d_x1,
        dec_part,
        conv_part,
        lat_part,
    )
    dec_low, dec_high, conv_rows, lat_sums, out_low, out_high = summed
    mixed = lax.dot_general(
        attn_heads.reshape(HEADS * HEAD_PAD, tokens_here),
        out_full,
        (((0,), (0,)), ((), ())),
        preferred_element_type=jnp.float32,
    )
    x_one = (y_one.astype(jnp.float32) - mixed).astype(jnp.bfloat16)
    normalized_gradient = lax.dot_general(
        dqkv.reshape(3 * HEADS * HEAD_PAD, tokens_here),
        qkv_full, (((0,), (1,)), ((), ())), preferred_element_type=jnp.float32
    )
    second_input_gradient = (
        halfway_split
        + layer_norm_reverse(
            normalized_gradient * layer_norm_gain, standardized_input, inverse_deviation
        )
    ).astype(jnp.bfloat16)
    g_deconv = jnp.concatenate([dec_low[:depth], dec_high[:depth]], axis=1)
    g_out = jnp.concatenate([out_low[:out_depth], out_high[:out_depth]], axis=1)
    g_lateral = lat_sums[:lat_rows]
    g_conv = conv_rows.reshape(conv_rows.shape[0], 3, 3, LAT).transpose(1, 2, 0, 3)
    return (x_one, d_x1, second_input_gradient, g_out, g_deconv, g_lateral, g_conv)


def solution(mesh):
    return jax.shard_map(
        per_device,
        mesh=mesh,
        in_specs=(
            P(("img", "sp"), None),
            P(("img", "sp"), None),
            P(("img", "sp"), None, None),
            P(),
            P("sp", None),
            P("sp", None),
            P("sp", None),
            P(),
            P(),
            P(),
            P(),
        ),
        out_specs=(
            P(("img", "sp"), None),
            P(("img", "sp"), None),
            P(("img", "sp"), None),
            P(("img", "sp"), None),
            P(("img", "sp"), None),
            P(("img", "sp"), None),
            P("img", None, "sp", None),
        ),
        check_vma=False,
    )
```

```python
import functools

import jax
import jax.numpy as jnp
from jax import lax
from jax.experimental import pallas as pl
from jax.experimental.pallas import tpu as pltpu
from jax.sharding import PartitionSpec as P

HEADS = 8
HEAD = 88
DEC = 384
LAT = 256
GRID_W = 64


epsilon = 1e-06
grad_scale = 0.015625


def apply_layer_norm(values):
    centered = values - jnp.mean(values, axis=-1, keepdims=True)
    inverse = lax.rsqrt(jnp.mean(centered * centered, axis=-1, keepdims=True) + epsilon)
    return (centered * inverse, inverse)


def layer_norm_reverse(upstream, normalized_rows, inverse):
    first = jnp.mean(upstream, axis=-1, keepdims=True)
    second = jnp.mean(upstream * normalized_rows, axis=-1, keepdims=True)
    return inverse * (upstream - first - normalized_rows * second)


MESH = pl.DeviceIdType.MESH
ROWS_PAD = 48
HEAD_PAD = 96


def place():
    s, i = lax.axis_index("sp"), lax.axis_index("img")
    return s // 8, (s // 4) % 2, s % 4, i // 2, i % 2


def at_sp(x, zl, y):
    return {"sp": (x * 2 + zl) * 4 + y}


def greet(targets):
    barrier = pltpu.get_barrier_semaphore()
    for target in targets:
        pl.semaphore_signal(barrier, inc=1, device_id=target, device_id_type=MESH)
    pl.semaphore_wait(barrier, len(targets))


def one_hot(rows, per, block):
    r = lax.broadcasted_iota(jnp.int32, (block, 4 * rows), 0)
    c = lax.broadcasted_iota(jnp.int32, (block, 4 * rows), 1)
    skipped = jnp.zeros_like(r)
    for k in (1, 2, 3):
        skipped += jnp.where(r >= k * per, rows - per, 0)
    return jnp.where(c == r + skipped, 1.0, 0.0)


def gather_kernel(shapes, *refs):
    count = len(shapes)
    ins = refs[:3]
    y_one, second, cot, w_lateral, lat_gain, w_conv, conv_gain = refs[3:10]
    qkv_out, w_out_out, half_out, d_x1_out, dec_out, conv_out, lat_out = refs[10:17]
    deconv, *rest = refs[17:]
    outs = [deconv, qkv_out, w_out_out]
    shards, packs, rest = rest[:3], rest[3:6], rest[6:]
    deconv_shard, out_shard, feature, pixels, act, dconv, cot_low, cot_high, norm_lat, dup, *sems = rest
    send, recv, local, halo_send, halo_recv = sems
    for shard, padded in ((ins[0], deconv_shard), (ins[2], out_shard)):
        padded[...] = jnp.zeros_like(padded)
        padded[: shard.shape[0], : shard.shape[1]] = shard[...]
    ins = [deconv_shard, ins[1], out_shard]
    x, zl, y, zh, core = place()
    s = lax.axis_index("sp")
    below, above = {"sp": (s + 1) % 32}, {"sp": (s + 31) % 32}
    xm, xp, xo = (x + 3) % 4, (x + 1) % 4, (x + 2) % 4
    left, right = at_sp(xm, zl, y), at_sp(xp, zl, y)
    across = (x * 2 + 1 - zl) * 4 + y
    up = {"img": ((zh + zl) % 4) * 2 + core, "sp": across}
    down = {"img": ((zh + zl + 3) % 4) * 2 + core, "sp": across}
    twin = {"img": zh * 2 + 1 - core}
    column = [at_sp(x, zl, (y + k) % 4) for k in (1, 2, 3)]
    greet(column + [left, right, up, down, twin, below, above])
    copies = {}

    def push(a, slot, src, dst, target):
        copy = pltpu.make_async_remote_copy(
            src_ref=src,
            dst_ref=dst,
            send_sem=send.at[a, slot],
            recv_sem=recv.at[a, slot],
            device_id=target,
            device_id_type=MESH,
        )
        copy.start()
        copies[a, slot] = copy

    def part(a):
        half = shapes[a][3] // 2
        return half, pl.multiple_of(core * half, 128)

    def region(a, bx, bz, lo, size):
        half, first = part(a)
        return outs[a].at[bx * 2 + bz, pl.ds(lo, size), pl.ds(first, half)]

    def forward(a, slot, bx, bz, lo, size, target):
        piece = region(a, bx, bz, lo, size)
        push(a, slot, piece, piece, target)

    for a in range(count):
        half, first = part(a)
        mine = ins[a].at[:, pl.ds(first, half)]
        for k in range(3):
            push(a, k, mine, shards[a].at[y], column[k])
        shards[a][y] = ins[a][:, pl.ds(first, half)]
    keeps = {}

    def pack(a):
        rows, per, block, _ = shapes[a]
        half, first = part(a)
        low = (block // 32) * 16
        high = block - low
        for k in range(3):
            copies[a, k].wait_recv()
        pick = one_hot(rows, per, block).astype(jnp.bfloat16)
        packs[a][...] = jnp.dot(
            pick, shards[a][...].reshape(4 * rows, half), preferred_element_type=jnp.float32
        ).astype(jnp.bfloat16)
        own, whole = packs[a], region(a, x, zl, 0, block)
        keep = pltpu.make_async_copy(own, whole, local.at[a])
        keep.start()
        keeps[a] = keep
        push(a, 3, own, whole, right)
        push(a, 4, own, whole, left)
        push(a, 7, own.at[pl.ds(0, low)], region(a, x, zl, 0, low), up)
        push(a, 8, own.at[pl.ds(low, high)], region(a, x, zl, low, high), down)
        push(a, 15, own, whole, twin)

    def near(a):
        block = shapes[a][2]
        low = (block // 32) * 16
        high = block - low
        copies[a, 3].wait_recv()
        forward(a, 5, xm, zl, 0, low, right)
        forward(a, 9, xm, zl, 0, low, up)
        forward(a, 10, xm, zl, low, high, down)
        forward(a, 16, xm, zl, 0, block, twin)
        copies[a, 4].wait_recv()
        forward(a, 6, xp, zl, low, high, left)
        forward(a, 11, xp, zl, 0, low, up)
        forward(a, 12, xp, zl, low, high, down)
        forward(a, 17, xp, zl, 0, block, twin)

    def far(a):
        block = shapes[a][2]
        low = (block // 32) * 16
        high = block - low
        copies[a, 5].wait_recv()
        forward(a, 13, xo, zl, 0, low, up)
        forward(a, 18, xo, zl, 0, low, twin)
        copies[a, 6].wait_recv()
        forward(a, 14, xo, zl, low, high, down)
        forward(a, 19, xo, zl, low, high, twin)

    def deep(a):
        block = shapes[a][2]
        low = (block // 32) * 16
        high = block - low
        for n, bx in enumerate((x, xm, xp, xo)):
            copies[a, 7 + 2 * n].wait_recv()
            forward(a, 20 + 2 * n, bx, 1 - zl, 0, low, twin)
            copies[a, 8 + 2 * n].wait_recv()
            forward(a, 21 + 2 * n, bx, 1 - zl, low, high, twin)

    def twins(a):
        for slot in range(15, 28):
            copies[a, slot].wait_recv()

    row = GRID_W
    inner_rows = 4 * row
    halos = {}

    def swap_edges(ref, first):
        ends = (
            (first, pl.ds(inner_rows, row), pl.ds(0, row), below),
            (first + 1, pl.ds(row, row), pl.ds(inner_rows + row, row), above),
        )
        for slot, src_rows, dst_rows, target in ends:
            copy = pltpu.make_async_remote_copy(
                src_ref=ref.at[pl.ds(1, 2), src_rows],
                dst_ref=ref.at[pl.ds(1, 2), dst_rows],
                send_sem=halo_send.at[slot],
                recv_sem=halo_recv.at[slot],
                device_id=target,
                device_id_type=MESH,
            )
            copy.start()
            halos[slot] = copy

    def fill_sides(ref, first):
        halos[first].wait_recv()
        halos[first + 1].wait_recv()
        for b in (1, 2):
            head, tail = pl.ds(0, row), pl.ds(inner_rows + row, row)
            ref[b, head] = jnp.where(s == 0, 0.0, ref[b, head].astype(jnp.float32)).astype(
                jnp.bfloat16
            )
            ref[b, tail] = jnp.where(s == 31, 0.0, ref[b, tail].astype(jnp.float32)).astype(
                jnp.bfloat16
            )
        rows = ref.shape[1]
        at = lax.broadcasted_iota(jnp.int32, (rows, LAT), 0) % row
        moved = pltpu.roll(ref[2].astype(jnp.float32), 1, 0)
        ref[0] = jnp.where(at == 0, 0.0, moved).astype(jnp.bfloat16)
        moved = pltpu.roll(ref[1].astype(jnp.float32), rows - 1, 0)
        ref[3] = jnp.where(at == row - 1, 0.0, moved).astype(jnp.bfloat16)

    def taps():
        return [(i, j) for i in range(3) for j in range(3)]

    def upward():
        feature[...] = ((y_one[...].astype(jnp.float32) + second[...].astype(jnp.float32)) * 0.5).astype(
            jnp.bfloat16
        )
        wide = cot[...].reshape(8 * row, LAT).astype(jnp.float32)
        cot_low[...] = wide[:, : LAT // 2]
        cot_high[...] = wide[:, LAT // 2 :]
        depth = deconv.shape[0] * deconv.shape[1]
        for ab in range(4):
            plane = pl.ds(ab * DEC, DEC)
            up = jnp.dot(
                feature[...],
                deconv[:, :, plane].reshape(depth, DEC),
                preferred_element_type=jnp.float32,
            ).astype(jnp.bfloat16)
            for r in range(2):
                pixels[pl.ds((ab % 2) * inner_rows + (2 * r + ab // 2) * row, row)] = up[
                    r * row : (r + 1) * row
                ]
        lat = jnp.dot(pixels[...], w_lateral[...], preferred_element_type=jnp.float32)
        lhat, linv = apply_layer_norm(lat)
        norm_lat[...] = lhat
        scaled = (lhat * lat_gain[...]).astype(jnp.bfloat16)
        for b in range(2):
            act[1 + b, pl.ds(row, inner_rows)] = scaled[b * inner_rows : (b + 1) * inner_rows]
        swap_edges(act, 0)
        return linv

    def convolve():
        fill_sides(act, 0)
        for b in range(2):
            total = jnp.zeros((inner_rows, LAT), jnp.float32)
            for i, j in taps():
                total += jnp.dot(
                    act[b + j, pl.ds(i * row, inner_rows)],
                    w_conv[3 * i + j],
                    preferred_element_type=jnp.float32,
                )
            chat, cinv = apply_layer_norm(total)
            every = pl.ds(b, inner_rows, stride=2)
            upstream = jnp.concatenate([cot_low[every, :], cot_high[every, :]], axis=1)
            upstream = upstream * conv_gain[...]
            dconv[1 + b, pl.ds(row, inner_rows)] = layer_norm_reverse(upstream, chat, cinv).astype(
                jnp.bfloat16
            )
        swap_edges(dconv, 2)

    def downward(linv):
        fill_sides(dconv, 2)
        for b in range(2):
            total = jnp.zeros((inner_rows, LAT), jnp.float32)
            for i, j in taps():
                total += lax.dot_general(
                    dconv[b - j + 2, pl.ds((2 - i) * row, inner_rows)],
                    w_conv[3 * i + j],
                    (((1,), (1,)), ((), ())),
                    preferred_element_type=jnp.float32,
                )
            here = slice(b * inner_rows, (b + 1) * inner_rows)
            dlat = layer_norm_reverse(
                total * lat_gain[...], norm_lat[pl.ds(b * inner_rows, inner_rows)], linv[here]
            ).astype(jnp.bfloat16)
            term = jnp.dot(
                pixels[pl.ds(b * inner_rows, inner_rows)].astype(jnp.float32).T.astype(jnp.bfloat16),
                dlat,
                preferred_element_type=jnp.float32,
            )
            lat_term = term if b == 0 else lat_term + term
            dpixels = lax.dot_general(
                dlat, w_lateral[...], (((1,), (1,)), ((), ())), preferred_element_type=jnp.float32
            ).astype(jnp.bfloat16)
            for line in range(4):
                r, a = line // 2, line % 2
                dup[pl.ds(r * row, row), pl.ds((2 * a + b) * DEC, DEC)] = dpixels[
                    line * row : (line + 1) * row
                ]
        lat_out[...] = (lat_term * grad_scale).astype(jnp.bfloat16)
        depth = deconv.shape[0] * deconv.shape[1]
        half = 0.5 * lax.dot_general(
            dup[...],
            deconv[...].reshape(depth, 4 * DEC),
            (((1,), (1,)), ((), ())),
            preferred_element_type=jnp.float32,
        )
        half_out[...] = half
        d_x1_out[...] = half.astype(jnp.bfloat16)

    def conv_term():
        turned_grads = [
            dconv[1 + b, pl.ds(row, inner_rows)].astype(jnp.float32).T.astype(jnp.bfloat16)
            for b in range(2)
        ]
        for i, j in taps():
            total = jnp.zeros((LAT, LAT), jnp.float32)
            for b in range(2):
                total += jnp.dot(
                    turned_grads[b],
                    act[b + j, pl.ds(i * row, inner_rows)],
                    preferred_element_type=jnp.float32,
                )
            conv_out[:, pl.ds((3 * i + j) * LAT, LAT)] = (total.T * grad_scale).astype(jnp.bfloat16)

    def deconv_term():
        rows, per, block, _ = shapes[0]
        wide = feature[...].astype(jnp.float32).T
        pick = one_hot(rows, per, block).T.astype(jnp.bfloat16)
        for g in range(8):
            group = jnp.dot(
                pick,
                wide[g * block : (g + 1) * block].astype(jnp.bfloat16),
                preferred_element_type=jnp.float32,
            ).astype(jnp.bfloat16)
            term = jnp.dot(group, dup[...], preferred_element_type=jnp.float32) * grad_scale
            dec_out[pl.ds(g * 4 * rows, 4 * rows)] = term.astype(jnp.bfloat16)

    pack(0)
    near(0)
    pack(1)
    far(0)
    pack(2)
    near(1)
    deep(0)
    twins(0)
    keeps[0].wait()
    linv = upward()
    convolve()
    far(1)
    near(2)
    downward(linv)
    far(2)
    deep(1)
    conv_term()
    deep(2)
    deconv_term()
    twins(1)
    twins(2)
    for a in range(1, count):
        keeps[a].wait()
    for copy in list(copies.values()) + list(halos.values()):
        copy.wait_send()


def gather_and_pyramid(shards, pers, *others):
    count = len(shards)
    shapes = []
    for shard, per in zip(shards, pers):
        block = -(-4 * per // 16) * 16
        width = -(-shard.shape[1] // 256) * 256
        shapes.append((-(-per // 16) * 16, per, block, width))
    halves = [(rows, block, width // 2) for rows, _, block, width in shapes]
    tokens, features = others[0].shape
    bf16, f32 = jnp.bfloat16, jnp.float32
    full = [jax.ShapeDtypeStruct((8, block, width), bf16) for _, _, block, width in shapes]
    pixel_count = 4 * tokens
    return pl.pallas_call(
        functools.partial(gather_kernel, shapes),
        out_shape=full[1:]
        + [
            jax.ShapeDtypeStruct((tokens, features), f32),
            jax.ShapeDtypeStruct((tokens, features), bf16),
            jax.ShapeDtypeStruct((32 * ROWS_PAD, 4 * DEC), bf16),
            jax.ShapeDtypeStruct((LAT, 9 * LAT), bf16),
            jax.ShapeDtypeStruct((DEC, LAT), bf16),
        ],
        in_specs=[pl.BlockSpec(memory_space=pltpu.VMEM)] * (count + len(others)),
        out_specs=[pl.BlockSpec(memory_space=pl.ANY)] * (count - 1)
        + [pl.BlockSpec(memory_space=pltpu.VMEM)] * 5,
        scratch_shapes=[pltpu.VMEM(full[0].shape, bf16)]
        + [pltpu.VMEM((4, rows, half), bf16) for rows, _, half in halves]
        + [pltpu.VMEM((block, half), bf16) for _, block, half in halves]
        + [
            pltpu.VMEM((shapes[0][0], shapes[0][3]), bf16),
            pltpu.VMEM((shapes[2][0], shapes[2][3]), bf16),
            pltpu.VMEM((tokens, features), bf16),
            pltpu.VMEM((pixel_count, DEC), bf16),
            pltpu.VMEM((4, 6 * GRID_W, LAT), bf16),
            pltpu.VMEM((4, 6 * GRID_W, LAT), bf16),
            pltpu.VMEM((pixel_count, LAT // 2), f32),
            pltpu.VMEM((pixel_count, LAT // 2), f32),
            pltpu.VMEM((pixel_count, LAT), f32),
            pltpu.VMEM((tokens, 4 * DEC), bf16),
            pltpu.SemaphoreType.DMA((count, 28)),
            pltpu.SemaphoreType.DMA((count, 28)),
            pltpu.SemaphoreType.DMA((count,)),
            pltpu.SemaphoreType.DMA((4,)),
            pltpu.SemaphoreType.DMA((4,)),
        ],
        compiler_params=pltpu.CompilerParams(
            collective_id=0, has_side_effects=True, vmem_limit_bytes=56 * 2**20
        ),
    )(*shards, *others)


AXES = {"x": 4, "z": 2, "y": 4}


def leads(order):
    left = list(AXES)
    sizes = []
    for axis in order:
        left = [name for name in left if name != axis]
        sizes.append([AXES[name] for name in left])
    return sizes


class Scatter:
    def __init__(self, plan, parts, buffers, send, recv, local):
        self.plan, self.parts = plan, parts
        self.land = [buffers[0], buffers[2], buffers[4]]
        self.sums = [buffers[1], buffers[3]]
        self.send, self.recv, self.local = send, recv, local
        x, zl, y, _, _ = place()
        self.me = {"x": x, "z": zl, "y": y}
        self.peers = {
            "x": [(x + k) % 4 for k in (1, 2, 3)],
            "y": [(y + k) % 4 for k in (1, 2, 3)],
            "z": [1 - zl],
        }
        self.copies, self.own = {}, {}

    def take(self, n, step, view, where):
        order = self.plan[n][3]
        left = [name for name in AXES if name not in order[:step]]
        lead = [slice(None)] * left.index(order[step])
        return view.at[(*lead, where)]

    def ship(self, n, step, view):
        axis = self.plan[n][3][step]
        for k, peer in enumerate(self.peers[axis]):
            at = dict(self.me)
            at[axis] = peer
            copy = pltpu.make_async_remote_copy(
                src_ref=self.take(n, step, view, peer),
                dst_ref=self.land[step][n].at[k],
                send_sem=self.send.at[n, 3 * step + k],
                recv_sem=self.recv.at[n, 3 * step + k],
                device_id=at_sp(at["x"], at["z"], at["y"]),
                device_id_type=MESH,
            )
            copy.start()
            self.copies[n, step, k] = copy

    def arrived(self, n, step):
        count = len(self.peers[self.plan[n][3][step]])
        for k in range(count):
            self.copies[n, step, k].wait_recv()
        return count

    def start(self, n):
        source, first, width, order = self.plan[n]
        view = self.parts[source].at[:, :, :, :, pl.ds(first, width)]
        own = self.take(n, 0, view, self.me[order[0]])
        self.own[n] = pltpu.make_async_copy(own, self.sums[0][n], self.local.at[n])
        self.own[n].start()
        self.ship(n, 0, view)

    def second(self, n):
        sums, land = self.sums[0][n], self.land[0][n]
        self.own[n].wait()
        count = self.arrived(n, 0)
        outer, inner = sums.shape[:2]

        def add(t, carry):
            p, q = t // inner, t % inner
            total = sums[p, q].astype(jnp.float32)
            for k in range(count):
                total += land[k, p, q].astype(jnp.float32)
            sums[p, q] = total.astype(jnp.bfloat16)
            return carry

        lax.fori_loop(0, outer * inner, add, 0)
        self.ship(n, 1, sums)

    def third(self, n):
        land, sums = self.land[1][n], self.sums[1][n]
        order = self.plan[n][3]
        count = self.arrived(n, 1)
        own = self.take(n, 1, self.sums[0][n], self.me[order[1]])
        for p in range(sums.shape[0]):
            total = own[p].astype(jnp.float32)
            for k in range(count):
                total += land[k, p].astype(jnp.float32)
            sums[p] = total.astype(jnp.bfloat16)
        self.ship(n, 2, sums)

    def finish(self, n, out):
        count = self.arrived(n, 2)
        total = self.sums[1][n][self.me[self.plan[n][3][2]]].astype(jnp.float32)
        for k in range(count):
            total += self.land[2][n][k].astype(jnp.float32)
        _, first, width, _ = self.plan[n]
        out[:, pl.ds(first, width)] = total[: out.shape[0]]

    def settle(self):
        for copy in self.copies.values():
            copy.wait_send()


def scatter_buffers(plan, rows):
    groups = [[], [], [], [], []]
    for source, _, width, order in plan:
        sizes = leads(order)
        for step in range(3):
            peers = AXES[order[step]] - 1
            tail = (rows[source], width)
            groups[2 * step].append(pltpu.VMEM((peers, *sizes[step], *tail), jnp.bfloat16))
            if step < 2:
                groups[2 * step + 1].append(pltpu.VMEM((*sizes[step], *tail), jnp.bfloat16))
    return groups


TILE = 128
QUERY_BLOCK = 512
KEY_BLOCK = 1024


def turned(block):
    wide = block.astype(jnp.float32)
    zeros = jnp.zeros((TILE - HEAD_PAD, TILE), jnp.float32)
    return jnp.concatenate([wide, zeros], axis=0).T


def head_rows(block):
    return block.T[:HEAD_PAD].astype(jnp.bfloat16)


SUM_PLAN = [
    (0, 0, 2 * DEC, "xyz"),
    (0, 2 * DEC, 2 * DEC, "zxy"),
    (1, 0, 9 * LAT, "zxy"),
    (2, 0, LAT, "zxy"),
    (3, 0, 768, "yxz"),
    (3, 768, 640, "xyz"),
]
OUT_ROWS = 22
OUT_ROWS_STEP = 24


def attention_kernel(proj, grad, d_x1, dec_part, conv_part, lat_part, *refs):
    attn_out, dqkv_out, *sum_outs = refs[:6]
    (
        q_in,
        g_in,
        kv_in,
        key_t,
        value_t,
        key,
        value,
        query,
        cot,
        query_t,
        cot_t,
        score,
        weight,
        inverse,
        offset,
        attended,
        o_send,
        dq_send,
        d_send,
        d_land,
        d_sum,
        o_land,
        d_res,
        out_part,
    ) = refs[6:30]
    chunks = len(SUM_PLAN)
    groups = [refs[30 + chunks * k : 30 + chunks * (k + 1)] for k in range(5)]
    send, recv, sum_send, sum_recv, sum_local = refs[30 + 5 * chunks :]
    sums = Scatter(
        SUM_PLAN, [dec_part, conv_part, lat_part, out_part], groups, sum_send, sum_recv, sum_local
    )
    x, zl, y, zh, core = place()
    m = x * 2 + zl
    plane = [(m + k) % 8 for k in range(8)]
    source = [(m + 8 - k) % 8 for k in range(8)]
    column = [(y + k) % 4 for k in range(4)]

    def at_plane(k):
        return {"sp": plane[k] * 4 + y}

    def at_column(k):
        return {"sp": m * 4 + column[k]}

    greet([at_plane(k) for k in range(1, 8)] + [at_column(k) for k in range(1, 4)])
    copies = {}

    def push(slot, src, dst, target):
        copy = pltpu.make_async_remote_copy(
            src_ref=src,
            dst_ref=dst,
            send_sem=send.at[slot],
            recv_sem=recv.at[slot],
            device_id=target,
            device_id_type=MESH,
        )
        copy.start()
        copies[slot] = copy

    kv_at, q_at, g_at, ring_at, o_at, dq_at, back_at, home_at = 0, 8, 16, 24, 48, 56, 64, 72
    for k in range(1, 8):
        push(kv_at + k, proj.at[pl.ds(1, 2), plane[k]], kv_in.at[y, m], at_plane(k))
    kv_in[y, m, 0] = proj[1, m]
    kv_in[y, m, 1] = proj[2, m]
    q_in[m] = proj[0, m]
    g_in[m] = grad[m]

    def pass_on(k):
        piece = kv_in.at[y, source[k]]
        for j in range(1, 4):
            push(ring_at + 3 * k + j - 1, piece, piece, at_column(j))

    pass_on(0)
    for k in range(1, 8):
        push(q_at + k, proj.at[0, plane[k]], q_in.at[m], at_plane(k))
    for k in range(1, 8):
        copies[kv_at + k].wait_recv()
        pass_on(k)
    for k in range(1, 8):
        push(g_at + k, grad.at[plane[k]], g_in.at[m], at_plane(k))
    for n in (0, 1, 2, 3):
        sums.start(n)
    zero_rows = jnp.zeros((TILE - HEAD_PAD, key_t.shape[1]), jnp.bfloat16)
    key_t[HEAD_PAD:] = zero_rows
    value_t[HEAD_PAD:] = zero_rows

    def prepare(t, carry):
        at = pl.ds(pl.multiple_of(t * TILE, TILE), TILE)
        block = kv_in[t // 8, t % 8, 0]
        key_t[:HEAD_PAD, at] = block
        key[at, :] = turned(block).astype(jnp.bfloat16)
        block = kv_in[t // 8, t % 8, 1]
        value_t[:HEAD_PAD, at] = block
        value[at, :] = turned(block).astype(jnp.bfloat16)
        return carry

    def prepare_queries(t, carry):
        query[pl.ds(pl.multiple_of(t * TILE, TILE), TILE), :] = turned(q_in[t]).astype(jnp.bfloat16)
        return carry

    def prepare_cots(t, carry):
        cot[pl.ds(pl.multiple_of(t * TILE, TILE), TILE), :] = turned(g_in[t]).astype(jnp.bfloat16)
        return carry

    lax.fori_loop(y * 8, y * 8 + 8, prepare, 0)
    for k in range(1, 8):
        copies[q_at + k].wait_recv()
    lax.fori_loop(0, 8, prepare_queries, 0)
    for j in range(1, 4):
        for k in range(8):
            copies[ring_at + 3 * k + j - 1].wait_recv()
        first = ((y + 4 - j) % 4) * 8
        lax.fori_loop(first, first + 8, prepare, 0)
    for k in range(1, 8):
        copies[g_at + k].wait_recv()
    lax.fori_loop(0, 8, prepare_cots, 0)

    tokens = key.shape[0]
    queries = query.shape[0]
    blocks = [pl.ds(c * KEY_BLOCK, KEY_BLOCK) for c in range(tokens // KEY_BLOCK)]

    def forward(i, carry):
        at = pl.ds(pl.multiple_of(i * QUERY_BLOCK, QUERY_BLOCK), QUERY_BLOCK)
        top = jnp.full((QUERY_BLOCK, 1), -jnp.inf, jnp.float32)
        for block in blocks:
            part = jnp.dot(query[at, :], key_t[:, block], preferred_element_type=jnp.float32)
            score[:, block] = part
            top = jnp.maximum(top, jnp.max(part, axis=1, keepdims=True))
        total = jnp.zeros((QUERY_BLOCK, 1), jnp.float32)
        mixed = jnp.zeros((QUERY_BLOCK, TILE), jnp.float32)
        for block in blocks:
            part = jnp.exp(score[:, block] - top)
            total += jnp.sum(part, axis=1, keepdims=True)
            rounded = part.astype(jnp.bfloat16)
            weight[at, block] = rounded
            mixed += jnp.dot(rounded, value[block, :], preferred_element_type=jnp.float32)
        inv = 1.0 / total
        mixed = mixed * inv
        attended[at, :] = mixed
        inverse[at, :] = inv
        offset[at, :] = jnp.sum(mixed * cot[at, :].astype(jnp.float32), axis=1, keepdims=True)
        return carry

    lax.fori_loop(0, queries // QUERY_BLOCK, forward, 0)
    for t in range(8):
        at = pl.ds(t * TILE, TILE)
        o_send[t] = head_rows(attended[at, :])
    for k in range(1, 8):
        push(o_at + k, o_send.at[plane[k]], o_land.at[m], at_plane(k))
    o_land[m] = o_send[m]
    for t in range(8):
        at = pl.ds(t * TILE, TILE)
        inv = inverse[at, :]
        query_t[:, at] = (query[at, :].astype(jnp.float32) * inv).T.astype(jnp.bfloat16)
        cot_t[:, at] = (cot[at, :].astype(jnp.float32) * inv).T.astype(jnp.bfloat16)

    def key_side(left, kind):
        for j in (1, 2, 3, 0):
            yy = column[j]
            at = pl.ds(pl.multiple_of(yy * 8 * TILE, 8 * TILE), 8 * TILE)
            result = jnp.dot(left[...], weight[:, at], preferred_element_type=jnp.float32)
            for t in range(8):
                d_send[kind, j, t] = result[:HEAD_PAD, t * TILE : (t + 1) * TILE].astype(
                    jnp.bfloat16
                )
            if j:
                push(back_at + 4 * kind + j, d_send.at[kind, j], d_land.at[kind, j - 1], at_column(j))

    def key_home(kind):
        for j in range(1, 4):
            copies[back_at + 4 * kind + j].wait_recv()
        for t in range(8):
            total = d_send[kind, 0, t].astype(jnp.float32)
            for j in range(3):
                total += d_land[kind, j, t].astype(jnp.float32)
            d_sum[kind, t] = total.astype(jnp.bfloat16)
        for k in range(1, 8):
            push(
                home_at + 8 * kind + k,
                d_sum.at[kind, plane[k]],
                d_res.at[kind + 1, m],
                at_plane(k),
            )
        d_res[kind + 1, m] = d_sum[kind, m]

    key_side(cot_t, 1)
    for k in range(1, 8):
        copies[o_at + k].wait_recv()
    attn_out[...] = o_land[...]
    spread = 4 * OUT_ROWS_STEP
    r = lax.broadcasted_iota(jnp.int32, (spread, HEAD_PAD), 0)
    c = lax.broadcasted_iota(jnp.int32, (spread, HEAD_PAD), 1)
    picked = c < 0
    for k in range(4):
        low, first = k * OUT_ROWS, k * OUT_ROWS_STEP
        picked |= (c - low == r - first) & (c >= low) & (c < low + OUT_ROWS) & (r >= first)
    pick = jnp.where(picked, 1.0, 0.0).astype(jnp.bfloat16)
    for t in range(8):
        rows = jnp.dot(pick, o_land[t], preferred_element_type=jnp.float32).astype(jnp.bfloat16)
        term = jnp.dot(rows, d_x1[...], preferred_element_type=jnp.float32) * grad_scale
        for k in range(4):
            out_part[t // 2, t % 2, k] = term[
                k * OUT_ROWS_STEP : (k + 1) * OUT_ROWS_STEP
            ].astype(jnp.bfloat16)
    sums.start(4)
    sums.start(5)
    for n in (3, 2, 0, 1):
        sums.second(n)

    def backward(i, carry):
        at = pl.ds(pl.multiple_of(i * QUERY_BLOCK, QUERY_BLOCK), QUERY_BLOCK)
        query_grad = jnp.zeros((QUERY_BLOCK, TILE), jnp.float32)
        shift = offset[at, :]
        for block in blocks:
            dprob = jnp.dot(cot[at, :], value_t[:, block], preferred_element_type=jnp.float32)
            dscore = (weight[at, block].astype(jnp.float32) * (dprob - shift)).astype(jnp.bfloat16)
            weight[at, block] = dscore
            query_grad += jnp.dot(dscore, key[block, :], preferred_element_type=jnp.float32)
        attended[at, :] = query_grad * (inverse[at, :] * HEAD ** (-0.5))
        return carry

    for i in range(queries // QUERY_BLOCK):
        backward(i, 0)
        if i == 0:
            key_home(1)
    key_side(query_t, 0)
    for t in range(8):
        dq_send[t] = head_rows(attended[pl.ds(t * TILE, TILE), :])
    for k in range(1, 8):
        push(dq_at + k, dq_send.at[plane[k]], d_res.at[0, m], at_plane(k))
    d_res[0, m] = dq_send[m]
    key_home(0)
    for n in (3, 2, 0, 1):
        sums.third(n)
    sums.second(4)
    sums.second(5)
    sums.third(4)
    sums.third(5)
    for first in (dq_at, home_at, home_at + 8):
        for k in range(1, 8):
            copies[first + k].wait_recv()
    dqkv_out[...] = d_res[...]
    for n in range(chunks):
        sums.finish(n, sum_outs[SUM_PLAN[n][0]])
    for copy in copies.values():
        copy.wait_send()
    sums.settle()


def attend_both_ways(proj, grad, d_x1, dec_part, conv_part, lat_part, own_rows):
    rows = [part.shape[3] for part in (dec_part, conv_part, lat_part)] + [OUT_ROWS_STEP]
    groups = scatter_buffers(SUM_PLAN, rows)
    heads = grad.shape[0]
    tokens, queries = 32 * TILE, 8 * TILE
    bf16, f32 = jnp.bfloat16, jnp.float32
    block = (HEAD_PAD, TILE)
    shapes = [
        ((8, *block), bf16),
        ((8, *block), bf16),
        ((4, 8, 2, *block), bf16),
        ((TILE, tokens), bf16),
        ((TILE, tokens), bf16),
        ((tokens, TILE), bf16),
        ((tokens, TILE), bf16),
        ((queries, TILE), bf16),
        ((queries, TILE), bf16),
        ((TILE, queries), bf16),
        ((TILE, queries), bf16),
        ((QUERY_BLOCK, tokens), f32),
        ((queries, tokens), bf16),
        ((queries, 1), f32),
        ((queries, 1), f32),
        ((queries, TILE), f32),
        ((8, *block), bf16),
        ((8, *block), bf16),
        ((2, 4, 8, *block), bf16),
        ((2, 3, 8, *block), bf16),
        ((2, 8, *block), bf16),
        ((8, *block), bf16),
        ((3, 8, *block), bf16),
        ((4, 2, 4, OUT_ROWS_STEP, d_x1.shape[1]), bf16),
    ]
    sum_sems = pltpu.SemaphoreType.DMA((len(SUM_PLAN), 9))
    return pl.pallas_call(
        attention_kernel,
        out_shape=[
            jax.ShapeDtypeStruct((heads, *block), bf16),
            jax.ShapeDtypeStruct((3, heads, *block), bf16),
        ]
        + [
            jax.ShapeDtypeStruct((w_rows, part.shape[-1]), f32)
            for w_rows, part in zip(own_rows, (dec_part, conv_part, lat_part, d_x1))
        ],
        in_specs=[pl.BlockSpec(memory_space=pltpu.VMEM)] * 3
        + [pl.BlockSpec(memory_space=pl.ANY)] * 3,
        out_specs=[pl.BlockSpec(memory_space=pltpu.VMEM)] * 6,
        scratch_shapes=[pltpu.VMEM(shape, kind) for shape, kind in shapes]
        + [buffer for group in groups for buffer in group]
        + [pltpu.SemaphoreType.DMA((88,)), pltpu.SemaphoreType.DMA((88,))]
        + [sum_sems, sum_sems, pltpu.SemaphoreType.DMA((len(SUM_PLAN),))],
        compiler_params=pltpu.CompilerParams(
            collective_id=2, has_side_effects=True, vmem_limit_bytes=56 * 2**20
        ),
    )(proj, grad, d_x1, dec_part, conv_part, lat_part)


def per_device(
    y_one,
    second_stream_state,
    cot,
    layer_norm_gain,
    w_qkv,
    w_out,
    w_deconv,
    w_lateral,
    lat_gain,
    w_conv,
    conv_gain,
):
    devices = lax.axis_size("sp")
    tokens_here = y_one.shape[0]
    score_scale = HEAD ** (-0.5)
    standardized_input, inverse_deviation = apply_layer_norm(
        second_stream_state.astype(jnp.float32)
    )
    normalized_rows = (standardized_input * layer_norm_gain).astype(jnp.bfloat16)
    depth, out_depth = w_qkv.shape[0], w_out.shape[0]
    qkv_shard = jnp.pad(
        w_qkv.reshape(depth, 3 * HEADS, HEAD),
        ((0, ROWS_PAD - depth), (0, 0), (0, HEAD_PAD - HEAD)),
    ).reshape(ROWS_PAD, 3 * HEADS * HEAD_PAD)
    qkv_full, out_full, halfway_split, d_x1, dec_part, conv_part, lat_part = gather_and_pyramid(
        [w_deconv, qkv_shard, w_out],
        [depth, depth, out_depth],
        y_one,
        second_stream_state,
        cot,
        w_lateral,
        lat_gain[None],
        w_conv.reshape(9, LAT, LAT),
        conv_gain[None],
    )
    dec_part = dec_part.reshape(4, 2, 4, ROWS_PAD, 4 * DEC)
    conv_part = conv_part.reshape(4, 2, 4, LAT // devices, 9 * LAT)
    lat_rows = DEC // devices
    lat_part = jnp.pad(
        lat_part.reshape(devices, lat_rows, LAT), ((0, 0), (0, 16 - lat_rows), (0, 0))
    ).reshape(4, 2, 4, 16, LAT)
    qkv_full = qkv_full.reshape(devices * depth, -1)
    out_full = out_full.reshape(HEADS * HEAD_PAD, -1)[:, : w_out.shape[1]]
    dattn = lax.dot_general(
        out_full, d_x1, (((1,), (1,)), ((), ())), preferred_element_type=jnp.float32
    ).astype(jnp.bfloat16)
    projected = lax.optimization_barrier(
        jnp.dot(normalized_rows, qkv_full, preferred_element_type=jnp.float32)
    )
    projected = projected.T.reshape(3, HEADS, HEAD_PAD, tokens_here)
    scales = jnp.array([score_scale, 1.0, 1.0], jnp.float32).reshape(3, 1, 1, 1)
    projected = (projected * scales).astype(jnp.bfloat16)
    attn_heads, dqkv, *summed = attend_both_ways(
        projected,
        dattn.reshape(HEADS, HEAD_PAD, tokens_here),
        d_x1,
        dec_part,
        conv_part,
        lat_part,
        (depth, LAT // devices, lat_rows, out_depth),
    )
    g_deconv, conv_rows, g_lateral, g_out = summed
    mixed = lax.dot_general(
        attn_heads.reshape(HEADS * HEAD_PAD, tokens_here),
        out_full,
        (((0,), (0,)), ((), ())),
        preferred_element_type=jnp.float32,
    )
    x_one = (y_one.astype(jnp.float32) - mixed).astype(jnp.bfloat16)
    normalized_gradient = lax.dot_general(
        dqkv.reshape(3 * HEADS * HEAD_PAD, tokens_here),
        qkv_full, (((0,), (1,)), ((), ())), preferred_element_type=jnp.float32
    )
    second_input_gradient = (
        halfway_split
        + layer_norm_reverse(
            normalized_gradient * layer_norm_gain, standardized_input, inverse_deviation
        )
    ).astype(jnp.bfloat16)
    g_conv = conv_rows.reshape(conv_rows.shape[0], 3, 3, LAT).transpose(1, 2, 0, 3)
    return (x_one, d_x1, second_input_gradient, g_out, g_deconv, g_lateral, g_conv)


def solution(mesh):
    return jax.shard_map(
        per_device,
        mesh=mesh,
        in_specs=(
            P(("img", "sp"), None),
            P(("img", "sp"), None),
            P(("img", "sp"), None, None),
            P(),
            P("sp", None),
            P("sp", None),
            P("sp", None),
            P(),
            P(),
            P(),
            P(),
        ),
        out_specs=(
            P(("img", "sp"), None),
            P(("img", "sp"), None),
            P(("img", "sp"), None),
            P(("img", "sp"), None),
            P(("img", "sp"), None),
            P(("img", "sp"), None),
            P("img", None, "sp", None),
        ),
        check_vma=False,
    )
```
